32 devices in a mesh: seq: 4 (over y, core), dp: 8 (over z, x).
Axes of the slice: x: 2, y: 2, z: 4, core: 2. Of those that a mesh axis runs over, the one named last changes fastest.
Arguments:
- tokens: bfloat16 [16, 1024, 1024], P('dp', 'seq'), may hold values from -6 to 6
- attn_gain: float32 [1024], P('dp'), may hold values from 0.5 to 1.5
- query_weight: float32 [1024, 1024], P('dp'), may hold values from -0.1875 to 0.1875
- latent_weight: float32 [1024, 512], P('dp'), may hold values from -0.1875 to 0.1875
- key_expand: float32 [256, 1024], P(None, 'dp'), may hold values from -0.375 to 0.375
- value_expand: float32 [256, 1024], P(None, 'dp'), may hold values from -0.375 to 0.375
- output_weight: float32 [1024, 1024], P('dp'), may hold values from -1.5 to 1.5
- mlp_gain: float32 [1024], P('dp'), may hold values from 0.5 to 1.5
- gate_weight: float32 [1024, 2816], P('dp'), may hold values from -0.1875 to 0.1875
- up_weight: float32 [1024, 2816], P('dp'), may hold values from -0.1875 to 0.1875
- down_weight: float32 [2816, 1024], P('dp'), may hold values from -0.109375 to 0.109375
- cotangent: bfloat16 [16, 1024, 1024], P('dp', 'seq'), may hold values from -6 to 6
- lengths: int32 [16, 2], P('dp'), may hold values from 0 to 1024, as said below
Outputs:
- layer_out: bfloat16 [16, 1024, 1024], P('dp', 'seq')
- grad_tokens: float32 [16, 1024, 1024], P('dp', 'seq')
- grad_attn_gain: float32 [1024], P('dp')
- grad_query: float32 [1024, 1024], P('dp')
- grad_latent: float32 [1024, 512], P('dp')
- grad_key_expand: float32 [256, 1024], P(None, 'dp')
- grad_value_expand: float32 [256, 1024], P(None, 'dp')
- grad_output: float32 [1024, 1024], P('dp')
- grad_mlp_gain: float32 [1024], P('dp')
- grad_gate: float32 [1024, 2816], P('dp')
- grad_up: float32 [1024, 2816], P('dp')
- grad_down: float32 [2816, 1024], P('dp')
The draws below stay inside these ranges and needn't reach their ends.
Inputs may be any that keep to these rules, and one draw needn't show every extreme that they name: Among each device's 2 rows (rows k * 2 to (k + 1) * 2 - 1) one, drawn from the seed, holds a single sequence: lengths 1024 and 0. Every other row holds two sequences: a first one of 256 to 768 positions and a second one of the rest. The two entries of a row sum to 1024.
All inputs are finite; a program needn't handle non-finite values.
Results may differ from the reference program's by a relative error of at most 0.023.
Values may be sent and summed in bfloat16 or wider, within the bound.
No kernel may reach another device: no remote copies, remote signals or barrier semaphores. Data moves between devices by JAX's collectives and lax.ppermute only.
A program may use at most 192 MiB of HBM per device.

```python
import jax
import jax.numpy as jnp
from jax import lax

D = 1024
H = 16
HD = 64
KVH = 2
LAT = 256
FF = 2816
SEQ_DEV = 256
B_DEV = 2
ROW = 1024
BATCH = 16


def draw_lengths(key, part):
    key = jax.random.fold_in(key, 7)
    pick_key, split_key = jax.random.split(key)
    groups = BATCH // B_DEV
    single = jax.random.randint(pick_key, (groups, 1), 0, B_DEV)
    places = jnp.arange(B_DEV, dtype=jnp.int32)[None, :]
    first = jax.random.randint(split_key, (groups, B_DEV), ROW // 4, 3 * ROW // 4 + 1)
    first = jnp.where(places == single, ROW, first)
    second = ROW - first
    return jnp.stack([first, second], axis=-1).reshape(BATCH, 2).astype(jnp.int32)


def shard_levels(own_key, extent, cuts, low, largest):
    loudness, own = 1.0, jax.random.fold_in(own_key, 6)
    for dim, blocks in cuts:
        draws = jnp.exp(jax.random.uniform(jax.random.fold_in(own, dim), (blocks,), jnp.float32, low / len(cuts), largest / len(cuts)))
        loudness = loudness * jnp.repeat(draws, extent[dim] // blocks).reshape([-1 if axis == dim else 1 for axis in range(len(extent))])
    return loudness


def noise(rng, shape, spread, most, shards=(), kind=jnp.bfloat16):
    factor_of = shard_levels(rng, shape, shards, -0.22, 0.18) if shards else 1.0
    values = jax.random.normal(rng, shape, jnp.float32) * spread * factor_of
    return jnp.minimum(jnp.maximum(values, -most), most).astype(kind)


def setup_inputs(seed: int = 0) -> dict:
    key_of = jax.random.split(jax.random.key(seed), 14)
    return {
        "tokens": noise(key_of[0], (BATCH, ROW, D), 1.0, 6.0, ((0, 8), (1, 4))),
        "attn_gain": jnp.clip(1.0 + 0.1 * jax.random.normal(key_of[1], (D,), jnp.float32), 0.5, 1.5),
        "query_weight": noise(key_of[2], (D, D), D ** -0.5, 0.1875, ((0, 8),), jnp.float32),
        "latent_weight": noise(key_of[3], (D, 2 * LAT), D ** -0.5, 0.1875, ((0, 8),), jnp.float32),
        "key_expand": noise(key_of[4], (LAT, D), LAT ** -0.5, 0.375, ((1, 8),), jnp.float32),
        "value_expand": noise(key_of[5], (LAT, D), LAT ** -0.5, 0.375, ((1, 8),), jnp.float32),
        "output_weight": noise(key_of[6], (D, D), (max(1, D * 16 // ROW)) ** -0.5, 1.5, ((0, 8),), jnp.float32),
        "mlp_gain": jnp.clip(1.0 + 0.1 * jax.random.normal(key_of[7], (D,), jnp.float32), 0.5, 1.5),
        "gate_weight": noise(key_of[8], (D, FF), D ** -0.5, 0.1875, ((0, 8),), jnp.float32),
        "up_weight": noise(key_of[9], (D, FF), D ** -0.5, 0.1875, ((0, 8),), jnp.float32),
        "down_weight": noise(key_of[10], (FF, D), FF ** -0.5, 0.109375, ((0, 8),), jnp.float32),
        "cotangent": noise(key_of[11], (BATCH, ROW, D), 1.0, 6.0, ((0, 8), (1, 4))),
        "lengths": draw_lengths(jax.random.fold_in(key_of[13], 71), 0),
    }


@jax.custom_vjp
def low(v):
    return lax.optimization_barrier(v.astype(jnp.bfloat16)).astype(jnp.float32)

@jax.custom_vjp
def low_back(v):
    return v

def low_keep(v):
    return (low(v), None)

def low_pass(kept, grad):
    return (grad,)

def back_keep(v):
    return (v, None)

def back_low(kept, grad):
    return (low(grad),)
low.defvjp(low_keep, low_pass)
low_back.defvjp(back_keep, back_low)
EPS = 1e-06
HIGH = lax.Precision.HIGHEST

def norm_rows(values, gain):
    return values * lax.rsqrt(lax.optimization_barrier(jnp.mean(values * values, axis=-1, keepdims=True)) + EPS) * gain

def expand(latent, weight):
    shaped = latent.reshape(latent.shape[:-1] + (KVH, LAT))
    table = weight.reshape(LAT, KVH, D // KVH)
    result = jnp.einsum('...gl,lgj->...gj', shaped, table, precision=HIGH)
    return result.reshape(latent.shape[:-1] + (D,))

def attend_row(query, keys, values, first):
    width = SEQ_DEV
    position = jnp.arange(ROW, dtype=jnp.int32)
    document = (position >= first).astype(jnp.int32)
    key_heads = keys.reshape(ROW, H, HD)
    value_heads = values.reshape(ROW, H, HD)

    def block(parts):
        query_block, rows = parts
        block_keys = low_back(key_heads)
        block_values = low_back(value_heads)
        row_document = (rows >= first).astype(jnp.int32)
        scores = jnp.einsum('qhd,khd->hqk', query_block, block_keys, precision=HIGH) * HD ** (-0.5)
        scores = low_back(scores)
        allowed = (position[None, :] <= rows[:, None]) & (document[None, :] == row_document[:, None])
        scores = jnp.where(allowed[None], scores, -1e+30)
        peak = lax.optimization_barrier(jnp.max(scores, axis=-1, keepdims=True))
        weights = jnp.exp(scores - peak)
        probs = weights / lax.optimization_barrier(jnp.sum(weights, axis=-1, keepdims=True))
        return jnp.einsum('hqk,khd->qhd', low(probs), block_values, precision=HIGH)
    blocks = (query.reshape(ROW // width, width, H, HD), position.reshape(ROW // width, width))
    result = lax.map(jax.checkpoint(block), blocks)
    return result.reshape(ROW, D)

def layer(inputs, attn_gain, query_weight, latent_weight, key_expand, value_expand, output_weight, mlp_gain, gate_weight, up_weight, down_weight, firsts):
    attn_gain, query_weight, latent_weight = (low(attn_gain), low(query_weight), low(latent_weight))
    key_expand, value_expand, output_weight = (low(key_expand), low(value_expand), low(output_weight))
    mlp_gain, gate_weight, up_weight, down_weight = (low(mlp_gain), low(gate_weight), low(up_weight), low(down_weight))
    first_norm = low(norm_rows(inputs, attn_gain))
    query = low(low_back(jnp.dot(first_norm, query_weight, precision=HIGH)))
    latent = low(low_back(jnp.dot(first_norm, latent_weight, precision=HIGH)))
    keys = low(expand(latent, key_expand))
    values = low(expand(latent, value_expand))

    def per_row(parts):
        return attend_row(parts[0], parts[1], parts[2], parts[3])
    attended = lax.map(jax.checkpoint(per_row), (query, keys, values, firsts))
    attended = low(low_back(attended))
    branch = low_back(jnp.dot(attended, output_weight, precision=HIGH))
    middle = inputs + branch
    second_norm = low(norm_rows(middle, mlp_gain))
    gate = low_back(jnp.dot(second_norm, gate_weight, precision=HIGH))
    upward = low_back(jnp.dot(second_norm, up_weight, precision=HIGH))
    hidden = low(jax.nn.silu(gate) * upward)
    return middle + jnp.dot(hidden, down_weight, precision=HIGH)

def reference(tokens, attn_gain, query_weight, latent_weight, key_expand, value_expand, output_weight, mlp_gain, gate_weight, up_weight, down_weight, cotangent, lengths):
    firsts = lengths[:, 0].astype(jnp.int32)

    def forward(inputs, *weights):
        return layer(inputs, *weights, firsts)
    output, pull = jax.vjp(forward, tokens.astype(jnp.float32), attn_gain, query_weight, latent_weight, key_expand, value_expand, output_weight, mlp_gain, gate_weight, up_weight, down_weight)
    grads = pull(cotangent.astype(jnp.float32))
    return (output.astype(jnp.bfloat16), grads[0], grads[1], grads[2], grads[3], grads[4], grads[5], grads[6], grads[7], grads[8], grads[9], grads[10])
```

```python
import jax
import jax.numpy as jnp
from jax import lax
from jax.experimental import pallas as pl
from jax.experimental.pallas import tpu as pltpu
from jax.sharding import PartitionSpec as P

D = 1024
H = 16
HD = 64
KVH = 2
LAT = 256
GH = H // KVH
GW = D // KVH
EPS = 1e-06
SCALE = HD ** (-0.5)
LOG2E = 1.4426950408889634
NEG = -1e30

LOW = jnp.bfloat16
F32 = jnp.float32
ALL = ("seq", "dp")
VMEM_LIMIT = 56 * 1024 * 1024


def mm(left, right):
    return jnp.dot(left, right, preferred_element_type=F32)


def tn(left, right):
    return lax.dot_general(left, right, (((0,), (0,)), ((), ())), preferred_element_type=F32)


def nt(left, right):
    return lax.dot_general(left, right, (((1,), (1,)), ((), ())), preferred_element_type=F32)


def block_bias(k0, q0, first, width):
    kpos = k0 + lax.broadcasted_iota(jnp.int32, (width, width), 0)
    qpos = q0 + lax.broadcasted_iota(jnp.int32, (width, width), 1)
    lowest = jnp.where(qpos >= first, first, 0)
    return jnp.where((kpos <= qpos) & (kpos >= lowest), 0.0, NEG)


def block_needed(k0, q0, first, width):
    before = jnp.logical_and(q0 >= first, k0 + (width - 1) < first)
    return jnp.logical_and(k0 <= q0, jnp.logical_not(before))


def forward_kernel(nkb, batch, width, meta, qt, kxt, vxt, c, ct, o_low, o_full, mix_out, lse_out, q_s, acc, m_s, l_s):
    b, qb = pl.program_id(0), pl.program_id(1)
    q0, first, diag = meta[nkb + qb], meta[nkb + 2 + b], meta[nkb + 2 + batch] + qb
    for h in range(GH):
        cols = slice(h * width, (h + 1) * width)
        rows = slice(h * HD, (h + 1) * HD)
        q_s[:, cols] = (tn(kxt[rows, :], qt[0, rows, :]) * (SCALE * LOG2E)).astype(LOW)
    m_s[...] = jnp.full_like(m_s, NEG)
    l_s[...] = jnp.zeros_like(l_s)
    acc[...] = jnp.zeros_like(acc)

    def step(j, carry):
        kb = lax.rem(diag + j, nkb)
        k0 = meta[kb]

        @pl.when(block_needed(k0, q0, first, width))
        def _():
            bias = block_bias(k0, q0, first, width)
            keys, keys_t = c[0, kb], ct[0, kb]
            for h in range(GH):
                cols = slice(h * width, (h + 1) * width)
                s = mm(keys, q_s[:, cols]) + bias
                m_old = m_s[:, cols]
                m_new = jnp.maximum(m_old, jnp.max(s, axis=0, keepdims=True))
                p = jnp.exp2(s - m_new)
                alpha = jnp.exp2(m_old - m_new)
                m_s[:, cols] = m_new
                l_s[:, cols] = l_s[:, cols] * alpha + jnp.sum(p, axis=0, keepdims=True)
                acc[:, cols] = acc[:, cols] * alpha + mm(keys_t, p.astype(LOW))

        return carry

    lax.fori_loop(0, nkb, step, 0)
    for h in range(GH):
        cols = slice(h * width, (h + 1) * width)
        rows = slice(h * HD, (h + 1) * HD)
        total = l_s[:, cols]
        mixed = (acc[:, cols] * (1.0 / total)).astype(LOW)
        mix_out[0, 0, :, cols] = mixed
        out = mm(vxt[rows, :], mixed)
        o_full[0, rows, :] = out
        o_low[0, rows, :] = out.astype(LOW)
        lse_out[0, 0, :, cols] = m_s[:, cols] + jnp.log(total) * LOG2E


def backward_kernel(
    nkb, batch, width, meta, qt, dot_, o_full, mix, lse, kxt, vxt, c, ct, dqt, dc, dkxt, dvxt,
    q_s, q_n, do_t, do_n, delta, dq, ds_s, p_s,
):
    b, qb = pl.program_id(0), pl.program_id(1)
    q0, first, diag = meta[nkb + qb], meta[nkb + 2 + b], meta[nkb + 2 + batch] + qb

    @pl.when(qb == 0)
    def _():
        dc[...] = jnp.zeros_like(dc)

    @pl.when(jnp.logical_and(b == 0, qb == 0))
    def _():
        dkxt[...] = jnp.zeros_like(dkxt)
        dvxt[...] = jnp.zeros_like(dvxt)

    for h in range(GH):
        cols = slice(h * width, (h + 1) * width)
        rows = slice(h * HD, (h + 1) * HD)
        qh, kh, doh, vh = qt[0, rows, :], kxt[rows, :], dot_[0, rows, :], vxt[rows, :]
        q_s[:, cols] = (tn(kh, qh) * (SCALE * LOG2E)).astype(LOW)
        q_n[cols, :] = (tn(qh, kh) * SCALE).astype(LOW)
        do_t[:, cols] = tn(vh, doh).astype(LOW)
        do_n[cols, :] = tn(doh, vh).astype(LOW)
        delta[:, cols] = jnp.sum(doh.astype(F32) * o_full[0, rows, :], axis=0, keepdims=True)
    dq[...] = jnp.zeros_like(dq)

    def step(j, carry):
        kb = lax.rem(diag + j, nkb)
        k0 = meta[kb]

        @pl.when(block_needed(k0, q0, first, width))
        def _():
            bias = block_bias(k0, q0, first, width)
            keys, keys_t = c[0, kb], ct[0, kb]
            for h in range(GH):
                cols = slice(h * width, (h + 1) * width)
                s = mm(keys, q_s[:, cols]) + bias
                p = jnp.exp2(s - lse[0, 0, :, cols])
                dp = mm(keys, do_t[:, cols])
                ds = (p * (dp - delta[:, cols])).astype(LOW)
                p_s[:, cols] = p.astype(LOW)
                ds_s[:, cols] = ds
                dq[:, cols] += mm(keys_t, ds)
            dc[0, kb] += mm(ds_s[...], q_n[...]) + mm(p_s[...], do_n[...])

        return carry

    lax.fori_loop(0, nkb, step, 0)
    for h in range(GH):
        cols = slice(h * width, (h + 1) * width)
        rows = slice(h * HD, (h + 1) * HD)
        dq_low = (dq[:, cols] * SCALE).astype(LOW)
        dqt[0, rows, :] = mm(kxt[rows, :], dq_low).astype(LOW)
        dkxt[rows, :] += nt(qt[0, rows, :], dq_low)
        dvxt[rows, :] += nt(dot_[0, rows, :], mix[0, 0, :, cols])


def attention_specs(nkb, width):
    wide = GH * width
    return {
        "meta": pl.BlockSpec(memory_space=pltpu.SMEM),
        "q": pl.BlockSpec((1, GW, width), lambda b, q: (b, 0, q)),
        "expand": pl.BlockSpec((GW, LAT), lambda b, q: (0, 0)),
        "c": pl.BlockSpec((1, nkb, width, LAT), lambda b, q: (b, 0, 0, 0)),
        "ct": pl.BlockSpec((1, nkb, LAT, width), lambda b, q: (b, 0, 0, 0)),
        "mix": pl.BlockSpec((1, 1, LAT, wide), lambda b, q: (b, q, 0, 0)),
        "lse": pl.BlockSpec((1, 1, 1, wide), lambda b, q: (b, q, 0, 0)),
    }


def attention_forward(meta, qt, kxt, vxt, c, ct):
    batch, nkb, width, _ = c.shape
    wide = GH * width
    sp = attention_specs(nkb, width)
    pairs = batch * 7 * GH * width * width * LAT * 2
    return pl.pallas_call(
        lambda *refs: forward_kernel(nkb, batch, width, *refs),
        grid=(batch, 2),
        in_specs=[sp["meta"], sp["q"], sp["expand"], sp["expand"], sp["c"], sp["ct"]],
        out_specs=[sp["q"], sp["q"], sp["mix"], sp["lse"]],
        out_shape=[
            jax.ShapeDtypeStruct(qt.shape, LOW),
            jax.ShapeDtypeStruct(qt.shape, F32),
            jax.ShapeDtypeStruct((batch, 2, LAT, wide), LOW),
            jax.ShapeDtypeStruct((batch, 2, 1, wide), F32),
        ],
        scratch_shapes=[
            pltpu.VMEM((LAT, wide), LOW),
            pltpu.VMEM((LAT, wide), F32),
            pltpu.VMEM((1, wide), F32),
            pltpu.VMEM((1, wide), F32),
        ],
        compiler_params=pltpu.CompilerParams(
            dimension_semantics=("arbitrary", "arbitrary"), vmem_limit_bytes=VMEM_LIMIT
        ),
        cost_estimate=pl.CostEstimate(
            flops=2 * pairs, bytes_accessed=16 << 20, transcendentals=batch * 7 * GH * width * width
        ),
        name="attention_forward",
    )(meta, qt, kxt, vxt, c, ct)


def attention_backward(meta, qt, dot_, o_full, mix, lse, kxt, vxt, c, ct):
    batch, nkb, width, _ = c.shape
    wide = GH * width
    sp = attention_specs(nkb, width)
    pairs = batch * 7 * GH * width * width * LAT * 2
    return pl.pallas_call(
        lambda *refs: backward_kernel(nkb, batch, width, *refs),
        grid=(batch, 2),
        in_specs=[
            sp["meta"], sp["q"], sp["q"], sp["q"], sp["mix"], sp["lse"],
            sp["expand"], sp["expand"], sp["c"], sp["ct"],
        ],
        out_specs=[sp["q"], sp["c"], sp["expand"], sp["expand"]],
        out_shape=[
            jax.ShapeDtypeStruct(qt.shape, LOW),
            jax.ShapeDtypeStruct(c.shape, F32),
            jax.ShapeDtypeStruct(kxt.shape, F32),
            jax.ShapeDtypeStruct(vxt.shape, F32),
        ],
        scratch_shapes=[
            pltpu.VMEM((LAT, wide), LOW),
            pltpu.VMEM((wide, LAT), LOW),
            pltpu.VMEM((LAT, wide), LOW),
            pltpu.VMEM((wide, LAT), LOW),
            pltpu.VMEM((1, wide), F32),
            pltpu.VMEM((LAT, wide), F32),
            pltpu.VMEM((width, wide), LOW),
            pltpu.VMEM((width, wide), LOW),
        ],
        compiler_params=pltpu.CompilerParams(
            dimension_semantics=("arbitrary", "arbitrary"), vmem_limit_bytes=VMEM_LIMIT
        ),
        cost_estimate=pl.CostEstimate(
            flops=5 * pairs, bytes_accessed=24 << 20, transcendentals=batch * 7 * GH * width * width
        ),
        name="attention_backward",
    )(meta, qt, dot_, o_full, mix, lse, kxt, vxt, c, ct)


class Place:
    def __init__(self):
        self.seq, self.dp = lax.axis_size("seq"), lax.axis_size("dp")
        s, d = lax.axis_index("seq"), lax.axis_index("dp")
        self.core, self.chip = s % 2, s // 2
        self.y, self.x, self.z = s // 2, d % 2, d // 2
        self.square = self.seq == 4 and self.dp == 8

    def pairs(self, move):
        found = []
        for s in range(self.seq):
            for d in range(self.dp):
                target = move(s, d)
                if target is not None:
                    found.append((s * self.dp + d, target[0] * self.dp + target[1]))
        return found

    def send(self, value, move):
        return lax.ppermute(value, ALL, self.pairs(move))

    def to_core(self, value):
        return self.send(value, lambda s, d: (s ^ 1, d))

    def to_y(self, value):
        return self.send(value, lambda s, d: (s ^ 2, d))

    def to_x(self, value):
        return self.send(value, lambda s, d: (s, d ^ 1))

    def to_z(self, value, step):
        return self.send(value, lambda s, d: (s, (d + 2 * step) % 8))

    def up_y(self, value):
        return self.send(value, lambda s, d: (s + 2, d) if s < 2 else None)

    def down_y(self, value):
        return self.send(value, lambda s, d: (s - 2, d) if s >= 2 else None)


def half(value, index, axis, count=2):
    size = value.shape[axis] // count
    return lax.dynamic_slice_in_dim(value, index * size, size, axis)


def ordered(flag, own, other, axis):
    return jnp.where(
        flag == 0, jnp.concatenate([own, other], axis), jnp.concatenate([other, own], axis)
    )


def add_low(own, other):
    return (own.astype(F32) + other.astype(F32)).astype(LOW)


def gather_z(pl_, piece):
    seen = [piece] + [pl_.to_z(piece, k) for k in (1, 2, 3)]
    seen = seen[::-1]
    return lax.dynamic_slice_in_dim(jnp.stack(seen + seen[:3]), 3 - pl_.z, 4, 0)


def gather_xy(pl_, base, x_first):
    if x_first:
        near = pl_.to_x(base)
        far, both = pl_.to_y(base), pl_.to_y(near)
    else:
        far = pl_.to_y(base)
        near, both = pl_.to_x(base), pl_.to_x(far)
    rel = {(0, 0): base, (1, 0): near, (0, 1): far, (1, 1): both}
    out = {}
    for x in range(2):
        for y in range(2):
            a = [jnp.where(pl_.y == y, rel[(r, 0)], rel[(r, 1)]) for r in range(2)]
            out[(x, y)] = jnp.where(pl_.x == x, a[0], a[1])
    return out


def over_x(got, y, cols=slice(None)):
    return jnp.stack([got[(0, y)][..., cols], got[(1, y)][..., cols]], axis=1)


def gather_rows(pl_, piece, x_first):
    got = gather_xy(pl_, gather_z(pl_, piece), x_first)
    block = jnp.concatenate([over_x(got, 0), over_x(got, 1)], axis=-1)
    mine = half(block, pl_.core, 0)
    other = pl_.to_core(half(block, 1 - pl_.core, 0))
    full = ordered(pl_.core, mine, other, -1)
    return full.reshape(-1, full.shape[-1])


def scatter_yx(pl_, keep, send, y_first):
    x, rest = pl_.x, 1 - pl_.x
    if y_first:
        one = add_low(keep, pl_.to_y(send))
        return add_low(half(one, x, 1), pl_.to_x(half(one, rest, 1)))[:, 0]
    one = add_low(half(keep, x, 1), pl_.to_x(half(keep, rest, 1)))
    two = add_low(half(send, x, 1), pl_.to_x(half(send, rest, 1)))
    return add_low(one, pl_.to_y(two))[:, 0]


def scatter_z(pl_, parts):
    total = half(parts, pl_.z, 0, 4)[0].astype(F32)
    for k in (1, 2, 3):
        total = total + pl_.to_z(half(parts, (pl_.z + k) % 4, 0, 4), k)[0].astype(F32)
    return total


def pick(flag, zero, one):
    return jnp.where(flag == 0, zero, one)


def scatter(pl_, zero, one):
    keep, send = pick(pl_.y, zero, one), pick(pl_.y, one, zero)
    a = scatter_yx(pl_, keep[:2], send[:2], True)
    b = scatter_yx(pl_, keep[2:], send[2:], False)
    return scatter_z(pl_, jnp.concatenate([a, b], 0))


def scatter_rows(pl_, grad):
    rows = grad.shape[0] // 4
    grad = grad.reshape(2, 2, rows, 2 * GW)
    mine, other = half(grad, pl_.core, 3), pl_.to_core(half(grad, 1 - pl_.core, 3))
    y = pl_.y
    a = scatter_yx(pl_, half(mine, y, 3), half(mine, 1 - y, 3), True)
    b = scatter_yx(pl_, half(other, y, 3), half(other, 1 - y, 3), False)
    own = scatter_z(pl_, ordered(pl_.core, a, b, 0)).astype(LOW)
    wide = ordered(y, own, pl_.to_y(own), 1)
    return ordered(pl_.core, wide, pl_.to_core(wide), 1).astype(F32)


class Square:
    def __init__(self, place):
        self.p = place

    def gather(self, w):
        p = self.p
        core, y = p.core, p.y
        ff = w["gate"].shape[1] // 2
        quarter = 2 * core + y

        def cols(value, count, index):
            return half(value, index, 1, count).astype(LOW)

        query = cols(w["query"], 4, quarter)
        latent = cols(w["latent"], 4, quarter)
        kv = half(pick(y, w["key"], w["value"]), core, 0).astype(LOW).T
        gains = jnp.stack([w["gain1"], w["gain2"]] + [jnp.zeros_like(w["gain1"])] * 6)
        first_a = jnp.concatenate([query, kv], 1)
        first_b = jnp.concatenate([latent, gains.astype(LOW)], 0)
        za, zb = gather_z(p, first_a), gather_z(p, first_b)
        got_a, got_b = gather_xy(p, za, True), gather_xy(p, zb, False)
        out = {}
        out["query"] = jnp.concatenate(
            [over_x(got_a, 0, slice(0, 256)), over_x(got_a, 1, slice(0, 256))], -1
        ).reshape(D, GW)
        lat = [over_x(got_b, i) for i in range(2)]
        out["latent"] = jnp.concatenate([v[:, :, :128] for v in lat], -1).reshape(D, LAT)
        out["gain1"] = lat[0][:, :, 128].reshape(D)
        out["gain2"] = lat[0][:, :, 129].reshape(D)
        kv_all = jnp.stack([over_x(got_a, i, slice(256, 384)) for i in range(2)])
        mine = half(kv_all, core, 1)
        other = p.to_core(half(kv_all, 1 - core, 1))
        kv_full = ordered(core, mine, other, -1).reshape(2, GW, LAT)
        out["key_t"], out["value_t"] = kv_full[0], kv_full[1]
        out["output"] = gather_rows(p, cols(w["output"], 4, quarter), False)
        gate_up = half(pick(y, w["gate"], w["up"]), core, 1).astype(LOW)
        zg = gather_z(p, gate_up)
        ga, gb = gather_xy(p, zg[:2], True), gather_xy(p, zg[2:], False)
        for i, name in ((0, "gate"), (1, "up")):
            out[name] = jnp.concatenate([over_x(ga, i), over_x(gb, i)], 0).reshape(D, ff)
        out["down"] = gather_rows(p, cols(w["down"], 4, quarter), True)
        return out

    def down(self, grad):
        return scatter_rows(self.p, grad)

    def output(self, grad):
        return scatter_rows(self.p, grad)

    def gate_up(self, gate, up):
        p = self.p
        ff = gate.shape[1]
        own = scatter(p, gate.reshape(4, 2, 128, ff), up.reshape(4, 2, 128, ff)).astype(LOW)
        other = p.to_y(own)
        both = jnp.stack([pick(p.y, own, other), pick(p.y, other, own)])
        full = ordered(p.core, both, p.to_core(both), 2).astype(F32)
        return full[0], full[1]

    def query_kv(self, query, key_t, value_t):
        p = self.p
        kv = jnp.stack([key_t, value_t]).reshape(2, 2, 2, 128, LAT)
        mine, other = half(kv, p.core, 4), p.to_core(half(kv, 1 - p.core, 4))
        kv = ordered(p.core, mine, other, 1)
        query = query.reshape(4, 2, 128, GW)
        own = scatter(
            p,
            jnp.concatenate([query[..., :256], kv[0]], -1),
            jnp.concatenate([query[..., 256:], kv[1]], -1),
        ).astype(LOW)
        other = p.to_y(own)
        zero, one = pick(p.y, own, other), pick(p.y, other, own)
        both = jnp.concatenate([zero[:, :256], one[:, :256], zero[:, 256:], one[:, 256:]], 1)
        far = p.to_core(both)
        grad_query = ordered(p.core, both[:, :GW], far[:, :GW], 1)
        grad_key = ordered(p.core, both[:, GW : GW + 128], far[:, GW : GW + 128], 1)
        grad_value = ordered(p.core, both[:, GW + 128 :], far[:, GW + 128 :], 1)
        return grad_query.astype(F32), grad_key.T.astype(F32), grad_value.T.astype(F32)

    def latent_gains(self, latent, gain1, gain2):
        p = self.p
        latent = latent.reshape(4, 2, 128, LAT)
        rest = jnp.zeros((4, 2, 7, 128), LOW)

        def part(i, gain):
            row = gain.astype(LOW).reshape(4, 2, 1, 128)
            return jnp.concatenate([latent[..., i * 128 : (i + 1) * 128], row, rest], 2)

        own = scatter(p, part(0, gain1), part(1, gain2)).astype(LOW)
        other = p.to_y(own)
        both = ordered(p.y, own, other, 1)
        far = p.to_core(both)
        grad = ordered(p.core, both[:128], far[:128], 1).astype(F32)
        gains = both[128].astype(F32) + far[128].astype(F32)
        return grad, gains[:128], gains[128:]


class Plain:
    def __init__(self, place):
        self.p = place
        count = place.seq // 2
        self.same_core = [[2 * i + c for i in range(count)] for c in range(2)]
        self.chip = [[2 * i, 2 * i + 1] for i in range(count)]

    def gather(self, w):
        core = self.p.core

        def full(value, axis=0):
            return lax.all_gather(value.astype(LOW), "dp", axis=axis, tiled=True)

        out = {name: full(half(w[name], core, 1)) for name in ("query", "latent", "gate", "up")}
        out["key_t"] = half(full(w["key"].T), core, 0)
        out["value_t"] = half(full(w["value"].T), core, 0)
        out["output"] = half(full(w["output"]), core, 0)
        out["down"] = half(full(w["down"]), core, 0)
        out["gain1"], out["gain2"] = full(w["gain1"]), full(w["gain2"])
        return out

    def columns(self, grad):
        share = lax.psum_scatter(grad.astype(LOW), "dp", scatter_dimension=0, tiled=True)
        share = lax.psum(share, "seq", axis_index_groups=self.same_core)
        return lax.all_gather(
            share, "seq", axis=1, tiled=True, axis_index_groups=self.chip
        ).astype(F32)

    def rows(self, grad):
        grad = grad.astype(LOW)
        grad = ordered(self.p.core, grad, jnp.zeros_like(grad), 0)
        share = lax.psum_scatter(grad, "dp", scatter_dimension=0, tiled=True)
        return lax.psum(share, "seq").astype(F32)

    def gain(self, grad):
        share = lax.psum_scatter(grad.astype(LOW), "dp", scatter_dimension=0, tiled=True)
        return lax.psum(share, "seq").astype(F32)

    def down(self, grad):
        return self.rows(grad)

    def output(self, grad):
        return self.rows(grad)

    def gate_up(self, gate, up):
        return self.columns(gate), self.columns(up)

    def query_kv(self, query, key_t, value_t):
        return self.columns(query), self.rows(key_t).T, self.rows(value_t).T

    def latent_gains(self, latent, gain1, gain2):
        return self.columns(latent), self.gain(gain1), self.gain(gain2)


def inverse_rms(values):
    return lax.rsqrt(jnp.mean(values * values, axis=-1, keepdims=True) + EPS)


def norm_back(grad, normed, inverse, gain):
    scaled = grad * gain
    return inverse * (scaled - normed * jnp.mean(scaled * normed, axis=-1, keepdims=True))


def per_device(
    tokens,
    attn_gain,
    query_weight,
    latent_weight,
    key_expand,
    value_expand,
    output_weight,
    mlp_gain,
    gate_weight,
    up_weight,
    down_weight,
    cotangent,
    lengths,
):
    p = Place()
    ways = Square(p) if p.square else Plain(p)
    batch, length, _ = tokens.shape
    count = 2 * batch * length
    w = ways.gather(
        {
            "gain1": attn_gain,
            "query": query_weight,
            "latent": latent_weight,
            "key": key_expand,
            "value": value_expand,
            "output": output_weight,
            "gain2": mlp_gain,
            "gate": gate_weight,
            "up": up_weight,
            "down": down_weight,
        }
    )

    def chip(own):
        return jnp.stack([own, p.to_core(own)], axis=1)

    def chip_sum(partial):
        return partial[:, 0] + p.to_core(partial[:, 1].astype(LOW)).astype(F32)

    gain1, gain2 = w["gain1"].astype(F32), w["gain2"].astype(F32)
    firsts = lengths[:, 0]
    chips = p.seq // 2

    rows = chip(tokens).astype(F32)
    first_low = (rows * inverse_rms(rows) * gain1).astype(LOW)
    first_flat = first_low.reshape(batch, 2 * length, D)
    latent = jnp.einsum(
        "btd,dl->btl", first_flat, w["latent"], preferred_element_type=F32
    ).astype(LOW)
    query_t = jnp.einsum(
        "dn,btd->bnt", w["query"], first_flat, preferred_element_type=F32
    ).astype(LOW)
    blocks = latent.reshape(batch, 2, length, LAT)
    starts = jnp.stack([p.core, 1 - p.core]).astype(jnp.int32) * length
    base = p.chip * 2 * length
    if p.square:
        keys = jnp.concatenate([blocks, p.up_y(blocks)], axis=1)
        far = jnp.where(p.chip == 0, 2 * length, 0)
        key_starts = jnp.concatenate([base + starts, far + starts])
        diag = jnp.zeros((1,), jnp.int32)
    else:
        keys = lax.all_gather(blocks, "seq", axis=1, tiled=True, axis_index_groups=ways.same_core)
        key_starts = (
            2 * length * jnp.arange(chips, dtype=jnp.int32)[:, None] + starts[None, :]
        ).reshape(-1)
        diag = (2 * p.chip).astype(jnp.int32).reshape(1)
    keys_t = jnp.swapaxes(keys, 2, 3)
    meta = jnp.concatenate([key_starts, base + starts, firsts, diag]).astype(jnp.int32)
    out_low, out_full, mixed, lse = attention_forward(
        meta, query_t, w["key_t"], w["value_t"], keys, keys_t
    )
    branch = jnp.einsum("bnt,nd->btd", out_low, w["output"], preferred_element_type=F32)
    middle = tokens.astype(F32) + chip_sum(branch.reshape(batch, 2, length, D))

    inverse2 = inverse_rms(middle)
    normed2 = middle * inverse2
    second = chip((normed2 * gain2).astype(LOW)).reshape(count, D)
    cot = chip(cotangent).reshape(count, D)
    gate = mm(second, w["gate"])
    up = mm(second, w["up"])
    sig = jax.nn.sigmoid(gate)
    act = gate * sig
    hidden = (act * up).astype(LOW)
    layer_out = (middle + chip_sum(mm(hidden, w["down"]).reshape(batch, 2, length, D))).astype(LOW)
    grad_down = ways.down(tn(hidden, cot).astype(LOW))
    d_hidden = nt(cot, w["down"])
    d_gate = (d_hidden * up * sig * (1.0 + gate * (1.0 - sig))).astype(LOW)
    d_up = (d_hidden * act).astype(LOW)
    grad_gate, grad_up = ways.gate_up(tn(second, d_gate).astype(LOW), tn(second, d_up).astype(LOW))
    d_second = chip_sum((nt(d_gate, w["gate"]) + nt(d_up, w["up"])).reshape(batch, 2, length, D))
    gain2_sum = jnp.sum(d_second * normed2, axis=(0, 1))
    d_middle = cotangent.astype(F32) + norm_back(d_second, normed2, inverse2, gain2)

    d_a = chip(d_middle.astype(LOW)).reshape(batch, 2 * length, D)
    grad_output = ways.output(
        jnp.einsum("bnt,btd->nd", out_low, d_a, preferred_element_type=F32).astype(LOW)
    )
    d_out_t = jnp.einsum(
        "nd,btd->bnt", w["output"], d_a, preferred_element_type=F32
    ).astype(LOW)
    dq_t, d_keys, d_key_t, d_value_t = attention_backward(
        meta, query_t, d_out_t, out_full, mixed, lse, w["key_t"], w["value_t"], keys, keys_t
    )
    if p.square:
        d_blocks = d_keys[:, :2] + p.down_y(d_keys[:, 2:].astype(LOW)).astype(F32)
    else:
        d_blocks = lax.psum_scatter(
            d_keys.astype(LOW),
            "seq",
            scatter_dimension=1,
            tiled=True,
            axis_index_groups=ways.same_core,
        )
    d_latent = d_blocks.astype(LOW).reshape(batch, 2 * length, LAT)
    grad_query, grad_key, grad_value = ways.query_kv(
        jnp.einsum("btd,bnt->dn", first_flat, dq_t, preferred_element_type=F32).astype(LOW),
        d_key_t.astype(LOW),
        d_value_t.astype(LOW),
    )
    d_first = jnp.einsum(
        "bnt,dn->btd", dq_t, w["query"], preferred_element_type=F32
    ) + jnp.einsum("btl,dl->btd", d_latent, w["latent"], preferred_element_type=F32)
    d_first = chip_sum(d_first.reshape(batch, 2, length, D))
    own = tokens.astype(F32)
    inverse1 = inverse_rms(own)
    normed1 = own * inverse1
    gain1_sum = jnp.sum(d_first * normed1, axis=(0, 1))
    grad_tokens = d_middle + norm_back(d_first, normed1, inverse1, gain1)
    grad_latent, grad_gain1, grad_gain2 = ways.latent_gains(
        jnp.einsum("btd,btl->dl", first_flat, d_latent, preferred_element_type=F32).astype(LOW),
        gain1_sum,
        gain2_sum,
    )
    return (
        layer_out,
        grad_tokens,
        grad_gain1,
        grad_query,
        grad_latent,
        grad_key,
        grad_value,
        grad_output,
        grad_gain2,
        grad_gate,
        grad_up,
        grad_down,
    )


def solution(mesh):
    rows, gain, weight, across = P("dp", "seq", None), P("dp"), P("dp", None), P(None, "dp")
    return jax.shard_map(
        per_device,
        mesh=mesh,
        in_specs=(
            rows, gain, weight, weight, across, across, weight, gain, weight, weight, weight, rows,
            P("dp", None),
        ),
        out_specs=(
            rows, rows, gain, weight, weight, across, across, weight, gain, weight, weight, weight,
        ),
        check_vma=False,
    )
```

```python
import jax
import jax.numpy as jnp
from jax import lax
from jax.experimental import pallas as pl
from jax.experimental.pallas import tpu as pltpu
from jax.sharding import PartitionSpec as P

D = 1024
H = 16
HD = 64
KVH = 2
LAT = 256
GH = H // KVH
GW = D // KVH
EPS = 1e-06
SCALE = HD ** (-0.5)
LOG2E = 1.4426950408889634
NEG = -1e30

LOW = jnp.bfloat16
F32 = jnp.float32
ALL = ("seq", "dp")
VMEM_LIMIT = 56 * 1024 * 1024


def mm(left, right):
    return jnp.dot(left, right, preferred_element_type=F32)


def tn(left, right):
    return lax.dot_general(left, right, (((0,), (0,)), ((), ())), preferred_element_type=F32)


def nt(left, right):
    return lax.dot_general(left, right, (((1,), (1,)), ((), ())), preferred_element_type=F32)


def block_bias(k0, q0, first, width):
    kpos = k0 + lax.broadcasted_iota(jnp.int32, (width, width), 0)
    qpos = q0 + lax.broadcasted_iota(jnp.int32, (width, width), 1)
    lowest = jnp.where(qpos >= first, first, 0)
    return jnp.where((kpos <= qpos) & (kpos >= lowest), 0.0, NEG)


def block_needed(k0, q0, first, width):
    before = jnp.logical_and(q0 >= first, k0 + (width - 1) < first)
    return jnp.logical_and(k0 <= q0, jnp.logical_not(before))


def forward_kernel(b, nkb, batch, width, meta, qt, kxt, vxt, c, o_low, o_full, mix_out, lse_out, q_s, acc, m_s, l_s):
    qb = pl.program_id(0)
    q0, first, diag = meta[nkb + qb], meta[nkb + 2 + b], meta[nkb + 2 + batch] + qb
    for h in range(GH):
        cols = slice(h * width, (h + 1) * width)
        rows = slice(h * HD, (h + 1) * HD)
        q_s[:, cols] = (tn(kxt[rows, :], qt[0, rows, :]) * (SCALE * LOG2E)).astype(LOW)
    m_s[...] = jnp.full_like(m_s, NEG)
    l_s[...] = jnp.zeros_like(l_s)
    acc[...] = jnp.zeros_like(acc)

    def step(j, carry):
        kb = lax.rem(diag + j, nkb)
        k0 = meta[kb]

        @pl.when(block_needed(k0, q0, first, width))
        def _():
            bias = block_bias(k0, q0, first, width)
            keys = c[0, kb]
            keys_t = keys.T
            for h in range(GH):
                cols = slice(h * width, (h + 1) * width)
                s = mm(keys, q_s[:, cols]) + bias
                m_old = m_s[:, cols]
                m_new = jnp.maximum(m_old, jnp.max(s, axis=0, keepdims=True))
                p = jnp.exp2(s - m_new)
                alpha = jnp.exp2(m_old - m_new)
                m_s[:, cols] = m_new
                l_s[:, cols] = l_s[:, cols] * alpha + jnp.sum(p, axis=0, keepdims=True)
                acc[:, cols] = acc[:, cols] * alpha + mm(keys_t, p.astype(LOW))

        return carry

    lax.fori_loop(0, nkb, step, 0)
    for h in range(GH):
        cols = slice(h * width, (h + 1) * width)
        rows = slice(h * HD, (h + 1) * HD)
        total = l_s[:, cols]
        mixed = (acc[:, cols] * (1.0 / total)).astype(LOW)
        mix_out[0, :, cols] = mixed
        out = mm(vxt[rows, :], mixed)
        o_full[0, rows, :] = out
        o_low[0, rows, :] = out.astype(LOW)
        lse_out[0, :, cols] = m_s[:, cols] + jnp.log(total) * LOG2E


def backward_kernel(
    b, qb, nkb, batch, width, add_dc, add_dw, meta, qt, dot_, o_full, mix, lse, kxt, vxt, c, *refs
):
    refs = list(refs)
    dc_old = refs.pop(0) if add_dc else None
    dk_old, dv_old = (refs.pop(0), refs.pop(0)) if add_dw else (None, None)
    dqt, dc, dkxt, dvxt, q_s, q_n, do_t, do_n, delta, dq, ds_s, p_s = refs
    q0, first, diag = meta[nkb + qb], meta[nkb + 2 + b], meta[nkb + 2 + batch] + qb
    dc[...] = dc_old[...] if add_dc else jnp.zeros_like(dc)

    for h in range(GH):
        cols = slice(h * width, (h + 1) * width)
        rows = slice(h * HD, (h + 1) * HD)
        qh, kh, doh, vh = qt[0, rows, :], kxt[rows, :], dot_[0, rows, :], vxt[rows, :]
        q_s[:, cols] = (tn(kh, qh) * (SCALE * LOG2E)).astype(LOW)
        q_n[cols, :] = (tn(qh, kh) * SCALE).astype(LOW)
        do_t[:, cols] = tn(vh, doh).astype(LOW)
        do_n[cols, :] = tn(doh, vh).astype(LOW)
        delta[:, cols] = jnp.sum(doh.astype(F32) * o_full[0, rows, :], axis=0, keepdims=True)
    dq[...] = jnp.zeros_like(dq)

    def step(j, carry):
        kb = lax.rem(diag + j, nkb)
        k0 = meta[kb]

        @pl.when(block_needed(k0, q0, first, width))
        def _():
            bias = block_bias(k0, q0, first, width)
            keys = c[0, kb]
            keys_t = keys.T
            for h in range(GH):
                cols = slice(h * width, (h + 1) * width)
                s = mm(keys, q_s[:, cols]) + bias
                p = jnp.exp2(s - lse[0, :, cols])
                dp = mm(keys, do_t[:, cols])
                ds = (p * (dp - delta[:, cols])).astype(LOW)
                p_s[:, cols] = p.astype(LOW)
                ds_s[:, cols] = ds
                dq[:, cols] += mm(keys_t, ds)
            dc[kb] += mm(ds_s[...], q_n[...]) + mm(p_s[...], do_n[...])

        return carry

    lax.fori_loop(0, nkb, step, 0)
    for h in range(GH):
        cols = slice(h * width, (h + 1) * width)
        rows = slice(h * HD, (h + 1) * HD)
        dq_low = (dq[:, cols] * SCALE).astype(LOW)
        dqt[rows, :] = mm(kxt[rows, :], dq_low).astype(LOW)
        dk, dv = nt(qt[0, rows, :], dq_low), nt(dot_[0, rows, :], mix[0, :, cols])
        dkxt[rows, :] = dk + dk_old[rows, :] if add_dw else dk
        dvxt[rows, :] = dv + dv_old[rows, :] if add_dw else dv


def attention_forward(b, meta, qt, kxt, vxt, c):
    batch, nkb, width, _ = c.shape
    wide = GH * width
    pairs = 7 * GH * width * width * LAT
    expand = pl.BlockSpec((GW, LAT), lambda q: (0, 0))
    out_spec = pl.BlockSpec((1, GW, width), lambda q: (0, 0, q))
    return pl.pallas_call(
        lambda *refs: forward_kernel(b, nkb, batch, width, *refs),
        grid=(2,),
        in_specs=[
            pl.BlockSpec(memory_space=pltpu.SMEM),
            pl.BlockSpec((1, GW, width), lambda q: (b, 0, q)),
            expand,
            expand,
            pl.BlockSpec((1, nkb, width, LAT), lambda q: (b, 0, 0, 0)),
        ],
        out_specs=[
            out_spec,
            out_spec,
            pl.BlockSpec((1, LAT, wide), lambda q: (q, 0, 0)),
            pl.BlockSpec((1, 1, wide), lambda q: (q, 0, 0)),
        ],
        out_shape=[
            jax.ShapeDtypeStruct((1, GW, 2 * width), LOW),
            jax.ShapeDtypeStruct((1, GW, 2 * width), F32),
            jax.ShapeDtypeStruct((2, LAT, wide), LOW),
            jax.ShapeDtypeStruct((2, 1, wide), F32),
        ],
        scratch_shapes=[
            pltpu.VMEM((LAT, wide), LOW),
            pltpu.VMEM((LAT, wide), F32),
            pltpu.VMEM((1, wide), F32),
            pltpu.VMEM((1, wide), F32),
        ],
        compiler_params=pltpu.CompilerParams(
            dimension_semantics=("arbitrary",), vmem_limit_bytes=VMEM_LIMIT
        ),
        cost_estimate=pl.CostEstimate(
            flops=4 * pairs, bytes_accessed=8 << 20, transcendentals=7 * GH * width * width
        ),
        name="attention_forward",
    )(meta, qt, kxt, vxt, c)


def attention_backward(b, qb, meta, qt, dot_, o_full, mix, lse, kxt, vxt, c, old_dc, old_dw):
    batch, nkb, width, _ = c.shape
    wide = GH * width
    pairs = 4 * GH * width * width * LAT * 2
    q_spec = pl.BlockSpec((1, GW, width), lambda i: (b, 0, qb))
    expand = pl.BlockSpec((GW, LAT), lambda i: (0, 0))
    return pl.pallas_call(
        lambda *refs: backward_kernel(
            b, qb, nkb, batch, width, bool(old_dc), bool(old_dw), *refs
        ),
        grid=(1,),
        in_specs=[
            pl.BlockSpec(memory_space=pltpu.SMEM),
            q_spec,
            q_spec,
            pl.BlockSpec((1, GW, width), lambda i: (0, 0, qb)),
            pl.BlockSpec((1, LAT, wide), lambda i: (qb, 0, 0)),
            pl.BlockSpec((1, 1, wide), lambda i: (qb, 0, 0)),
            expand,
            expand,
            pl.BlockSpec((1, nkb, width, LAT), lambda i: (b, 0, 0, 0)),
        ]
        + [pl.BlockSpec((nkb, width, LAT), lambda i: (0, 0, 0))] * len(old_dc)
        + [expand] * len(old_dw),
        out_specs=[
            pl.BlockSpec((GW, width), lambda i: (0, 0)),
            pl.BlockSpec((nkb, width, LAT), lambda i: (0, 0, 0)),
            expand,
            expand,
        ],
        out_shape=[
            jax.ShapeDtypeStruct((GW, width), LOW),
            jax.ShapeDtypeStruct((nkb, width, LAT), F32),
            jax.ShapeDtypeStruct(kxt.shape, F32),
            jax.ShapeDtypeStruct(vxt.shape, F32),
        ],
        scratch_shapes=[
            pltpu.VMEM((LAT, wide), LOW),
            pltpu.VMEM((wide, LAT), LOW),
            pltpu.VMEM((LAT, wide), LOW),
            pltpu.VMEM((wide, LAT), LOW),
            pltpu.VMEM((1, wide), F32),
            pltpu.VMEM((LAT, wide), F32),
            pltpu.VMEM((width, wide), LOW),
            pltpu.VMEM((width, wide), LOW),
        ],
        compiler_params=pltpu.CompilerParams(
            dimension_semantics=("arbitrary",), vmem_limit_bytes=VMEM_LIMIT
        ),
        cost_estimate=pl.CostEstimate(
            flops=5 * pairs, bytes_accessed=6 << 20, transcendentals=4 * GH * width * width
        ),
        name="attention_backward",
    )(meta, qt, dot_, o_full, mix, lse, kxt, vxt, c, *old_dc, *old_dw)


class Place:
    def __init__(self):
        self.seq, self.dp = lax.axis_size("seq"), lax.axis_size("dp")
        s, d = lax.axis_index("seq"), lax.axis_index("dp")
        self.core, self.chip = s % 2, s // 2
        self.y, self.x, self.z = s // 2, d % 2, d // 2
        self.square = self.seq == 4 and self.dp == 8

    def pairs(self, move):
        found = []
        for s in range(self.seq):
            for d in range(self.dp):
                target = move(s, d)
                if target is not None:
                    found.append((s * self.dp + d, target[0] * self.dp + target[1]))
        return found

    def send(self, value, move):
        return lax.ppermute(value, ALL, self.pairs(move))

    def to_core(self, value):
        return self.send(value, lambda s, d: (s ^ 1, d))

    def to_y(self, value):
        return self.send(value, lambda s, d: (s ^ 2, d))

    def to_x(self, value):
        return self.send(value, lambda s, d: (s, d ^ 1))

    def to_z(self, value, step):
        return self.send(value, lambda s, d: (s, (d + 2 * step) % 8))

    def up_y(self, value):
        return self.send(value, lambda s, d: (s + 2, d) if s < 2 else None)

    def down_y(self, value):
        return self.send(value, lambda s, d: (s - 2, d) if s >= 2 else None)


def half(value, index, axis, count=2):
    size = value.shape[axis] // count
    return lax.dynamic_slice_in_dim(value, index * size, size, axis)


def ordered(flag, own, other, axis):
    return jnp.where(
        flag == 0, jnp.concatenate([own, other], axis), jnp.concatenate([other, own], axis)
    )


def after(value, *others):
    return lax.optimization_barrier((value, others))[0]


def add_low(own, other):
    return (own.astype(F32) + other.astype(F32)).astype(LOW)


class Plain:
    def __init__(self, place):
        self.p = place
        count = place.seq // 2
        self.same_core = [[2 * i + c for i in range(count)] for c in range(2)]
        self.chip = [[2 * i, 2 * i + 1] for i in range(count)]

    def gather(self, w):
        core = self.p.core

        def full(value, axis=0):
            return lax.all_gather(value.astype(LOW), "dp", axis=axis, tiled=True)

        out = {name: full(half(w[name], core, 1)) for name in ("query", "latent", "gate", "up")}
        out["key_t"] = half(full(w["key"].T), core, 0)
        out["value_t"] = half(full(w["value"].T), core, 0)
        out["output"] = half(full(w["output"]), core, 0)
        out["down"] = half(full(w["down"]), core, 0)
        out["gain1"], out["gain2"] = full(w["gain1"]), full(w["gain2"])
        return out

    def columns(self, grad):
        share = lax.psum_scatter(grad.astype(LOW), "dp", scatter_dimension=0, tiled=True)
        share = lax.psum(share, "seq", axis_index_groups=self.same_core)
        return lax.all_gather(
            share, "seq", axis=1, tiled=True, axis_index_groups=self.chip
        ).astype(F32)

    def rows(self, grad):
        grad = grad.astype(LOW)
        grad = ordered(self.p.core, grad, jnp.zeros_like(grad), 0)
        share = lax.psum_scatter(grad, "dp", scatter_dimension=0, tiled=True)
        return lax.psum(share, "seq").astype(F32)

    def gain(self, grad):
        share = lax.psum_scatter(grad.astype(LOW), "dp", scatter_dimension=0, tiled=True)
        return lax.psum(share, "seq").astype(F32)


def inverse_rms(values):
    return lax.rsqrt(jnp.mean(values * values, axis=-1, keepdims=True) + EPS)


def norm_back(grad, normed, inverse, gain):
    scaled = grad * gain
    return inverse * (scaled - normed * jnp.mean(scaled * normed, axis=-1, keepdims=True))


def dots(spec, left, right):
    return jnp.einsum(spec, left, right, preferred_element_type=F32)


def pick(flag, zero, one):
    return jnp.where(flag == 0, zero, one)


def chip(p, own):
    return jnp.stack([own, p.to_core(own)], axis=1)


def chip_sum(p, partial):
    return partial[:, 0] + p.to_core(partial[:, 1].astype(LOW)).astype(F32)


def plain_layer(
    p, tokens, attn_gain, query_weight, latent_weight, key_expand, value_expand, output_weight,
    mlp_gain, gate_weight, up_weight, down_weight, cotangent, lengths,
):
    ways = Plain(p)
    batch, length, _ = tokens.shape
    count = 2 * batch * length
    w = ways.gather(
        {
            "gain1": attn_gain, "query": query_weight, "latent": latent_weight,
            "key": key_expand, "value": value_expand, "output": output_weight,
            "gain2": mlp_gain, "gate": gate_weight, "up": up_weight, "down": down_weight,
        }
    )
    gain1, gain2 = w["gain1"].astype(F32), w["gain2"].astype(F32)
    firsts = lengths[:, 0]
    chips = p.seq // 2
    rows = chip(p, tokens).astype(F32)
    first_low = (rows * inverse_rms(rows) * gain1).astype(LOW)
    first_flat = first_low.reshape(batch, 2 * length, D)
    latent = dots("btd,dl->btl", first_flat, w["latent"]).astype(LOW)
    query_t = dots("dn,btd->bnt", w["query"], first_flat).astype(LOW)
    blocks = latent.reshape(batch, 2, length, LAT)
    starts = jnp.stack([p.core, 1 - p.core]).astype(jnp.int32) * length
    base = p.chip * 2 * length
    keys = lax.all_gather(blocks, "seq", axis=1, tiled=True, axis_index_groups=ways.same_core)
    key_starts = (
        2 * length * jnp.arange(chips, dtype=jnp.int32)[:, None] + starts[None, :]
    ).reshape(-1)
    diag = (2 * p.chip).astype(jnp.int32).reshape(1)
    meta = jnp.concatenate([key_starts, base + starts, firsts, diag]).astype(jnp.int32)
    att = [
        attention_forward(b, meta, query_t, w["key_t"], w["value_t"], keys)
        for b in range(batch)
    ]
    out_low = jnp.concatenate([a[0] for a in att])
    branch = dots("bnt,nd->btd", out_low, w["output"])
    middle = tokens.astype(F32) + chip_sum(p, branch.reshape(batch, 2, length, D))
    inverse2 = inverse_rms(middle)
    normed2 = middle * inverse2
    second = chip(p, (normed2 * gain2).astype(LOW)).reshape(count, D)
    cot = chip(p, cotangent).reshape(count, D)
    gate = mm(second, w["gate"])
    up = mm(second, w["up"])
    sig = jax.nn.sigmoid(gate)
    act = gate * sig
    hidden = (act * up).astype(LOW)
    partial = mm(hidden, w["down"]).reshape(batch, 2, length, D)
    layer_out = (middle + chip_sum(p, partial)).astype(LOW)
    grad_down = ways.rows(tn(hidden, cot))
    d_hidden = nt(cot, w["down"])
    d_gate = (d_hidden * up * sig * (1.0 + gate * (1.0 - sig))).astype(LOW)
    d_up = (d_hidden * act).astype(LOW)
    grad_gate, grad_up = ways.columns(tn(second, d_gate)), ways.columns(tn(second, d_up))
    partial = (nt(d_gate, w["gate"]) + nt(d_up, w["up"])).reshape(batch, 2, length, D)
    d_second = chip_sum(p, partial)
    gain2_sum = jnp.sum(d_second * normed2, axis=(0, 1))
    d_middle = cotangent.astype(F32) + norm_back(d_second, normed2, inverse2, gain2)
    d_a = chip(p, d_middle.astype(LOW)).reshape(batch, 2 * length, D)
    grad_output = ways.rows(dots("bnt,btd->nd", out_low, d_a))
    d_out_t = dots("nd,btd->bnt", w["output"], d_a).astype(LOW)
    d_queries, d_keys, sums = [], [], ()
    for b in range(batch):
        far = ()
        for qb in range(2):
            found = attention_backward(
                b, qb, meta, query_t, d_out_t, *att[b][1:], w["key_t"], w["value_t"], keys,
                far, sums,
            )
            far, sums = found[1:2], found[2:]
            d_queries.append(found[0])
        d_keys.append(far[0])
    dq_t = jnp.stack([jnp.concatenate(d_queries[2 * b : 2 * b + 2], 1) for b in range(batch)])
    d_keys = jnp.stack(d_keys)
    d_key_t, d_value_t = sums
    d_blocks = lax.psum_scatter(
        d_keys.astype(LOW), "seq", scatter_dimension=1, tiled=True,
        axis_index_groups=ways.same_core,
    )
    d_latent = d_blocks.astype(LOW).reshape(batch, 2 * length, LAT)
    grad_query = ways.columns(dots("btd,bnt->dn", first_flat, dq_t))
    grad_latent = ways.columns(dots("btd,btl->dl", first_flat, d_latent))
    d_first = dots("bnt,dn->btd", dq_t, w["query"]) + dots("btl,dl->btd", d_latent, w["latent"])
    d_first = chip_sum(p, d_first.reshape(batch, 2, length, D))
    own = tokens.astype(F32)
    inverse1 = inverse_rms(own)
    normed1 = own * inverse1
    gain1_sum = jnp.sum(d_first * normed1, axis=(0, 1))
    grad_tokens = d_middle + norm_back(d_first, normed1, inverse1, gain1)
    return (
        layer_out, grad_tokens, ways.gain(gain1_sum), grad_query, grad_latent,
        ways.rows(d_key_t).T, ways.rows(d_value_t).T, grad_output, ways.gain(gain2_sum),
        grad_gate, grad_up, grad_down,
    )


class Live:
    def __init__(self, values):
        self.__dict__.update(values)

    @property
    def pop(self):
        return Taken(self)


class Taken:
    def __init__(self, live):
        self.live = live

    def __getattr__(self, name):
        return self.live.__dict__.pop(name)


def sync(v):
    return Live(lax.optimization_barrier(dict(v.__dict__)))


def z_gather(p, piece):
    seen = [piece] + [p.to_z(piece, k) for k in (1, 2, 3)]
    out = []
    for z in range(4):
        back = (p.z - z) % 4
        pair = [jnp.where(back % 2 == 0, seen[k], seen[k + 1]) for k in (0, 2)]
        out.append(jnp.where(back < 2, pair[0], pair[1]))
    return jnp.stack(out)


def z_scatter(p, parts):
    total = half(parts, p.z, 0, 4)[0].astype(F32)
    for k in (1, 2, 3):
        total = total + p.to_z(half(parts, (p.z + k) % 4, 0, 4), k)[0].astype(F32)
    return total.astype(LOW)


def to_xy(p, value):
    return p.send(value, lambda s, d: (s ^ 2, d ^ 1))


def add_all(parts):
    return sum(part.astype(F32) for part in parts).astype(LOW)


def place_kernel(plan, sources, outs, where, *refs):
    src, dst = refs[:sources], refs[sources:]
    spot = where[0], where[1], where[2]
    for make in plan:
        source, there, out, here = make(*spot)
        dst[out][here] = src[source][there].astype(LOW)


def placed(p, plan, sources, shapes):
    where = jnp.stack([p.x, p.y, p.core]).astype(jnp.int32)
    inside = pl.BlockSpec(memory_space=pltpu.VMEM)
    return pl.pallas_call(
        lambda *refs: place_kernel(plan, len(sources), len(shapes), *refs),
        in_specs=[pl.BlockSpec(memory_space=pltpu.SMEM)] + [inside] * len(sources),
        out_specs=[inside] * len(shapes),
        out_shape=[jax.ShapeDtypeStruct(shape, LOW) for shape in shapes],
        compiler_params=pltpu.CompilerParams(vmem_limit_bytes=VMEM_LIMIT),
        name="place",
    )(where, *sources)


def lanes(start, width):
    return pl.ds(pl.multiple_of(start, 128), width)


RELATIVE = [(0, 0), (1, 0), (0, 1), (1, 1)]


def spread(p, parts):
    return parts[0], p.to_x(parts[1]), p.to_y(parts[2]), to_xy(p, parts[3])


def square_layer(
    p, tokens, attn_gain, query_weight, latent_weight, key_expand, value_expand, output_weight,
    mlp_gain, gate_weight, up_weight, down_weight, cotangent, lengths,
):
    batch, length, _ = tokens.shape
    count = 2 * batch * length
    core, x, y = p.core, p.x, p.y
    ff = gate_weight.shape[1] // 2
    quarter = 2 * core + y
    v = Live({})

    def cols(value, parts, index):
        return half(value, index, 1, parts).astype(LOW)

    def x_own(value):
        return half(value, x, 1)

    def x_other(value):
        return half(value, 1 - x, 1)

    v.pgu = jnp.concatenate([cols(gate_weight, 2, core), cols(up_weight, 2, core)], 1)
    v.tok = p.to_core(tokens)
    v = sync(v)
    kv = half(pick(y, key_expand, value_expand), core, 0).astype(LOW).T
    gains = jnp.stack([attn_gain, mlp_gain] + [jnp.zeros_like(attn_gain)] * 6).astype(LOW)
    piece = [
        cols(latent_weight, 4, quarter), cols(output_weight, 4, quarter),
        cols(query_weight, 4, quarter), kv,
    ]
    piece = jnp.concatenate(piece, 1)
    pad = jnp.zeros((8, piece.shape[1] - 128), LOW)
    piece = jnp.concatenate([piece, jnp.concatenate([gains, pad], 1)], 0)
    first = z_gather(p, piece)
    v.a, v.b = first[:, :, :384], first[:, :, 384:]
    rows = jnp.stack([tokens, v.pop.tok], 1).astype(F32)
    v.normed1 = rows * inverse_rms(rows)
    v.pd = cols(down_weight, 4, quarter)
    v = sync(v)

    w_gu = lax.all_gather(v.pop.pgu, "dp", axis=0, tiled=True)
    v.ax, v.by = p.to_x(v.a), p.to_y(v.b)
    v = sync(v)
    v.ay, v.axy = p.to_y(v.a), p.to_y(v.ax)
    v.bx, v.bxy = p.to_x(v.b), p.to_x(v.by)
    v = sync(v)

    v.from_ab = (v.pop.a, v.pop.ax, v.pop.ay, v.pop.axy, v.pop.b, v.pop.bx, v.pop.by, v.pop.bxy)
    plan = []
    for n, (r, k) in enumerate(RELATIVE):
        low = pl.ds(0, 128)
        plan += [
            lambda x, y, c, n=n, r=r, k=k: (
                n, (slice(None), low, pl.ds(0, 128)), 0,
                (slice(None), x ^ r, slice(None), lanes((y ^ k) * 128, 128)),
            ),
            lambda x, y, c, n=n, r=r, k=k: (
                4 + n, (slice(None), low, pl.ds(0, 256)), 1,
                (slice(None), x ^ r, slice(None), lanes((y ^ k) * 256, 256)),
            ),
            lambda x, y, c, n=n: (n, (pl.ds(2 * (1 - c), 2), low, pl.ds(128, 256)), 2, n),
            lambda x, y, c, n=n: (4 + n, (pl.ds(2 * (1 - c), 2), low, pl.ds(256, 128)), 3, n),
        ]
    wl, wq, v.wo_send, v.kv_send = placed(
        p, plan, v.from_ab,
        [(4, 2, 128, LAT), (4, 2, 128, GW), (4, 2, 128, 256), (4, 2, 128, 128)],
    )
    v.wl, v.wq = wl.reshape(D, LAT), wq.reshape(D, GW)
    gains = [part[:, 128:130, :128] for part in v.from_ab[:2]]
    gains = pick(x, jnp.stack(gains, 2), jnp.stack(gains[::-1], 2)).astype(F32)
    v.gain1, v.gain2 = gains[:, 0].reshape(D), gains[:, 1].reshape(D)
    v.first = (v.pop.normed1 * v.gain1).astype(LOW).reshape(batch, 2 * length, D)
    v.keys = dots("btd,dl->btl", v.first, v.wl).astype(LOW).reshape(batch, 2, length, LAT)
    v = sync(v)
    far_keys = p.up_y(v.keys)
    wo_come, kv_come = p.to_core(v.pop.wo_send), p.to_core(v.pop.kv_send)
    v.zd = z_gather(p, v.pop.pd)
    v.qt = dots("dn,btd->bnt", v.wq, v.first).astype(LOW)
    plan = []
    for n, (r, k) in enumerate(RELATIVE):
        for s in range(2):
            plan += [
                lambda x, y, c, n=n, r=r, k=k, s=s: (
                    (n, (pl.ds(2 * c, 2), pl.ds(0, 128), pl.ds(128, 256))) if s == 0 else (8, n)
                ) + (0, (slice(None), x ^ r, slice(None), lanes(((c ^ s) * 2 + (y ^ k)) * 256, 256))),
                lambda x, y, c, n=n, r=r, k=k, s=s: (
                    (4 + n, (pl.ds(2 * c, 2), pl.ds(0, 128), pl.ds(256, 128))) if s == 0 else (9, n)
                ) + (1, (y ^ k, slice(None), x ^ r, slice(None), lanes((c ^ s) * 128, 128))),
            ]
    wo, kv = placed(
        p, plan, (*v.pop.from_ab, wo_come, kv_come), [(2, 2, 128, D), (2, 2, 2, 128, LAT)]
    )
    v.wo, kv = wo.reshape(GW, D), kv.reshape(2, GW, LAT)
    v.kxt, v.vxt = kv[0], kv[1]
    starts = jnp.stack([core, 1 - core]).astype(jnp.int32) * length
    base = p.chip * 2 * length
    far = pick(p.chip, 2 * length, 0)
    meta = [base + starts, far + starts, base + starts, lengths[:, 0], jnp.zeros((1,), jnp.int32)]
    v.meta = jnp.concatenate(meta).astype(jnp.int32)
    v.keys = jnp.concatenate([v.keys, far_keys], axis=1)
    v = sync(v)

    def forward(b):
        return attention_forward(b, v.meta, v.qt, v.kxt, v.vxt, v.keys)

    v.dax, v.dby = p.to_x(v.zd[:2]), p.to_y(v.zd[2:])
    v.cot = chip(p, cotangent).reshape(count, D)
    v.att0 = forward(0)
    v = sync(v)
    v.day, v.daxy = p.to_y(v.zd[:2]), p.to_y(v.dax)
    v.dbx, v.dbxy = p.to_x(v.zd[2:]), p.to_x(v.dby)
    cot = half(v.cot, core, 1)
    v.cot_c = [half(cot, i, 1) for i in (y, 1 - y)] + [half(v.cot, 1 - core, 1)]
    v.att1 = forward(1)
    v = sync(v)

    down = (v.pop.zd, v.pop.dax, v.pop.day, v.pop.daxy, v.pop.dby, v.pop.dbx, v.pop.dbxy)
    fronts = [down[0][:2], down[1], down[2], down[3]]
    backs = [down[0][2:], down[5], down[4], down[6]]
    mine = [pick(core, front, back) for front, back in zip(fronts, backs)]
    come = [p.to_core(pick(core, back, front)) for front, back in zip(fronts, backs)]
    v.down = mine + come
    v.out = jnp.concatenate([v.att0[0], v.att1[0]])
    branch = dots("bnt,nd->btd", v.out, v.wo).reshape(batch, 2, length, D)
    v.middle = tokens.astype(F32) + chip_sum(p, branch)
    v.inv2 = inverse_rms(v.middle)
    second = v.middle * v.inv2 * v.gain2
    v.second = chip(p, second.astype(LOW)).reshape(count, D)
    v = sync(v)

    plan = []
    for n, (r, k) in enumerate(RELATIVE):
        for s in range(2):
            plan += [
                lambda x, y, c, n=n, r=r, k=k, s=s: (
                    4 * s + n, slice(None), 0,
                    (slice(None), x ^ r, slice(None), lanes(((c ^ s) * 2 + (y ^ k)) * 256, 256)),
                )
            ]
    wd = placed(p, plan, v.pop.down, [(2, 2, ff // 4, D)])[0]
    v.wd = wd.reshape(ff, D)
    v.w_gu = w_gu
    v = sync(v)
    v.act = mm(v.second, v.w_gu)
    gate, up = v.act[:, :ff], v.act[:, ff:]
    v.hidden = (gate * jax.nn.sigmoid(gate) * up).astype(LOW)
    cot_y, cot_far, cot_core = v.pop.cot_c
    v.gd_a = tn(v.hidden, cot_y).astype(LOW).reshape(2, 2, -1, 256)
    v.gd_ay = tn(v.hidden, cot_far).astype(LOW).reshape(2, 2, -1, 256)
    v.gd_send = tn(v.hidden, cot_core).astype(LOW).reshape(2, 2, -1, 512)
    v = sync(v)

    v.gd_b = p.to_core(v.pop.gd_send)
    gate, up = v.act[:, :ff], v.pop.act[:, ff:]
    sig = jax.nn.sigmoid(gate)
    d_hidden = nt(v.cot, v.wd)
    d_gate = d_hidden * up * sig * (1.0 + gate * (1.0 - sig))
    d_up = d_hidden * (gate * sig)
    v.d_gu = jnp.concatenate([d_gate, d_up], 1).astype(LOW)
    v = sync(v)
    v.gd_ay, v.gd_bx = p.to_y(v.gd_ay), p.to_x(x_other(v.gd_b))
    v.gg = tn(v.pop.second, v.d_gu).astype(LOW)
    v = sync(v)
    gg = lax.psum_scatter(v.pop.gg, "dp", scatter_dimension=0, tiled=True)
    v.gd_a = add_low(v.gd_a, v.pop.gd_ay)
    v.gd_b = add_low(x_own(v.gd_b), v.pop.gd_bx)
    v.gd_ax, v.gd_by = p.to_x(x_other(v.gd_a)), p.to_y(half(v.gd_b, 1 - y, 3))
    d_second = chip_sum(p, nt(v.pop.d_gu, v.pop.w_gu).reshape(batch, 2, length, D))
    normed2 = v.middle * v.inv2
    v.gain2_sum = jnp.sum(d_second * normed2, axis=(0, 1))
    v.d_middle = cotangent.astype(F32) + norm_back(d_second, normed2, v.pop.inv2, v.pop.gain2)
    v = sync(v)
    v.d_a = chip(p, v.d_middle.astype(LOW)).reshape(batch, 2 * length, D)
    gd_a = add_low(x_own(v.pop.gd_a), v.pop.gd_ax)[:, 0]
    gd_b = add_low(half(v.pop.gd_b, y, 3), v.pop.gd_by)[:, 0]
    v.gd = ordered(core, gd_a, gd_b, 0)
    partial = mm(v.pop.hidden, v.pop.wd).reshape(batch, 2, length, D)
    layer_out = (v.pop.middle + chip_sum(p, partial)).astype(LOW)
    v.out_done = layer_out
    v.dot = dots("nd,btd->bnt", v.pop.wo, v.d_a).astype(LOW)
    v = sync(v)
    layer_out = v.pop.out_done

    def backward(b, qb, old_dc, old_dw):
        att = (v.att0, v.att1)[b][1:]
        return attention_backward(
            b, qb, v.meta, v.qt, v.dot, *att, v.kxt, v.vxt, v.keys, old_dc, old_dw
        )

    v.gd = z_scatter(p, v.gd)
    v.back00 = backward(0, 0, (), ())
    go = dots("bnt,btd->nd", v.pop.out, v.pop.d_a).astype(LOW).reshape(2, 2, 128, D)
    v.go_a, v.go_b = half(go, core, 3), half(go, 1 - core, 3)
    v = sync(v)
    v.gd1, v.go_b = p.to_y(v.gd), p.to_core(v.go_b)
    v.back01 = backward(0, 1, v.back00[1:2], v.back00[2:])
    v = sync(v)
    d_keys = v.back01[1]
    v.dk0, v.dk_far0 = d_keys[:2], p.down_y(d_keys[2:].astype(LOW))
    v.gd = ordered(y, v.gd, v.pop.gd1, 1)
    v.gd1 = p.to_core(v.gd)
    plan = []
    for n, (r, k) in enumerate(RELATIVE):
        for s in range(2):
            plan += [
                lambda x, y, c, n=n, r=r, k=k, s=s: (
                    s, (slice(None), x ^ r, slice(None), lanes((y ^ k) * 256, 256)),
                    n, pl.ds(2 * (c ^ s), 2),
                )
            ]
    v.go = spread(p, placed(p, plan, (v.pop.go_a, v.pop.go_b), [(4, 128, 256)] * 4))
    v.back10 = backward(1, 0, (), v.back01[2:])
    v = sync(v)
    v.go = z_scatter(p, add_all(v.pop.go))
    v.dk0 = (v.dk0 + v.pop.dk_far0.astype(F32)).astype(LOW).reshape(1, 2 * length, LAT)
    grad_down = ordered(core, v.pop.gd, v.pop.gd1, 1).astype(F32)
    v.back11 = backward(1, 1, v.back10[1:2], v.back10[2:])
    v.down_done = grad_down
    v = sync(v)
    grad_down = v.pop.down_done

    back = [[v.pop.back00, v.pop.back01], [v.pop.back10, v.pop.back11]]
    d_keys = back[1][1][1]
    v.far1 = p.down_y(d_keys[2:].astype(LOW))
    v.dk1 = d_keys[:2]
    plan = []
    for n in range(2):
        for s in range(2):
            plan += [
                lambda x, y, c, n=n, s=s: (n, (slice(None), lanes((c ^ s) * 128, 128)), s, n)
            ]
    v.kv_mine, kv_send = placed(p, plan, back[1][1][2:], [(2, GW, 128)] * 2)
    v.kv_come = p.to_core(kv_send)
    dq_t = jnp.stack([jnp.concatenate([part[0] for part in row], 1) for row in back])
    v.gq = dots("btd,bnt->dn", v.first, dq_t).astype(LOW)
    v.d_first = dots("bnt,dn->btd", dq_t, v.wq)
    v = sync(v)
    dk1 = (v.pop.dk1 + v.pop.far1.astype(F32)).astype(LOW).reshape(1, 2 * length, LAT)
    d_latent = jnp.concatenate([v.pop.dk0, dk1])
    gl = dots("btd,btl->dl", v.pop.first, d_latent).astype(LOW).reshape(4, 2, 128, LAT)
    plan = []
    for n, (r, k) in enumerate(RELATIVE):
        full = slice(None)
        plan += [
            lambda x, y, c, n=n, r=r, k=k: (
                0, (full, x ^ r, full, lanes((y ^ k) * 256, 256)), n, (full, full, pl.ds(0, 256)),
            ),
            lambda x, y, c, n=n, r=r, k=k: (
                1, (full, x ^ r, full, lanes((y ^ k) * 128, 128)), n, (full, full, pl.ds(384, 128)),
            ),
        ]
        for s in range(2):
            plan += [
                lambda x, y, c, n=n, r=r, k=k, s=s: (
                    2 + s, (y ^ k, full, x ^ r), n, (pl.ds(2 * (c ^ s), 2), full, pl.ds(256, 128)),
                )
            ]
    kv = [part.reshape(2, 2, 2, 128, 128) for part in (v.pop.kv_mine, v.pop.kv_come)]
    parts = placed(p, plan, (v.pop.gq.reshape(4, 2, 128, GW), gl, *kv), [(4, 128, 512)] * 4)
    v.found = spread(p, parts)
    d_first = v.pop.d_first + dots("btl,dl->btd", d_latent, v.wl)
    d_first = chip_sum(p, d_first.reshape(batch, 2, length, D))
    own = tokens.astype(F32)
    inverse1 = inverse_rms(own)
    normed1 = own * inverse1
    gains = jnp.stack([jnp.sum(d_first * normed1, axis=(0, 1)), v.pop.gain2_sum])
    gains = gains.astype(LOW).reshape(16, 128)
    v.gains = spread(p, [gains] * 4)
    v.tokens_done = v.d_middle + norm_back(d_first, normed1, inverse1, v.gain1)
    v.gg = gg
    v = sync(v)
    grad_tokens = v.pop.tokens_done
    gains = sum(part.astype(F32) for part in v.pop.gains).reshape(2, 4, 2, 128)
    gains = x_own(jnp.moveaxis(gains, 0, 2).reshape(4, 2, 2, 128))[:, 0].astype(LOW)
    gains = jnp.pad(gains, ((0, 0), (0, 6), (0, 384)))
    v.q = z_scatter(p, jnp.concatenate([add_all(v.pop.found), gains], 1))
    v.gg = add_low(v.gg, p.to_y(v.gg))
    v.go1 = p.to_y(v.go)
    v = sync(v)
    v.q1 = p.to_y(v.q)
    v.gg1 = p.to_core(v.gg)
    v.go = ordered(y, v.go, v.pop.go1, 1)
    v.go1 = p.to_core(v.go)
    v = sync(v)
    q0, q1 = pick(y, v.q, v.q1), pick(y, v.pop.q1, v.pop.q)
    mine = jnp.concatenate([q0, q1], 1)
    other = p.to_core(mine)
    grad_gate = ordered(core, v.gg[:, :ff], v.gg1[:, :ff], 1).astype(F32)
    grad_up = ordered(core, v.gg[:, ff:], v.gg1[:, ff:], 1).astype(F32)
    grad_output = ordered(core, v.go, v.go1, 1).astype(F32)
    zero, one = pick(core, mine, other), pick(core, other, mine)

    def columns(start, width):
        found = [part[:128, i : i + width] for part in (zero, one) for i in (start, start + 512)]
        return jnp.concatenate(found, 1).astype(F32)

    def expand_grad(start):
        return jnp.concatenate([p_[:128, start : start + 128] for p_ in (zero, one)], 1)

    gains = mine[128:130, :128].astype(F32) + other[128:130, :128].astype(F32)
    return (
        layer_out, grad_tokens, gains[0], columns(0, 256), columns(384, 128),
        expand_grad(256).T.astype(F32), expand_grad(768).T.astype(F32), grad_output, gains[1],
        grad_gate, grad_up, grad_down,
    )


def per_device(*arguments):
    p = Place()
    return (square_layer if p.square else plain_layer)(p, *arguments)


def solution(mesh):
    rows, gain, weight, across = P("dp", "seq", None), P("dp"), P("dp", None), P(None, "dp")
    return jax.shard_map(
        per_device,
        mesh=mesh,
        in_specs=(
            rows, gain, weight, weight, across, across, weight, gain, weight, weight, weight, rows,
            P("dp", None),
        ),
        out_specs=(
            rows, rows, gain, weight, weight, across, across, weight, gain, weight, weight, weight,
        ),
        check_vma=False,
    )
```

```python
import jax
import jax.numpy as jnp
from jax import lax
from jax.experimental import pallas as pl
from jax.experimental.pallas import tpu as pltpu
from jax.sharding import PartitionSpec as P

D = 1024
H = 16
HD = 64
KVH = 2
LAT = 256
GH = H // KVH
GW = D // KVH
EPS = 1e-06
SCALE = HD ** (-0.5)
LOG2E = 1.4426950408889634
NEG = -1e30

LOW = jnp.bfloat16
F32 = jnp.float32
ALL = ("seq", "dp")
VMEM_LIMIT = 56 * 1024 * 1024


def mm(left, right):
    return jnp.dot(left, right, preferred_element_type=F32)


def tn(left, right):
    return lax.dot_general(left, right, (((0,), (0,)), ((), ())), preferred_element_type=F32)


def nt(left, right):
    return lax.dot_general(left, right, (((1,), (1,)), ((), ())), preferred_element_type=F32)


def block_bias(k0, q0, first, width):
    kpos = k0 + lax.broadcasted_iota(jnp.int32, (width, width), 0)
    qpos = q0 + lax.broadcasted_iota(jnp.int32, (width, width), 1)
    lowest = jnp.where(qpos >= first, first, 0)
    return jnp.where((kpos <= qpos) & (kpos >= lowest), 0.0, NEG)


def block_needed(k0, q0, first, width):
    before = jnp.logical_and(q0 >= first, k0 + (width - 1) < first)
    return jnp.logical_and(k0 <= q0, jnp.logical_not(before))


def forward_kernel(b, nkb, batch, width, meta, qt, kxt, vxt, c, o_low, o_full, mix_out, lse_out, q_s, acc, m_s, l_s, p_s):
    qb = pl.program_id(0)
    q0, first, diag = meta[nkb + qb], meta[nkb + 2 + b], meta[nkb + 2 + batch] + qb
    for h in range(GH):
        cols = slice(h * width, (h + 1) * width)
        rows = slice(h * HD, (h + 1) * HD)
        q_s[:, cols] = (tn(kxt[rows, :], qt[0, rows, :]) * (SCALE * LOG2E)).astype(LOW)
    m_s[...] = jnp.full_like(m_s, NEG)
    l_s[...] = jnp.zeros_like(l_s)
    acc[...] = jnp.zeros_like(acc)

    def step(j, carry):
        kb = lax.rem(diag + j, nkb)
        k0 = meta[kb]

        @pl.when(block_needed(k0, q0, first, width))
        def _():
            bias = block_bias(k0, q0, first, width)
            keys = c[0, kb]
            keys_t = keys.T
            alphas = []
            for h in range(GH):
                cols = slice(h * width, (h + 1) * width)
                s = mm(keys, q_s[:, cols]) + bias
                m_old = m_s[:, cols]
                m_new = jnp.maximum(m_old, jnp.max(s, axis=0, keepdims=True))
                p = jnp.exp2(s - m_new)
                alpha = jnp.exp2(m_old - m_new)
                m_s[:, cols] = m_new
                l_s[:, cols] = l_s[:, cols] * alpha + jnp.sum(p, axis=0, keepdims=True)
                p_s[:, cols] = p.astype(LOW)
                alphas.append(alpha)
            acc[...] = acc[...] * jnp.concatenate(alphas, 1) + mm(keys_t, p_s[...])

        return carry

    lax.fori_loop(0, nkb, step, 0)
    for h in range(GH):
        cols = slice(h * width, (h + 1) * width)
        rows = slice(h * HD, (h + 1) * HD)
        total = l_s[:, cols]
        mixed = (acc[:, cols] * (1.0 / total)).astype(LOW)
        mix_out[0, :, cols] = mixed
        out = mm(vxt[rows, :], mixed)
        o_full[0, rows, :] = out
        o_low[0, rows, :] = out.astype(LOW)
        lse_out[0, :, cols] = m_s[:, cols] + jnp.log(total) * LOG2E


def backward_kernel(
    b, nkb, batch, width, add_dw, meta, qt, dot_, o_full, mix, lse, kxt, vxt, c, *refs
):
    refs = list(refs)
    dk_old, dv_old = (refs.pop(0), refs.pop(0)) if add_dw else (None, None)
    dqt, dc, dkxt, dvxt, q_s, do_t, delta, dq, ds_s, p_s = refs
    qb = pl.program_id(0)
    q0, first, diag = meta[nkb + qb], meta[nkb + 2 + b], meta[nkb + 2 + batch] + qb

    @pl.when(qb == 0)
    def _():
        dc[...] = jnp.zeros_like(dc)
        dkxt[...] = dk_old[...] if add_dw else jnp.zeros_like(dkxt)
        dvxt[...] = dv_old[...] if add_dw else jnp.zeros_like(dvxt)


    for h in range(GH):
        cols = slice(h * width, (h + 1) * width)
        rows = slice(h * HD, (h + 1) * HD)
        qh, kh, doh, vh = qt[0, rows, :], kxt[rows, :], dot_[0, rows, :], vxt[rows, :]
        q_s[:, cols] = (tn(kh, qh) * (SCALE * LOG2E)).astype(LOW)
        do_t[:, cols] = tn(vh, doh).astype(LOW)
        delta[:, cols] = jnp.sum(doh.astype(F32) * o_full[0, rows, :], axis=0, keepdims=True)
    dq[...] = jnp.zeros_like(dq)

    def step(j, carry):
        kb = lax.rem(diag + j, nkb)
        k0 = meta[kb]

        @pl.when(block_needed(k0, q0, first, width))
        def _():
            bias = block_bias(k0, q0, first, width)
            keys = c[0, kb]
            keys_t = keys.T
            for h in range(GH):
                cols = slice(h * width, (h + 1) * width)
                s = mm(keys, q_s[:, cols]) + bias
                p = jnp.exp2(s - lse[0, :, cols])
                dp = mm(keys, do_t[:, cols])
                ds = (p * (dp - delta[:, cols])).astype(LOW)
                p_s[:, cols] = p.astype(LOW)
                ds_s[:, cols] = ds
            dq[...] += mm(keys_t, ds_s[...])
            dc[kb] += nt(ds_s[...], q_s[...]) * (1.0 / LOG2E) + nt(p_s[...], do_t[...])

        return carry

    lax.fori_loop(0, nkb, step, 0)
    for h in range(GH):
        cols = slice(h * width, (h + 1) * width)
        rows = slice(h * HD, (h + 1) * HD)
        dq_low = (dq[:, cols] * SCALE).astype(LOW)
        dqt[rows, :] = mm(kxt[rows, :], dq_low).astype(LOW)
        dkxt[rows, :] += nt(qt[0, rows, :], dq_low)
        dvxt[rows, :] += nt(dot_[0, rows, :], mix[0, :, cols])


def attention_forward(b, meta, qt, kxt, vxt, c):
    batch, nkb, width, _ = c.shape
    wide = GH * width
    pairs = 7 * GH * width * width * LAT
    expand = pl.BlockSpec((GW, LAT), lambda q: (0, 0))
    out_spec = pl.BlockSpec((1, GW, width), lambda q: (0, 0, q))
    return pl.pallas_call(
        lambda *refs: forward_kernel(b, nkb, batch, width, *refs),
        grid=(2,),
        in_specs=[
            pl.BlockSpec(memory_space=pltpu.SMEM),
            pl.BlockSpec((1, GW, width), lambda q: (b, 0, q)),
            expand,
            expand,
            pl.BlockSpec((1, nkb, width, LAT), lambda q: (b, 0, 0, 0)),
        ],
        out_specs=[
            out_spec,
            out_spec,
            pl.BlockSpec((1, LAT, wide), lambda q: (q, 0, 0)),
            pl.BlockSpec((1, 1, wide), lambda q: (q, 0, 0)),
        ],
        out_shape=[
            jax.ShapeDtypeStruct((1, GW, 2 * width), LOW),
            jax.ShapeDtypeStruct((1, GW, 2 * width), F32),
            jax.ShapeDtypeStruct((2, LAT, wide), LOW),
            jax.ShapeDtypeStruct((2, 1, wide), F32),
        ],
        scratch_shapes=[
            pltpu.VMEM((LAT, wide), LOW),
            pltpu.VMEM((LAT, wide), F32),
            pltpu.VMEM((1, wide), F32),
            pltpu.VMEM((1, wide), F32),
            pltpu.VMEM((width, wide), LOW),
        ],
        compiler_params=pltpu.CompilerParams(
            dimension_semantics=("arbitrary",), vmem_limit_bytes=VMEM_LIMIT
        ),
        cost_estimate=pl.CostEstimate(
            flops=4 * pairs, bytes_accessed=8 << 20, transcendentals=7 * GH * width * width
        ),
        name="attention_forward",
    )(meta, qt, kxt, vxt, c)


def attention_backward(b, meta, qt, dot_, o_full, mix, lse, kxt, vxt, c, old_dw):
    batch, nkb, width, _ = c.shape
    wide = GH * width
    pairs = 7 * GH * width * width * LAT * 2
    expand = pl.BlockSpec((GW, LAT), lambda q: (0, 0))
    return pl.pallas_call(
        lambda *refs: backward_kernel(b, nkb, batch, width, bool(old_dw), *refs),
        grid=(2,),
        in_specs=[
            pl.BlockSpec(memory_space=pltpu.SMEM),
            pl.BlockSpec((1, GW, width), lambda q: (b, 0, q)),
            pl.BlockSpec((1, GW, width), lambda q: (b, 0, q)),
            pl.BlockSpec((1, GW, width), lambda q: (0, 0, q)),
            pl.BlockSpec((1, LAT, wide), lambda q: (q, 0, 0)),
            pl.BlockSpec((1, 1, wide), lambda q: (q, 0, 0)),
            expand,
            expand,
            pl.BlockSpec((1, nkb, width, LAT), lambda q: (b, 0, 0, 0)),
        ]
        + [expand] * len(old_dw),
        out_specs=[
            pl.BlockSpec((GW, width), lambda q: (0, q)),
            pl.BlockSpec((nkb, width, LAT), lambda q: (0, 0, 0)),
            expand,
            expand,
        ],
        out_shape=[
            jax.ShapeDtypeStruct((GW, 2 * width), LOW),
            jax.ShapeDtypeStruct((nkb, width, LAT), F32),
            jax.ShapeDtypeStruct(kxt.shape, F32),
            jax.ShapeDtypeStruct(vxt.shape, F32),
        ],
        scratch_shapes=[
            pltpu.VMEM((LAT, wide), LOW),
            pltpu.VMEM((LAT, wide), LOW),
            pltpu.VMEM((1, wide), F32),
            pltpu.VMEM((LAT, wide), F32),
            pltpu.VMEM((width, wide), LOW),
            pltpu.VMEM((width, wide), LOW),
        ],
        compiler_params=pltpu.CompilerParams(
            dimension_semantics=("arbitrary",), vmem_limit_bytes=VMEM_LIMIT
        ),
        cost_estimate=pl.CostEstimate(
            flops=5 * pairs, bytes_accessed=10 << 20, transcendentals=7 * GH * width * width
        ),
        name="attention_backward",
    )(meta, qt, dot_, o_full, mix, lse, kxt, vxt, c, *old_dw)


def hidden_kernel(x, w, act, hidden):
    width = hidden.shape[1]
    both = mm(x[...], w[...])
    act[...] = both
    gate, up = both[:, :width], both[:, width:]
    hidden[...] = (gate * jax.nn.sigmoid(gate) * up).astype(LOW)


def hidden_back_kernel(cot, down, w, act, grad, own, other):
    width = down.shape[0]
    d_hidden = nt(cot[...], down[...])
    gate, up = act[:, :width], act[:, width:]
    sig = jax.nn.sigmoid(gate)
    grad[:, :width] = (d_hidden * up * sig * (1.0 + gate * (1.0 - sig))).astype(LOW)
    grad[:, width:] = (d_hidden * (gate * sig)).astype(LOW)
    back = nt(grad[...], w[...])
    mine = pl.program_id(0) < pl.num_programs(0) // 2

    @pl.when(mine)
    def _():
        own[...] = back

    @pl.when(jnp.logical_not(mine))
    def _():
        other[...] = back.astype(LOW)


TILE = 256


def tiled(width):
    return pl.BlockSpec((TILE, width), lambda i: (i, 0))


def resident(shape):
    return pl.BlockSpec(shape, lambda i: (0, 0), pipeline_mode=pl.Buffered(1))


def feed_forward(x, w):
    count, both = x.shape[0], w.shape[1]
    return pl.pallas_call(
        hidden_kernel,
        grid=(count // TILE,),
        in_specs=[tiled(x.shape[1]), resident(w.shape)],
        out_specs=[tiled(both), tiled(both // 2)],
        out_shape=[
            jax.ShapeDtypeStruct((count, both), F32),
            jax.ShapeDtypeStruct((count, both // 2), LOW),
        ],
        compiler_params=pltpu.CompilerParams(vmem_limit_bytes=VMEM_LIMIT),
        cost_estimate=pl.CostEstimate(
            flops=2 * x.size * both, bytes_accessed=20 << 20, transcendentals=count * both // 2
        ),
        name="feed_forward",
    )(x, w)


def feed_forward_back(cot, down, w, act):
    count, both = act.shape
    width, steps = w.shape[0], count // TILE
    return pl.pallas_call(
        hidden_back_kernel,
        grid=(steps,),
        in_specs=[tiled(cot.shape[1]), resident(down.shape), resident(w.shape), tiled(both)],
        out_specs=[
            tiled(both),
            pl.BlockSpec((TILE, width), lambda i: (jnp.minimum(i, steps // 2 - 1), 0)),
            pl.BlockSpec((TILE, width), lambda i: (jnp.maximum(i - steps // 2, 0), 0)),
        ],
        out_shape=[
            jax.ShapeDtypeStruct((count, both), LOW),
            jax.ShapeDtypeStruct((count // 2, width), F32),
            jax.ShapeDtypeStruct((count // 2, width), LOW),
        ],
        compiler_params=pltpu.CompilerParams(vmem_limit_bytes=VMEM_LIMIT),
        cost_estimate=pl.CostEstimate(
            flops=3 * cot.size * both, bytes_accessed=30 << 20, transcendentals=count * both // 2
        ),
        name="feed_forward_back",
    )(cot, down, w, act)


class Place:
    def __init__(self):
        self.seq, self.dp = lax.axis_size("seq"), lax.axis_size("dp")
        s, d = lax.axis_index("seq"), lax.axis_index("dp")
        self.core, self.chip = s % 2, s // 2
        self.y, self.x, self.z = s // 2, d % 2, d // 2
        self.square = self.seq == 4 and self.dp == 8

    def pairs(self, move):
        found = []
        for s in range(self.seq):
            for d in range(self.dp):
                target = move(s, d)
                if target is not None:
                    found.append((s * self.dp + d, target[0] * self.dp + target[1]))
        return found

    def send(self, value, move):
        return lax.ppermute(value, ALL, self.pairs(move))

    def to_core(self, value):
        return self.send(value, lambda s, d: (s ^ 1, d))

    def to_y(self, value):
        return self.send(value, lambda s, d: (s ^ 2, d))

    def to_x(self, value):
        return self.send(value, lambda s, d: (s, d ^ 1))

    def to_z(self, value, step):
        return self.send(value, lambda s, d: (s, (d + 2 * step) % 8))

    def up_y(self, value):
        return self.send(value, lambda s, d: (s + 2, d) if s < 2 else None)

    def down_y(self, value):
        return self.send(value, lambda s, d: (s - 2, d) if s >= 2 else None)


def half(value, index, axis, count=2):
    size = value.shape[axis] // count
    return lax.dynamic_slice_in_dim(value, index * size, size, axis)


def ordered(flag, own, other, axis):
    return jnp.where(
        flag == 0, jnp.concatenate([own, other], axis), jnp.concatenate([other, own], axis)
    )


def after(value, *others):
    return lax.optimization_barrier((value, others))[0]


def add_low(own, other):
    return (own.astype(F32) + other.astype(F32)).astype(LOW)


class Plain:
    def __init__(self, place):
        self.p = place
        count = place.seq // 2
        self.same_core = [[2 * i + c for i in range(count)] for c in range(2)]
        self.chip = [[2 * i, 2 * i + 1] for i in range(count)]

    def gather(self, w):
        core = self.p.core

        def full(value, axis=0):
            return lax.all_gather(value.astype(LOW), "dp", axis=axis, tiled=True)

        out = {name: full(half(w[name], core, 1)) for name in ("query", "latent", "gate", "up")}
        out["key_t"] = half(full(w["key"].T), core, 0)
        out["value_t"] = half(full(w["value"].T), core, 0)
        out["output"] = half(full(w["output"]), core, 0)
        out["down"] = half(full(w["down"]), core, 0)
        out["gain1"], out["gain2"] = full(w["gain1"]), full(w["gain2"])
        return out

    def columns(self, grad):
        share = lax.psum_scatter(grad.astype(LOW), "dp", scatter_dimension=0, tiled=True)
        share = lax.psum(share, "seq", axis_index_groups=self.same_core)
        return lax.all_gather(
            share, "seq", axis=1, tiled=True, axis_index_groups=self.chip
        ).astype(F32)

    def rows(self, grad):
        grad = grad.astype(LOW)
        grad = ordered(self.p.core, grad, jnp.zeros_like(grad), 0)
        share = lax.psum_scatter(grad, "dp", scatter_dimension=0, tiled=True)
        return lax.psum(share, "seq").astype(F32)

    def gain(self, grad):
        share = lax.psum_scatter(grad.astype(LOW), "dp", scatter_dimension=0, tiled=True)
        return lax.psum(share, "seq").astype(F32)


def inverse_rms(values):
    return lax.rsqrt(jnp.mean(values * values, axis=-1, keepdims=True) + EPS)


def norm_back(grad, normed, inverse, gain):
    scaled = grad * gain
    return inverse * (scaled - normed * jnp.mean(scaled * normed, axis=-1, keepdims=True))


def dots(spec, left, right):
    return jnp.einsum(spec, left, right, preferred_element_type=F32)


def pick(flag, zero, one):
    return jnp.where(flag == 0, zero, one)


def chip(p, own):
    return jnp.stack([own, p.to_core(own)], axis=1)


def chip_sum(p, partial):
    return partial[:, 0] + p.to_core(partial[:, 1].astype(LOW)).astype(F32)


def plain_layer(
    p, tokens, attn_gain, query_weight, latent_weight, key_expand, value_expand, output_weight,
    mlp_gain, gate_weight, up_weight, down_weight, cotangent, lengths,
):
    ways = Plain(p)
    batch, length, _ = tokens.shape
    count = 2 * batch * length
    w = ways.gather(
        {
            "gain1": attn_gain, "query": query_weight, "latent": latent_weight,
            "key": key_expand, "value": value_expand, "output": output_weight,
            "gain2": mlp_gain, "gate": gate_weight, "up": up_weight, "down": down_weight,
        }
    )
    gain1, gain2 = w["gain1"].astype(F32), w["gain2"].astype(F32)
    firsts = lengths[:, 0]
    chips = p.seq // 2
    rows = chip(p, tokens).astype(F32)
    first_low = (rows * inverse_rms(rows) * gain1).astype(LOW)
    first_flat = first_low.reshape(batch, 2 * length, D)
    latent = dots("btd,dl->btl", first_flat, w["latent"]).astype(LOW)
    query_t = dots("dn,btd->bnt", w["query"], first_flat).astype(LOW)
    blocks = latent.reshape(batch, 2, length, LAT)
    starts = jnp.stack([p.core, 1 - p.core]).astype(jnp.int32) * length
    base = p.chip * 2 * length
    keys = lax.all_gather(blocks, "seq", axis=1, tiled=True, axis_index_groups=ways.same_core)
    key_starts = (
        2 * length * jnp.arange(chips, dtype=jnp.int32)[:, None] + starts[None, :]
    ).reshape(-1)
    diag = (2 * p.chip).astype(jnp.int32).reshape(1)
    meta = jnp.concatenate([key_starts, base + starts, firsts, diag]).astype(jnp.int32)
    att = [
        attention_forward(b, meta, query_t, w["key_t"], w["value_t"], keys)
        for b in range(batch)
    ]
    out_low = jnp.concatenate([a[0] for a in att])
    branch = dots("bnt,nd->btd", out_low, w["output"])
    middle = tokens.astype(F32) + chip_sum(p, branch.reshape(batch, 2, length, D))
    inverse2 = inverse_rms(middle)
    normed2 = middle * inverse2
    second = chip(p, (normed2 * gain2).astype(LOW)).reshape(count, D)
    cot = chip(p, cotangent).reshape(count, D)
    gate = mm(second, w["gate"])
    up = mm(second, w["up"])
    sig = jax.nn.sigmoid(gate)
    act = gate * sig
    hidden = (act * up).astype(LOW)
    partial = mm(hidden, w["down"]).reshape(batch, 2, length, D)
    layer_out = (middle + chip_sum(p, partial)).astype(LOW)
    grad_down = ways.rows(tn(hidden, cot))
    d_hidden = nt(cot, w["down"])
    d_gate = (d_hidden * up * sig * (1.0 + gate * (1.0 - sig))).astype(LOW)
    d_up = (d_hidden * act).astype(LOW)
    grad_gate, grad_up = ways.columns(tn(second, d_gate)), ways.columns(tn(second, d_up))
    partial = (nt(d_gate, w["gate"]) + nt(d_up, w["up"])).reshape(batch, 2, length, D)
    d_second = chip_sum(p, partial)
    gain2_sum = jnp.sum(d_second * normed2, axis=(0, 1))
    d_middle = cotangent.astype(F32) + norm_back(d_second, normed2, inverse2, gain2)
    d_a = chip(p, d_middle.astype(LOW)).reshape(batch, 2 * length, D)
    grad_output = ways.rows(dots("bnt,btd->nd", out_low, d_a))
    d_out_t = dots("nd,btd->bnt", w["output"], d_a).astype(LOW)
    d_queries, d_keys, sums = [], [], ()
    for b in range(batch):
        found = attention_backward(
            b, meta, query_t, d_out_t, *att[b][1:], w["key_t"], w["value_t"], keys, sums
        )
        sums = found[2:]
        d_queries.append(found[0])
        d_keys.append(found[1])
    dq_t, d_keys = jnp.stack(d_queries), jnp.stack(d_keys)
    d_key_t, d_value_t = sums
    d_blocks = lax.psum_scatter(
        d_keys.astype(LOW), "seq", scatter_dimension=1, tiled=True,
        axis_index_groups=ways.same_core,
    )
    d_latent = d_blocks.astype(LOW).reshape(batch, 2 * length, LAT)
    grad_query = ways.columns(dots("btd,bnt->dn", first_flat, dq_t))
    grad_latent = ways.columns(dots("btd,btl->dl", first_flat, d_latent))
    d_first = dots("bnt,dn->btd", dq_t, w["query"]) + dots("btl,dl->btd", d_latent, w["latent"])
    d_first = chip_sum(p, d_first.reshape(batch, 2, length, D))
    own = tokens.astype(F32)
    inverse1 = inverse_rms(own)
    normed1 = own * inverse1
    gain1_sum = jnp.sum(d_first * normed1, axis=(0, 1))
    grad_tokens = d_middle + norm_back(d_first, normed1, inverse1, gain1)
    return (
        layer_out, grad_tokens, ways.gain(gain1_sum), grad_query, grad_latent,
        ways.rows(d_key_t).T, ways.rows(d_value_t).T, grad_output, ways.gain(gain2_sum),
        grad_gate, grad_up, grad_down,
    )


class Live:
    def __init__(self, values):
        self.__dict__.update(values)

    @property
    def pop(self):
        return Taken(self)


class Taken:
    def __init__(self, live):
        self.live = live

    def __getattr__(self, name):
        return self.live.__dict__.pop(name)


def sync(v):
    return Live(lax.optimization_barrier(dict(v.__dict__)))


def in_z(p, seen):
    out = []
    for z in range(4):
        back = (p.z - z) % 4
        pair = [jnp.where(back % 2 == 0, seen[k], seen[k + 1]) for k in (0, 2)]
        out.append(jnp.where(back < 2, pair[0], pair[1]))
    return jnp.stack(out)


def z_gather(p, piece):
    return in_z(p, [piece] + [p.to_z(piece, k) for k in (1, 2, 3)])


def z_scatter(p, parts):
    total = half(parts, p.z, 0, 4)[0].astype(F32)
    for k in (1, 2, 3):
        total = total + p.to_z(half(parts, (p.z + k) % 4, 0, 4), k)[0].astype(F32)
    return total.astype(LOW)


def summed(p, make):
    come = p.to_core(make(1).astype(LOW))
    return make(0) + come.astype(F32)


def core_first(p, own):
    return jnp.concatenate([own, p.to_core(own)], 0)


def to_xy(p, value):
    return p.send(value, lambda s, d: (s ^ 2, d ^ 1))


def add_all(parts):
    return sum(part.astype(F32) for part in parts).astype(LOW)


def place_kernel(plan, sources, outs, where, *refs):
    src, dst = refs[:sources], refs[sources:]
    spot = where[0], where[1], where[2]
    for make in plan:
        source, there, out, here = make(*spot)
        dst[out][here] = src[source][there].astype(LOW)


def placed(p, plan, sources, shapes):
    where = jnp.stack([p.x, p.y, p.core]).astype(jnp.int32)
    inside = pl.BlockSpec(memory_space=pltpu.VMEM)
    return pl.pallas_call(
        lambda *refs: place_kernel(plan, len(sources), len(shapes), *refs),
        in_specs=[pl.BlockSpec(memory_space=pltpu.SMEM)] + [inside] * len(sources),
        out_specs=[inside] * len(shapes),
        out_shape=[jax.ShapeDtypeStruct(shape, LOW) for shape in shapes],
        compiler_params=pltpu.CompilerParams(vmem_limit_bytes=VMEM_LIMIT),
        name="place",
    )(where, *sources)


def lanes(start, width):
    return pl.ds(pl.multiple_of(start, 128), width)


RELATIVE = [(0, 0), (1, 0), (0, 1), (1, 1)]


def spread(p, parts):
    return parts[0], p.to_x(parts[1]), p.to_y(parts[2]), to_xy(p, parts[3])


def square_layer(
    p, tokens, attn_gain, query_weight, latent_weight, key_expand, value_expand, output_weight,
    mlp_gain, gate_weight, up_weight, down_weight, cotangent, lengths,
):
    batch, length, _ = tokens.shape
    count = 2 * batch * length
    core, x, y = p.core, p.x, p.y
    ff = gate_weight.shape[1] // 2
    quarter = 2 * core + y
    v = Live({})

    def cols(value, parts, index):
        return half(value, index, 1, parts).astype(LOW)

    def x_own(value):
        return half(value, x, 1)

    def x_other(value):
        return half(value, 1 - x, 1)

    v.pgu = jnp.concatenate([cols(gate_weight, 2, core), cols(up_weight, 2, core)], 1)
    v.tok = p.to_core(tokens)
    v = sync(v)
    w_gu = lax.all_gather(v.pop.pgu, "dp", axis=0, tiled=True)
    kv = half(pick(y, key_expand, value_expand), core, 0).astype(LOW).T
    gains = jnp.stack([attn_gain, mlp_gain] + [jnp.zeros_like(attn_gain)] * 6).astype(LOW)
    piece = [
        cols(latent_weight, 4, quarter), cols(output_weight, 4, quarter),
        cols(query_weight, 4, quarter), kv,
    ]
    piece = jnp.concatenate(piece, 1)
    pad = jnp.zeros((8, piece.shape[1] - 128), LOW)
    piece = jnp.concatenate([piece, jnp.concatenate([gains, pad], 1)], 0)
    first = z_gather(p, piece)
    v.a, v.b = first[:, :, :384], first[:, :, 384:]
    rows = jnp.stack([tokens, v.pop.tok], 1).astype(F32)
    v.normed1 = rows * inverse_rms(rows)
    v.pd = cols(down_weight, 4, quarter)
    v = sync(v)

    v.ax, v.by = p.to_x(v.a), p.to_y(v.b)
    v.zd1 = p.to_z(v.pd, 1)
    v = sync(v)
    v.zd2 = p.to_z(v.pd, 2)
    v.ay, v.axy = p.to_y(v.a), p.to_y(v.ax)
    v.bx, v.bxy = p.to_x(v.b), p.to_x(v.by)
    v = sync(v)

    v.from_ab = (v.pop.a, v.pop.ax, v.pop.ay, v.pop.axy, v.pop.b, v.pop.bx, v.pop.by, v.pop.bxy)
    plan = []
    for n, (r, k) in enumerate(RELATIVE):
        low = pl.ds(0, 128)
        plan += [
            lambda x, y, c, n=n, r=r, k=k: (
                n, (slice(None), low, pl.ds(0, 128)), 0,
                (slice(None), x ^ r, slice(None), lanes((y ^ k) * 128, 128)),
            ),
            lambda x, y, c, n=n, r=r, k=k: (
                4 + n, (slice(None), low, pl.ds(0, 256)), 1,
                (slice(None), x ^ r, slice(None), lanes((y ^ k) * 256, 256)),
            ),
            lambda x, y, c, n=n: (n, (pl.ds(2 * (1 - c), 2), low, pl.ds(128, 256)), 2, n),
            lambda x, y, c, n=n: (4 + n, (pl.ds(2 * (1 - c), 2), low, pl.ds(256, 128)), 3, n),
        ]
    wl, wq, v.wo_send, v.kv_send = placed(
        p, plan, v.from_ab,
        [(4, 2, 128, LAT), (4, 2, 128, GW), (4, 2, 128, 256), (4, 2, 128, 128)],
    )
    v.wl, v.wq = wl.reshape(D, LAT), wq.reshape(D, GW)
    gains = [part[:, 128:130, :128] for part in v.from_ab[:2]]
    gains = pick(x, jnp.stack(gains, 2), jnp.stack(gains[::-1], 2)).astype(F32)
    v.gain1, v.gain2 = gains[:, 0].reshape(D), gains[:, 1].reshape(D)
    v.first = (v.pop.normed1 * v.gain1).astype(LOW).reshape(batch, 2 * length, D)
    v.keys = dots("btd,dl->btl", v.first, v.wl).astype(LOW).reshape(batch, 2, length, LAT)
    v = sync(v)
    far_keys = p.up_y(v.keys)
    wo_come, kv_come = p.to_core(v.pop.wo_send), p.to_core(v.pop.kv_send)
    v.zd3 = p.to_z(v.pd, 3)
    v.qt = dots("dn,btd->bnt", v.wq, v.first).astype(LOW)
    plan = []
    for n, (r, k) in enumerate(RELATIVE):
        for s in range(2):
            plan += [
                lambda x, y, c, n=n, r=r, k=k, s=s: (
                    (n, (pl.ds(2 * c, 2), pl.ds(0, 128), pl.ds(128, 256))) if s == 0 else (8, n)
                ) + (0, (slice(None), x ^ r, slice(None), lanes(((c ^ s) * 2 + (y ^ k)) * 256, 256))),
                lambda x, y, c, n=n, r=r, k=k, s=s: (
                    (4 + n, (pl.ds(2 * c, 2), pl.ds(0, 128), pl.ds(256, 128))) if s == 0 else (9, n)
                ) + (1, (y ^ k, slice(None), x ^ r, slice(None), lanes((c ^ s) * 128, 128))),
            ]
    wo, kv = placed(
        p, plan, (*v.pop.from_ab, wo_come, kv_come), [(2, 2, 128, D), (2, 2, 2, 128, LAT)]
    )
    v.wo, kv = wo.reshape(GW, D), kv.reshape(2, GW, LAT)
    v.kxt, v.vxt = kv[0], kv[1]
    starts = jnp.stack([core, 1 - core]).astype(jnp.int32) * length
    base = p.chip * 2 * length
    far = pick(p.chip, 2 * length, 0)
    meta = [base + starts, far + starts, base + starts, lengths[:, 0], jnp.zeros((1,), jnp.int32)]
    v.meta = jnp.concatenate(meta).astype(jnp.int32)
    v.keys = jnp.concatenate([v.keys, far_keys], axis=1)
    v = sync(v)

    def forward(b):
        return attention_forward(b, v.meta, v.qt, v.kxt, v.vxt, v.keys)

    v.zd = in_z(p, [v.pop.pd, v.pop.zd1, v.pop.zd2, v.pop.zd3])
    v.dax, v.dby = p.to_x(v.zd[:2]), p.to_y(v.zd[2:])
    v.cot = core_first(p, cotangent.reshape(count // 2, D))
    v.att0 = forward(0)
    v = sync(v)
    v.day, v.daxy = p.to_y(v.zd[:2]), p.to_y(v.dax)
    v.dbx, v.dbxy = p.to_x(v.zd[2:]), p.to_x(v.dby)
    cot = half(v.cot, core, 1)
    v.cot_c = [half(cot, i, 1) for i in (y, 1 - y)] + [half(v.cot, 1 - core, 1)]
    v.att1 = forward(1)
    v = sync(v)

    front, back = v.zd[:2], v.pop.zd[2:]
    fronts, backs = [front, v.pop.dax, v.pop.day, v.pop.daxy], [back, v.pop.dbx, v.pop.dby, v.pop.dbxy]
    mine = [pick(core, front, back) for front, back in zip(fronts, backs)]
    v.down = mine + [p.to_core(pick(core, back, front)) for front, back in zip(fronts, backs)]
    v.out = jnp.concatenate([v.att0[0], v.att1[0]])
    branch = summed(
        p, lambda i: dots("bnt,nd->btd", v.out[:, :, i * length : (i + 1) * length], v.wo)
    )
    v.middle = tokens.astype(F32) + branch
    v.inv2 = inverse_rms(v.middle)
    second = v.middle * v.inv2 * v.gain2
    v.second = core_first(p, second.astype(LOW).reshape(count // 2, D))
    v = sync(v)

    v.w_gu = w_gu
    v.act, v.hidden = feed_forward(v.second, v.w_gu)
    cot_y, cot_far, cot_core = v.pop.cot_c
    v.gd_b = p.to_core(tn(v.hidden, cot_core).astype(LOW).reshape(2, 2, -1, 512))
    v.gd_a = tn(v.hidden, cot_y).astype(LOW).reshape(2, 2, -1, 256)
    v.gd_ay = tn(v.hidden, cot_far).astype(LOW).reshape(2, 2, -1, 256)
    plan = []
    for n, (r, k) in enumerate(RELATIVE):
        for s in range(2):
            plan += [
                lambda x, y, c, n=n, r=r, k=k, s=s: (
                    4 * s + n, slice(None), 0,
                    (slice(None), x ^ r, slice(None), lanes(((c ^ s) * 2 + (y ^ k)) * 256, 256)),
                )
            ]
    wd = placed(p, plan, v.pop.down, [(2, 2, ff // 4, D)])[0]
    v.wd = wd.reshape(ff, D)
    v = sync(v)

    v.gd_ay, v.gd_bx = p.to_y(v.gd_ay), p.to_x(x_other(v.gd_b))
    v.d_gu, v.ds_own, v.ds_other = feed_forward_back(v.cot, v.wd, v.pop.w_gu, v.pop.act)
    v = sync(v)
    v.gd_a = add_low(v.gd_a, v.pop.gd_ay)
    v.gd_b = add_low(x_own(v.gd_b), v.pop.gd_bx)
    v.gd_ax, v.gd_by = p.to_x(x_other(v.gd_a)), p.to_y(half(v.gd_b, 1 - y, 3))
    d_second = (v.pop.ds_own + p.to_core(v.pop.ds_other).astype(F32)).reshape(batch, length, D)
    v.gg = tn(v.pop.second, v.pop.d_gu).astype(LOW)
    normed2 = v.middle * v.inv2
    v.gain2_sum = jnp.sum(d_second * normed2, axis=(0, 1))
    v.d_middle = cotangent.astype(F32) + norm_back(d_second, normed2, v.pop.inv2, v.pop.gain2)
    v.d_a = chip(p, v.d_middle.astype(LOW)).reshape(batch, 2 * length, D)
    v = sync(v)
    gg = lax.psum_scatter(v.pop.gg, "dp", scatter_dimension=0, tiled=True)
    gd_a = add_low(x_own(v.pop.gd_a), v.pop.gd_ax)[:, 0]
    gd_b = add_low(half(v.pop.gd_b, y, 3), v.pop.gd_by)[:, 0]
    v.gd = ordered(core, gd_a, gd_b, 0)

    def gd_step(k):
        return p.to_z(half(v.gd, (p.z + k) % 4, 0, 4), k)

    v.gd1 = gd_step(1)
    go = dots("bnt,btd->nd", v.pop.out, v.d_a).astype(LOW).reshape(2, 2, 128, D)
    v.go_a, v.go_b = half(go, core, 3), p.to_core(half(go, 1 - core, 3))
    rows = count // 2
    branch = summed(p, lambda i: mm(v.hidden[i * rows : (i + 1) * rows], v.wd))
    v.out_done = (v.pop.middle + branch.reshape(batch, length, D)).astype(LOW)
    del v.hidden, v.wd
    v.dot = dots("nd,btd->bnt", v.pop.wo, v.pop.d_a).astype(LOW)
    v = sync(v)
    layer_out = v.pop.out_done

    full = slice(None)
    v.gd2 = gd_step(2)
    plan = []
    for n, (r, k) in enumerate(RELATIVE):
        for s in range(2):
            plan += [
                lambda x, y, c, n=n, r=r, k=k, s=s: (
                    s, (full, x ^ r, full, lanes((y ^ k) * 256, 256)), n, pl.ds(2 * (c ^ s), 2),
                )
            ]
    v.go = spread(p, placed(p, plan, (v.pop.go_a, v.pop.go_b), [(4, 128, 256)] * 4))
    v.back0 = attention_backward(
        0, v.meta, v.qt, v.dot, *v.att0[1:], v.kxt, v.vxt, v.keys, ()
    )
    v = sync(v)
    v.gd3 = gd_step(3)
    v.go = z_scatter(p, add_all(v.go))
    d_keys = v.back0[1]
    v.dk0, v.dk_far0 = d_keys[:2], p.down_y(d_keys[2:].astype(LOW))
    v.back1 = attention_backward(
        1, v.meta, v.qt, v.dot, *v.att1[1:], v.kxt, v.vxt, v.keys, v.back0[2:]
    )
    v = sync(v)

    back0, back1 = v.pop.back0, v.pop.back1
    v.far1 = p.down_y(back1[1][2:].astype(LOW))
    v.dk1 = back1[1][:2]
    v.dk0 = (v.dk0 + v.pop.dk_far0.astype(F32)).astype(LOW).reshape(1, 2 * length, LAT)
    plan = []
    for n in range(2):
        for s in range(2):
            plan += [
                lambda x, y, c, n=n, s=s: (n, (slice(None), lanes((c ^ s) * 128, 128)), s, n)
            ]
    v.kv_mine, kv_send = placed(p, plan, back1[2:], [(2, GW, 128)] * 2)
    v.kv_come = p.to_core(kv_send)
    v.gd = add_all([half(v.gd, p.z, 0, 4), v.pop.gd1, v.pop.gd2, v.pop.gd3])[0]
    v.gd1, v.go1 = p.to_y(v.gd), p.to_y(v.go)
    v.dq_t = jnp.stack([back0[0], back1[0]])
    gq = dots("btd,bnt->dn", v.first, v.dq_t).astype(LOW).reshape(4, 2, 128, GW)
    plan = []
    for n, (r, k) in enumerate(RELATIVE):
        plan += [
            lambda x, y, c, n=n, r=r, k=k: (
                0, (full, x ^ r, full, lanes((y ^ k) * 256, 256)), n, (full, full, full),
            )
        ]
    v.parts_q = placed(p, plan, (gq,), [(4, 128, 256)] * 4)
    v = sync(v)
    v.found_q = spread(p, v.pop.parts_q)
    v.gd, v.go = ordered(y, v.gd, v.pop.gd1, 1), ordered(y, v.go, v.pop.go1, 1)
    v.gd1, v.go1 = p.to_core(v.gd), p.to_core(v.go)
    dk1 = (v.pop.dk1 + v.pop.far1.astype(F32)).astype(LOW).reshape(1, 2 * length, LAT)
    d_latent = jnp.concatenate([v.pop.dk0, dk1])
    gl = dots("btd,btl->dl", v.pop.first, d_latent).astype(LOW).reshape(4, 2, 128, LAT)
    plan = []
    for n, (r, k) in enumerate(RELATIVE):
        plan += [
            lambda x, y, c, n=n, r=r, k=k: (
                0, (full, x ^ r, full, lanes((y ^ k) * 128, 128)), n, (full, full, pl.ds(128, 128)),
            )
        ]
        for s in range(2):
            plan += [
                lambda x, y, c, n=n, r=r, k=k, s=s: (
                    1 + s, (y ^ k, full, x ^ r), n, (pl.ds(2 * (c ^ s), 2), full, pl.ds(0, 128)),
                )
            ]
    kv = [part.reshape(2, 2, 2, 128, 128) for part in (v.pop.kv_mine, v.pop.kv_come)]
    v.found = spread(p, placed(p, plan, (gl, *kv), [(4, 128, 256)] * 4))
    dq_t = v.pop.dq_t

    def first_grad(i):
        part = slice(i * length, (i + 1) * length)
        by_q = dots("bnt,dn->btd", dq_t[:, :, part], v.wq)
        return by_q + dots("btl,dl->btd", d_latent[:, part], v.wl)

    d_first = summed(p, first_grad)
    own = tokens.astype(F32)
    inverse1 = inverse_rms(own)
    normed1 = own * inverse1
    gains = jnp.stack([jnp.sum(d_first * normed1, axis=(0, 1)), v.pop.gain2_sum])
    gains = gains.astype(LOW).reshape(16, 128)
    v.gains = spread(p, [gains] * 4)
    v.tokens_done = v.d_middle + norm_back(d_first, normed1, inverse1, v.gain1)
    v.gg = gg
    v = sync(v)
    grad_tokens = v.pop.tokens_done
    grad_down = ordered(core, v.pop.gd, v.pop.gd1, 1).astype(F32)
    grad_output = ordered(core, v.pop.go, v.pop.go1, 1).astype(F32)
    gains = sum(part.astype(F32) for part in v.pop.gains).reshape(2, 4, 2, 128)
    gains = x_own(jnp.moveaxis(gains, 0, 2).reshape(4, 2, 2, 128))[:, 0].astype(LOW)
    gains = jnp.pad(gains, ((0, 0), (0, 6), (0, 384)))
    q = jnp.concatenate([add_all(v.pop.found_q), add_all(v.pop.found)], -1)
    v.q = z_scatter(p, jnp.concatenate([q, gains], 1))
    v.gg = add_low(v.gg, p.to_y(v.gg))
    v.done = grad_down, grad_output
    v = sync(v)
    grad_down, grad_output = v.pop.done
    v.q1 = p.to_y(v.q)
    v.gg1 = p.to_core(v.gg)
    v = sync(v)
    q0, q1 = pick(y, v.q, v.q1), pick(y, v.pop.q1, v.pop.q)
    mine = jnp.concatenate([q0, q1], 1)
    other = p.to_core(mine)
    grad_gate = ordered(core, v.gg[:, :ff], v.gg1[:, :ff], 1).astype(F32)
    grad_up = ordered(core, v.gg[:, ff:], v.gg1[:, ff:], 1).astype(F32)
    zero, one = pick(core, mine, other), pick(core, other, mine)

    def columns(start, width):
        found = [part[:128, i : i + width] for part in (zero, one) for i in (start, start + 512)]
        return jnp.concatenate(found, 1).astype(F32)

    def expand_grad(start):
        return jnp.concatenate([p_[:128, start : start + 128] for p_ in (zero, one)], 1)

    gains = mine[128:130, :128].astype(F32) + other[128:130, :128].astype(F32)
    return (
        layer_out, grad_tokens, gains[0], columns(0, 256), columns(384, 128),
        expand_grad(256).T.astype(F32), expand_grad(768).T.astype(F32), grad_output, gains[1],
        grad_gate, grad_up, grad_down,
    )


def per_device(*arguments):
    p = Place()
    return (square_layer if p.square else plain_layer)(p, *arguments)


def solution(mesh):
    rows, gain, weight, across = P("dp", "seq", None), P("dp"), P("dp", None), P(None, "dp")
    return jax.shard_map(
        per_device,
        mesh=mesh,
        in_specs=(
            rows, gain, weight, weight, across, across, weight, gain, weight, weight, weight, rows,
            P("dp", None),
        ),
        out_specs=(
            rows, rows, gain, weight, weight, across, across, weight, gain, weight, weight, weight,
        ),
        check_vma=False,
    )
```

```python
import jax
import jax.numpy as jnp
from jax import lax
from jax.experimental import pallas as pl
from jax.experimental.pallas import tpu as pltpu
from jax.sharding import PartitionSpec as P

D = 1024
H = 16
HD = 64
KVH = 2
LAT = 256
GH = H // KVH
GW = D // KVH
EPS = 1e-06
SCALE = HD ** (-0.5)
LOG2E = 1.4426950408889634
NEG = -1e30

LOW = jnp.bfloat16
F32 = jnp.float32
ALL = ("seq", "dp")
VMEM_LIMIT = 56 * 1024 * 1024


def mm(left, right):
    return jnp.dot(left, right, preferred_element_type=F32)


def tn(left, right):
    return lax.dot_general(left, right, (((0,), (0,)), ((), ())), preferred_element_type=F32)


def nt(left, right):
    return lax.dot_general(left, right, (((1,), (1,)), ((), ())), preferred_element_type=F32)


def block_bias(k0, q0, first, width):
    kpos = k0 + lax.broadcasted_iota(jnp.int32, (width, width), 0)
    qpos = q0 + lax.broadcasted_iota(jnp.int32, (width, width), 1)
    lowest = jnp.where(qpos >= first, first, 0)
    return jnp.where((kpos <= qpos) & (kpos >= lowest), 0.0, NEG)


def block_needed(k0, q0, first, width):
    before = jnp.logical_and(q0 >= first, k0 + (width - 1) < first)
    return jnp.logical_and(k0 <= q0, jnp.logical_not(before))


def forward_kernel(nkb, batch, width, meta, qt, kxt, vxt, c, o_low, o_full, mix_out, lse_out, q_s, acc, m_s, l_s, p_s):
    b, qb = pl.program_id(0), pl.program_id(1)
    q0, first, diag = meta[nkb + qb], meta[nkb + 2 + b], meta[nkb + 2 + batch] + qb
    for h in range(GH):
        cols = slice(h * width, (h + 1) * width)
        rows = slice(h * HD, (h + 1) * HD)
        q_s[:, cols] = (tn(kxt[rows, :], qt[0, rows, :]) * (SCALE * LOG2E)).astype(LOW)
    m_s[...] = jnp.full_like(m_s, NEG)
    l_s[...] = jnp.zeros_like(l_s)
    acc[...] = jnp.zeros_like(acc)

    def step(j, carry):
        kb = lax.rem(diag + j, nkb)
        k0 = meta[kb]

        @pl.when(block_needed(k0, q0, first, width))
        def _():
            bias = block_bias(k0, q0, first, width)
            keys = c[0, kb]
            keys_t = keys.T
            alphas = []
            for h in range(GH):
                cols = slice(h * width, (h + 1) * width)
                s = mm(keys, q_s[:, cols]) + bias
                m_old = m_s[:, cols]
                m_new = jnp.maximum(m_old, jnp.max(s, axis=0, keepdims=True))
                p = jnp.exp2(s - m_new)
                alpha = jnp.exp2(m_old - m_new)
                m_s[:, cols] = m_new
                l_s[:, cols] = l_s[:, cols] * alpha + jnp.sum(p, axis=0, keepdims=True)
                p_s[:, cols] = p.astype(LOW)
                alphas.append(alpha)
            acc[...] = acc[...] * jnp.concatenate(alphas, 1) + mm(keys_t, p_s[...])

        return carry

    lax.fori_loop(0, nkb, step, 0)
    for h in range(GH):
        cols = slice(h * width, (h + 1) * width)
        rows = slice(h * HD, (h + 1) * HD)
        total = l_s[:, cols]
        mixed = (acc[:, cols] * (1.0 / total)).astype(LOW)
        mix_out[0, 0, :, cols] = mixed
        out = mm(vxt[rows, :], mixed)
        o_full[0, rows, :] = out
        o_low[0, rows, :] = out.astype(LOW)
        lse_out[0, 0, :, cols] = m_s[:, cols] + jnp.log(total) * LOG2E


def backward_kernel(
    b, nkb, batch, width, add_dw, meta, qt, dot_, o_full, mix, lse, kxt, vxt, c, *refs
):
    refs = list(refs)
    dk_old, dv_old = (refs.pop(0), refs.pop(0)) if add_dw else (None, None)
    dqt, dc, dkxt, dvxt, q_s, do_t, delta, dq, ds_s, p_s = refs
    qb = pl.program_id(0)
    q0, first, diag = meta[nkb + qb], meta[nkb + 2 + b], meta[nkb + 2 + batch] + qb

    @pl.when(qb == 0)
    def _():
        dc[...] = jnp.zeros_like(dc)
        dkxt[...] = dk_old[...] if add_dw else jnp.zeros_like(dkxt)
        dvxt[...] = dv_old[...] if add_dw else jnp.zeros_like(dvxt)


    for h in range(GH):
        cols = slice(h * width, (h + 1) * width)
        rows = slice(h * HD, (h + 1) * HD)
        qh, kh, doh, vh = qt[0, rows, :], kxt[rows, :], dot_[0, rows, :], vxt[rows, :]
        q_s[:, cols] = (tn(kh, qh) * (SCALE * LOG2E)).astype(LOW)
        do_t[:, cols] = tn(vh, doh).astype(LOW)
        delta[:, cols] = jnp.sum(doh.astype(F32) * o_full[0, rows, :], axis=0, keepdims=True)
    dq[...] = jnp.zeros_like(dq)

    def step(j, carry):
        kb = lax.rem(diag + j, nkb)
        k0 = meta[kb]

        @pl.when(block_needed(k0, q0, first, width))
        def _():
            bias = block_bias(k0, q0, first, width)
            keys = c[0, kb]
            keys_t = keys.T
            for h in range(GH):
                cols = slice(h * width, (h + 1) * width)
                s = mm(keys, q_s[:, cols]) + bias
                p = jnp.exp2(s - lse[0, 0, :, cols])
                dp = mm(keys, do_t[:, cols])
                ds = (p * (dp - delta[:, cols])).astype(LOW)
                p_s[:, cols] = p.astype(LOW)
                ds_s[:, cols] = ds
            dq[...] += mm(keys_t, ds_s[...])
            dc[kb] += nt(ds_s[...], q_s[...]) * (1.0 / LOG2E) + nt(p_s[...], do_t[...])

        return carry

    lax.fori_loop(0, nkb, step, 0)
    for h in range(GH):
        cols = slice(h * width, (h + 1) * width)
        rows = slice(h * HD, (h + 1) * HD)
        dq_low = (dq[:, cols] * SCALE).astype(LOW)
        dqt[rows, :] = mm(kxt[rows, :], dq_low).astype(LOW)
        dkxt[rows, :] += nt(qt[0, rows, :], dq_low)
        dvxt[rows, :] += nt(dot_[0, rows, :], mix[0, 0, :, cols])


def attention_forward(meta, qt, kxt, vxt, c):
    batch, nkb, width, _ = c.shape
    wide = GH * width
    pairs = batch * 7 * GH * width * width * LAT
    expand = pl.BlockSpec((GW, LAT), lambda b, q: (0, 0))
    q_spec = pl.BlockSpec((1, GW, width), lambda b, q: (b, 0, q))
    return pl.pallas_call(
        lambda *refs: forward_kernel(nkb, batch, width, *refs),
        grid=(batch, 2),
        in_specs=[
            pl.BlockSpec(memory_space=pltpu.SMEM),
            q_spec,
            expand,
            expand,
            pl.BlockSpec((1, nkb, width, LAT), lambda b, q: (b, 0, 0, 0)),
        ],
        out_specs=[
            q_spec,
            q_spec,
            pl.BlockSpec((1, 1, LAT, wide), lambda b, q: (b, q, 0, 0)),
            pl.BlockSpec((1, 1, 1, wide), lambda b, q: (b, q, 0, 0)),
        ],
        out_shape=[
            jax.ShapeDtypeStruct(qt.shape, LOW),
            jax.ShapeDtypeStruct(qt.shape, F32),
            jax.ShapeDtypeStruct((batch, 2, LAT, wide), LOW),
            jax.ShapeDtypeStruct((batch, 2, 1, wide), F32),
        ],
        scratch_shapes=[
            pltpu.VMEM((LAT, wide), LOW),
            pltpu.VMEM((LAT, wide), F32),
            pltpu.VMEM((1, wide), F32),
            pltpu.VMEM((1, wide), F32),
            pltpu.VMEM((width, wide), LOW),
        ],
        compiler_params=pltpu.CompilerParams(
            dimension_semantics=("arbitrary", "arbitrary"), vmem_limit_bytes=VMEM_LIMIT
        ),
        cost_estimate=pl.CostEstimate(
            flops=4 * pairs, bytes_accessed=16 << 20, transcendentals=batch * 7 * GH * width * width
        ),
        name="attention_forward",
    )(meta, qt, kxt, vxt, c)


def attention_backward(b, meta, qt, dot_, o_full, mix, lse, kxt, vxt, c, old_dw):
    batch, nkb, width, _ = c.shape
    wide = GH * width
    pairs = 7 * GH * width * width * LAT * 2
    expand = pl.BlockSpec((GW, LAT), lambda q: (0, 0))
    return pl.pallas_call(
        lambda *refs: backward_kernel(b, nkb, batch, width, bool(old_dw), *refs),
        grid=(2,),
        in_specs=[
            pl.BlockSpec(memory_space=pltpu.SMEM),
            pl.BlockSpec((1, GW, width), lambda q: (b, 0, q)),
            pl.BlockSpec((1, GW, width), lambda q: (b, 0, q)),
            pl.BlockSpec((1, GW, width), lambda q: (b, 0, q)),
            pl.BlockSpec((1, 1, LAT, wide), lambda q: (b, q, 0, 0)),
            pl.BlockSpec((1, 1, 1, wide), lambda q: (b, q, 0, 0)),
            expand,
            expand,
            pl.BlockSpec((1, nkb, width, LAT), lambda q: (b, 0, 0, 0)),
        ]
        + [expand] * len(old_dw),
        out_specs=[
            pl.BlockSpec((GW, width), lambda q: (0, q)),
            pl.BlockSpec((nkb, width, LAT), lambda q: (0, 0, 0)),
            expand,
            expand,
        ],
        out_shape=[
            jax.ShapeDtypeStruct((GW, 2 * width), LOW),
            jax.ShapeDtypeStruct((nkb, width, LAT), F32),
            jax.ShapeDtypeStruct(kxt.shape, F32),
            jax.ShapeDtypeStruct(vxt.shape, F32),
        ],
        scratch_shapes=[
            pltpu.VMEM((LAT, wide), LOW),
            pltpu.VMEM((LAT, wide), LOW),
            pltpu.VMEM((1, wide), F32),
            pltpu.VMEM((LAT, wide), F32),
            pltpu.VMEM((width, wide), LOW),
            pltpu.VMEM((width, wide), LOW),
        ],
        compiler_params=pltpu.CompilerParams(
            dimension_semantics=("arbitrary",), vmem_limit_bytes=VMEM_LIMIT
        ),
        cost_estimate=pl.CostEstimate(
            flops=5 * pairs, bytes_accessed=10 << 20, transcendentals=7 * GH * width * width
        ),
        name="attention_backward",
    )(meta, qt, dot_, o_full, mix, lse, kxt, vxt, c, *old_dw)


def hidden_kernel(x, w, act, hidden):
    width = hidden.shape[1]
    both = mm(x[...], w[...])
    act[...] = both
    gate, up = both[:, :width], both[:, width:]
    hidden[...] = (gate * jax.nn.sigmoid(gate) * up).astype(LOW)


def hidden_back_kernel(cot, down, w, act, grad, own, other):
    width = down.shape[0]
    d_hidden = nt(cot[...], down[...])
    gate, up = act[:, :width], act[:, width:]
    sig = jax.nn.sigmoid(gate)
    grad[:, :width] = (d_hidden * up * sig * (1.0 + gate * (1.0 - sig))).astype(LOW)
    grad[:, width:] = (d_hidden * (gate * sig)).astype(LOW)
    back = nt(grad[...], w[...])
    mine = pl.program_id(0) < pl.num_programs(0) // 2

    @pl.when(mine)
    def _():
        own[...] = back

    @pl.when(jnp.logical_not(mine))
    def _():
        other[...] = back.astype(LOW)


TILE = 256


def tiled(width):
    return pl.BlockSpec((TILE, width), lambda i: (i, 0))


def resident(shape):
    return pl.BlockSpec(shape, lambda i: (0, 0), pipeline_mode=pl.Buffered(1))


def feed_forward(x, w):
    count, both = x.shape[0], w.shape[1]
    return pl.pallas_call(
        hidden_kernel,
        grid=(count // TILE,),
        in_specs=[tiled(x.shape[1]), resident(w.shape)],
        out_specs=[tiled(both), tiled(both // 2)],
        out_shape=[
            jax.ShapeDtypeStruct((count, both), F32),
            jax.ShapeDtypeStruct((count, both // 2), LOW),
        ],
        compiler_params=pltpu.CompilerParams(vmem_limit_bytes=VMEM_LIMIT),
        cost_estimate=pl.CostEstimate(
            flops=2 * x.size * both, bytes_accessed=20 << 20, transcendentals=count * both // 2
        ),
        name="feed_forward",
    )(x, w)


def feed_forward_back(cot, down, w, act):
    count, both = act.shape
    width, steps = w.shape[0], count // TILE
    return pl.pallas_call(
        hidden_back_kernel,
        grid=(steps,),
        in_specs=[tiled(cot.shape[1]), resident(down.shape), resident(w.shape), tiled(both)],
        out_specs=[
            tiled(both),
            pl.BlockSpec((TILE, width), lambda i: (jnp.minimum(i, steps // 2 - 1), 0)),
            pl.BlockSpec((TILE, width), lambda i: (jnp.maximum(i - steps // 2, 0), 0)),
        ],
        out_shape=[
            jax.ShapeDtypeStruct((count, both), LOW),
            jax.ShapeDtypeStruct((count // 2, width), F32),
            jax.ShapeDtypeStruct((count // 2, width), LOW),
        ],
        compiler_params=pltpu.CompilerParams(vmem_limit_bytes=VMEM_LIMIT),
        cost_estimate=pl.CostEstimate(
            flops=3 * cot.size * both, bytes_accessed=30 << 20, transcendentals=count * both // 2
        ),
        name="feed_forward_back",
    )(cot, down, w, act)


class Place:
    def __init__(self):
        self.seq, self.dp = lax.axis_size("seq"), lax.axis_size("dp")
        s, d = lax.axis_index("seq"), lax.axis_index("dp")
        self.core, self.chip = s % 2, s // 2
        self.y, self.x, self.z = s // 2, d % 2, d // 2
        self.square = self.seq == 4 and self.dp == 8

    def pairs(self, move):
        found = []
        for s in range(self.seq):
            for d in range(self.dp):
                target = move(s, d)
                if target is not None:
                    found.append((s * self.dp + d, target[0] * self.dp + target[1]))
        return found

    def send(self, value, move):
        return lax.ppermute(value, ALL, self.pairs(move))

    def to_core(self, value):
        return self.send(value, lambda s, d: (s ^ 1, d))

    def to_y(self, value):
        return self.send(value, lambda s, d: (s ^ 2, d))

    def to_x(self, value):
        return self.send(value, lambda s, d: (s, d ^ 1))

    def to_z(self, value, step):
        return self.send(value, lambda s, d: (s, (d + 2 * step) % 8))

    def up_y(self, value):
        return self.send(value, lambda s, d: (s + 2, d) if s < 2 else None)

    def down_y(self, value):
        return self.send(value, lambda s, d: (s - 2, d) if s >= 2 else None)


def half(value, index, axis, count=2):
    size = value.shape[axis] // count
    return lax.dynamic_slice_in_dim(value, index * size, size, axis)


def ordered(flag, own, other, axis):
    return jnp.where(
        flag == 0, jnp.concatenate([own, other], axis), jnp.concatenate([other, own], axis)
    )


def after(value, *others):
    return lax.optimization_barrier((value, others))[0]


def add_low(own, other):
    return (own.astype(F32) + other.astype(F32)).astype(LOW)


class Plain:
    def __init__(self, place):
        self.p = place
        count = place.seq // 2
        self.same_core = [[2 * i + c for i in range(count)] for c in range(2)]
        self.chip = [[2 * i, 2 * i + 1] for i in range(count)]

    def gather(self, w):
        core = self.p.core

        def full(value, axis=0):
            return lax.all_gather(value.astype(LOW), "dp", axis=axis, tiled=True)

        out = {name: full(half(w[name], core, 1)) for name in ("query", "latent", "gate", "up")}
        out["key_t"] = half(full(w["key"].T), core, 0)
        out["value_t"] = half(full(w["value"].T), core, 0)
        out["output"] = half(full(w["output"]), core, 0)
        out["down"] = half(full(w["down"]), core, 0)
        out["gain1"], out["gain2"] = full(w["gain1"]), full(w["gain2"])
        return out

    def columns(self, grad):
        share = lax.psum_scatter(grad.astype(LOW), "dp", scatter_dimension=0, tiled=True)
        share = lax.psum(share, "seq", axis_index_groups=self.same_core)
        return lax.all_gather(
            share, "seq", axis=1, tiled=True, axis_index_groups=self.chip
        ).astype(F32)

    def rows(self, grad):
        grad = grad.astype(LOW)
        grad = ordered(self.p.core, grad, jnp.zeros_like(grad), 0)
        share = lax.psum_scatter(grad, "dp", scatter_dimension=0, tiled=True)
        return lax.psum(share, "seq").astype(F32)

    def gain(self, grad):
        share = lax.psum_scatter(grad.astype(LOW), "dp", scatter_dimension=0, tiled=True)
        return lax.psum(share, "seq").astype(F32)


def inverse_rms(values):
    return lax.rsqrt(jnp.mean(values * values, axis=-1, keepdims=True) + EPS)


def norm_back(grad, normed, inverse, gain):
    scaled = grad * gain
    return inverse * (scaled - normed * jnp.mean(scaled * normed, axis=-1, keepdims=True))


def dots(spec, left, right):
    return jnp.einsum(spec, left, right, preferred_element_type=F32)


def pick(flag, zero, one):
    return jnp.where(flag == 0, zero, one)


def chip(p, own):
    return jnp.stack([own, p.to_core(own)], axis=1)


def chip_sum(p, partial):
    return partial[:, 0] + p.to_core(partial[:, 1].astype(LOW)).astype(F32)


def plain_layer(
    p, tokens, attn_gain, query_weight, latent_weight, key_expand, value_expand, output_weight,
    mlp_gain, gate_weight, up_weight, down_weight, cotangent, lengths,
):
    ways = Plain(p)
    batch, length, _ = tokens.shape
    count = 2 * batch * length
    w = ways.gather(
        {
            "gain1": attn_gain, "query": query_weight, "latent": latent_weight,
            "key": key_expand, "value": value_expand, "output": output_weight,
            "gain2": mlp_gain, "gate": gate_weight, "up": up_weight, "down": down_weight,
        }
    )
    gain1, gain2 = w["gain1"].astype(F32), w["gain2"].astype(F32)
    firsts = lengths[:, 0]
    chips = p.seq // 2
    rows = chip(p, tokens).astype(F32)
    first_low = (rows * inverse_rms(rows) * gain1).astype(LOW)
    first_flat = first_low.reshape(batch, 2 * length, D)
    latent = dots("btd,dl->btl", first_flat, w["latent"]).astype(LOW)
    query_t = dots("dn,btd->bnt", w["query"], first_flat).astype(LOW)
    blocks = latent.reshape(batch, 2, length, LAT)
    starts = jnp.stack([p.core, 1 - p.core]).astype(jnp.int32) * length
    base = p.chip * 2 * length
    keys = lax.all_gather(blocks, "seq", axis=1, tiled=True, axis_index_groups=ways.same_core)
    key_starts = (
        2 * length * jnp.arange(chips, dtype=jnp.int32)[:, None] + starts[None, :]
    ).reshape(-1)
    diag = (2 * p.chip).astype(jnp.int32).reshape(1)
    meta = jnp.concatenate([key_starts, base + starts, firsts, diag]).astype(jnp.int32)
    out_low, *att = attention_forward(meta, query_t, w["key_t"], w["value_t"], keys)
    branch = dots("bnt,nd->btd", out_low, w["output"])
    middle = tokens.astype(F32) + chip_sum(p, branch.reshape(batch, 2, length, D))
    inverse2 = inverse_rms(middle)
    normed2 = middle * inverse2
    second = chip(p, (normed2 * gain2).astype(LOW)).reshape(count, D)
    cot = chip(p, cotangent).reshape(count, D)
    gate = mm(second, w["gate"])
    up = mm(second, w["up"])
    sig = jax.nn.sigmoid(gate)
    act = gate * sig
    hidden = (act * up).astype(LOW)
    partial = mm(hidden, w["down"]).reshape(batch, 2, length, D)
    layer_out = (middle + chip_sum(p, partial)).astype(LOW)
    grad_down = ways.rows(tn(hidden, cot))
    d_hidden = nt(cot, w["down"])
    d_gate = (d_hidden * up * sig * (1.0 + gate * (1.0 - sig))).astype(LOW)
    d_up = (d_hidden * act).astype(LOW)
    grad_gate, grad_up = ways.columns(tn(second, d_gate)), ways.columns(tn(second, d_up))
    partial = (nt(d_gate, w["gate"]) + nt(d_up, w["up"])).reshape(batch, 2, length, D)
    d_second = chip_sum(p, partial)
    gain2_sum = jnp.sum(d_second * normed2, axis=(0, 1))
    d_middle = cotangent.astype(F32) + norm_back(d_second, normed2, inverse2, gain2)
    d_a = chip(p, d_middle.astype(LOW)).reshape(batch, 2 * length, D)
    grad_output = ways.rows(dots("bnt,btd->nd", out_low, d_a))
    d_out_t = dots("nd,btd->bnt", w["output"], d_a).astype(LOW)
    d_queries, d_keys, sums = [], [], ()
    for b in range(batch):
        found = attention_backward(
            b, meta, query_t, d_out_t, *att, w["key_t"], w["value_t"], keys, sums
        )
        sums = found[2:]
        d_queries.append(found[0])
        d_keys.append(found[1])
    dq_t, d_keys = jnp.stack(d_queries), jnp.stack(d_keys)
    d_key_t, d_value_t = sums
    d_blocks = lax.psum_scatter(
        d_keys.astype(LOW), "seq", scatter_dimension=1, tiled=True,
        axis_index_groups=ways.same_core,
    )
    d_latent = d_blocks.astype(LOW).reshape(batch, 2 * length, LAT)
    grad_query = ways.columns(dots("btd,bnt->dn", first_flat, dq_t))
    grad_latent = ways.columns(dots("btd,btl->dl", first_flat, d_latent))
    d_first = dots("bnt,dn->btd", dq_t, w["query"]) + dots("btl,dl->btd", d_latent, w["latent"])
    d_first = chip_sum(p, d_first.reshape(batch, 2, length, D))
    own = tokens.astype(F32)
    inverse1 = inverse_rms(own)
    normed1 = own * inverse1
    gain1_sum = jnp.sum(d_first * normed1, axis=(0, 1))
    grad_tokens = d_middle + norm_back(d_first, normed1, inverse1, gain1)
    return (
        layer_out, grad_tokens, ways.gain(gain1_sum), grad_query, grad_latent,
        ways.rows(d_key_t).T, ways.rows(d_value_t).T, grad_output, ways.gain(gain2_sum),
        grad_gate, grad_up, grad_down,
    )


class Live:
    def __init__(self, values):
        self.__dict__.update(values)

    @property
    def pop(self):
        return Taken(self)


class Taken:
    def __init__(self, live):
        self.live = live

    def __getattr__(self, name):
        return self.live.__dict__.pop(name)


def sync(v):
    return Live(lax.optimization_barrier(dict(v.__dict__)))


def in_z(p, seen):
    out = []
    for z in range(4):
        back = (p.z - z) % 4
        pair = [jnp.where(back % 2 == 0, seen[k], seen[k + 1]) for k in (0, 2)]
        out.append(jnp.where(back < 2, pair[0], pair[1]))
    return jnp.stack(out)


def z_gather(p, piece):
    return in_z(p, [piece] + [p.to_z(piece, k) for k in (1, 2, 3)])


def z_scatter(p, parts):
    total = half(parts, p.z, 0, 4)[0].astype(F32)
    for k in (1, 2, 3):
        total = total + p.to_z(half(parts, (p.z + k) % 4, 0, 4), k)[0].astype(F32)
    return total.astype(LOW)


def summed(p, make):
    come = p.to_core(make(1).astype(LOW))
    return make(0) + come.astype(F32)


def core_first(p, own):
    return jnp.concatenate([own, p.to_core(own)], 0)


def to_xy(p, value):
    return p.send(value, lambda s, d: (s ^ 2, d ^ 1))


def add_all(parts):
    return sum(part.astype(F32) for part in parts).astype(LOW)


def place_kernel(plan, sources, outs, where, *refs):
    src, dst = refs[:sources], refs[sources:]
    spot = where[0], where[1], where[2]
    for make in plan:
        source, there, out, here = make(*spot)
        if isinstance(source, int):
            dst[out][here] = src[source][there].astype(LOW)
            continue
        flag, sides = source[0], source[1:]
        for value in range(2):

            @pl.when(flag == value)
            def _(side=sides[value], there=there, out=out, here=here):
                dst[out][here] = src[side][there].astype(LOW)


def placed(p, plan, sources, shapes):
    where = jnp.stack([p.x, p.y, p.core]).astype(jnp.int32)
    inside = pl.BlockSpec(memory_space=pltpu.VMEM)
    return pl.pallas_call(
        lambda *refs: place_kernel(plan, len(sources), len(shapes), *refs),
        in_specs=[pl.BlockSpec(memory_space=pltpu.SMEM)] + [inside] * len(sources),
        out_specs=[inside] * len(shapes),
        out_shape=[jax.ShapeDtypeStruct(shape, LOW) for shape in shapes],
        compiler_params=pltpu.CompilerParams(vmem_limit_bytes=VMEM_LIMIT),
        name="place",
    )(where, *sources)


def lanes(start, width):
    return pl.ds(pl.multiple_of(start, 128), width)


RELATIVE = [(0, 0), (1, 0), (0, 1), (1, 1)]


def spread(p, parts):
    return parts[0], p.to_x(parts[1]), p.to_y(parts[2]), to_xy(p, parts[3])


def square_layer(
    p, tokens, attn_gain, query_weight, latent_weight, key_expand, value_expand, output_weight,
    mlp_gain, gate_weight, up_weight, down_weight, cotangent, lengths,
):
    batch, length, _ = tokens.shape
    count = 2 * batch * length
    core, x, y = p.core, p.x, p.y
    ff = gate_weight.shape[1] // 2
    quarter = 2 * core + y
    v = Live({})

    def cols(value, parts, index):
        return half(value, index, 1, parts).astype(LOW)

    def x_own(value):
        return half(value, x, 1)

    def x_other(value):
        return half(value, 1 - x, 1)

    v.pgu = jnp.concatenate([cols(gate_weight, 2, core), cols(up_weight, 2, core)], 1)
    v.tok = p.to_core(tokens)
    v = sync(v)
    kv = half(pick(y, key_expand, value_expand), core, 0).astype(LOW).T
    gains = jnp.stack([attn_gain, mlp_gain] + [jnp.zeros_like(attn_gain)] * 6).astype(LOW)
    piece = [
        cols(latent_weight, 4, quarter), cols(output_weight, 4, quarter),
        cols(query_weight, 4, quarter), kv,
    ]
    piece = jnp.concatenate(piece, 1)
    pad = jnp.zeros((8, piece.shape[1] - 128), LOW)
    piece = jnp.concatenate([piece, jnp.concatenate([gains, pad], 1)], 0)
    first = z_gather(p, piece)
    v.a, v.b = first[:, :, :384], first[:, :, 384:]
    rows = jnp.stack([tokens, v.pop.tok], 1).astype(F32)
    v.normed1 = rows * inverse_rms(rows)
    v.pd = cols(down_weight, 4, quarter)
    v = sync(v)

    v.ax, v.by = p.to_x(v.a), p.to_y(v.b)
    w_gu = lax.all_gather(v.pop.pgu, "dp", axis=0, tiled=True)
    v = sync(v)
    v.zd2 = p.to_z(v.pd, 2)
    v.ay, v.axy = p.to_y(v.a), p.to_y(v.ax)
    v.bx, v.bxy = p.to_x(v.b), p.to_x(v.by)
    v = sync(v)

    v.zd1 = p.to_z(v.pd, 1)
    v.from_ab = (v.pop.a, v.pop.ax, v.pop.ay, v.pop.axy, v.pop.b, v.pop.bx, v.pop.by, v.pop.bxy)
    plan = []
    for n, (r, k) in enumerate(RELATIVE):
        low = pl.ds(0, 128)
        plan += [
            lambda x, y, c, n=n, r=r, k=k: (
                n, (slice(None), low, pl.ds(0, 128)), 0,
                (slice(None), x ^ r, slice(None), lanes((y ^ k) * 128, 128)),
            ),
            lambda x, y, c, n=n, r=r, k=k: (
                4 + n, (slice(None), low, pl.ds(0, 256)), 1,
                (slice(None), x ^ r, slice(None), lanes((y ^ k) * 256, 256)),
            ),
            lambda x, y, c, n=n: (n, (pl.ds(2 * (1 - c), 2), low, pl.ds(128, 256)), 2, n),
            lambda x, y, c, n=n: (4 + n, (pl.ds(2 * (1 - c), 2), low, pl.ds(256, 128)), 3, n),
        ]
    wl, wq, v.wo_send, v.kv_send = placed(
        p, plan, v.from_ab,
        [(4, 2, 128, LAT), (4, 2, 128, GW), (4, 2, 128, 256), (4, 2, 128, 128)],
    )
    v.wl, v.wq = wl.reshape(D, LAT), wq.reshape(D, GW)
    gains = [part[:, 128:130, :128] for part in v.from_ab[:2]]
    gains = pick(x, jnp.stack(gains, 2), jnp.stack(gains[::-1], 2)).astype(F32)
    v.gain1, v.gain2 = gains[:, 0].reshape(D), gains[:, 1].reshape(D)
    v.first = (v.pop.normed1 * v.gain1).astype(LOW).reshape(batch, 2 * length, D)
    v.keys = dots("btd,dl->btl", v.first, v.wl).astype(LOW).reshape(batch, 2, length, LAT)
    v = sync(v)
    far_keys = p.up_y(v.keys)
    wo_come, kv_come = p.to_core(v.pop.wo_send), p.to_core(v.pop.kv_send)
    v.zd3 = p.to_z(v.pd, 3)
    v.qt = dots("dn,btd->bnt", v.wq, v.first).astype(LOW)
    plan = []
    for n, (r, k) in enumerate(RELATIVE):
        for s in range(2):
            plan += [
                lambda x, y, c, n=n, r=r, k=k, s=s: (
                    (n, (pl.ds(2 * c, 2), pl.ds(0, 128), pl.ds(128, 256))) if s == 0 else (8, n)
                ) + (0, (slice(None), x ^ r, slice(None), lanes(((c ^ s) * 2 + (y ^ k)) * 256, 256))),
                lambda x, y, c, n=n, r=r, k=k, s=s: (
                    (4 + n, (pl.ds(2 * c, 2), pl.ds(0, 128), pl.ds(256, 128))) if s == 0 else (9, n)
                ) + (1, (y ^ k, slice(None), x ^ r, slice(None), lanes((c ^ s) * 128, 128))),
            ]
    wo, kv = placed(
        p, plan, (*v.pop.from_ab, wo_come, kv_come), [(2, 2, 128, D), (2, 2, 2, 128, LAT)]
    )
    v.wo, kv = wo.reshape(GW, D), kv.reshape(2, GW, LAT)
    v.kxt, v.vxt = kv[0], kv[1]
    starts = jnp.stack([core, 1 - core]).astype(jnp.int32) * length
    base = p.chip * 2 * length
    far = pick(p.chip, 2 * length, 0)
    meta = [base + starts, far + starts, base + starts, lengths[:, 0], jnp.zeros((1,), jnp.int32)]
    v.meta = jnp.concatenate(meta).astype(jnp.int32)
    v.keys = jnp.concatenate([v.keys, far_keys], axis=1)
    v = sync(v)

    v.cot = core_first(p, cotangent.reshape(count // 2, D))
    v.zd = in_z(p, [v.pop.pd, v.pop.zd1, v.pop.zd2, v.pop.zd3])
    v.dax, v.dby = p.to_x(v.zd[:2]), p.to_y(v.zd[2:])
    cot = half(v.cot, core, 1)
    v.cot_c = [half(cot, i, 1) for i in (y, 1 - y)] + [half(v.cot, 1 - core, 1)]
    v.out, *v.att = attention_forward(v.meta, v.qt, v.kxt, v.vxt, v.keys)
    v = sync(v)

    v.day, v.daxy = p.to_y(v.zd[:2]), p.to_y(v.dax)
    v.dbx, v.dbxy = p.to_x(v.zd[2:]), p.to_x(v.dby)
    branch = summed(
        p, lambda i: dots("bnt,nd->btd", v.out[:, :, i * length : (i + 1) * length], v.wo)
    )
    v.middle = tokens.astype(F32) + branch
    v.inv2 = inverse_rms(v.middle)
    second = v.middle * v.inv2 * v.gain2
    v.second = core_first(p, second.astype(LOW).reshape(count // 2, D))
    v = sync(v)

    front, back = v.zd[:2], v.pop.zd[2:]
    sides = (front, v.pop.dax, v.pop.day, v.pop.daxy, back, v.pop.dbx, v.pop.dby, v.pop.dbxy)
    whole = slice(None)
    plan = [lambda x, y, c, n=n: ((c, 4 + n, n), whole, 0, n) for n in range(4)]
    v.come = p.to_core(placed(p, plan, sides, [(4, 2, ff // 4, 256)])[0])
    v.sides = sides
    v.w_gu = w_gu
    v.act, v.hidden = feed_forward(v.second, v.w_gu)
    v = sync(v)
    plan = []
    for n, (r, k) in enumerate(RELATIVE):
        for s in range(2):
            plan += [
                lambda x, y, c, n=n, r=r, k=k, s=s: (
                    ((c, n, 4 + n), whole) if s == 0 else (8, n)
                ) + (
                    0, (whole, x ^ r, whole, lanes(((c ^ s) * 2 + (y ^ k)) * 256, 256)),
                )
            ]
    wd = placed(p, plan, (*v.pop.sides, v.pop.come), [(2, 2, ff // 4, D)])[0]
    v.wd = wd.reshape(ff, D)

    v.d_gu, v.ds_own, v.ds_other = feed_forward_back(v.cot, v.wd, v.pop.w_gu, v.pop.act)
    v = sync(v)
    d_second = (v.pop.ds_own + p.to_core(v.pop.ds_other).astype(F32)).reshape(batch, length, D)
    v.gg = tn(v.pop.second, v.pop.d_gu).astype(LOW)
    normed2 = v.middle * v.inv2
    v.gain2_sum = jnp.sum(d_second * normed2, axis=(0, 1))
    v.d_middle = cotangent.astype(F32) + norm_back(d_second, normed2, v.pop.inv2, v.pop.gain2)
    v.d_a = chip(p, v.d_middle.astype(LOW)).reshape(batch, 2 * length, D)
    v = sync(v)
    gg = lax.psum_scatter(v.pop.gg, "dp", scatter_dimension=0, tiled=True)
    go = dots("bnt,btd->nd", v.pop.out, v.d_a).astype(LOW).reshape(2, 2, 128, D)
    go_core = half(go, core, 3)
    go_parts = [half(go_core, y, 3), half(go_core, 1 - y, 3), half(go, 1 - core, 3)]
    gd_parts = [tn(v.hidden, part).astype(LOW) for part in v.pop.cot_c]
    v.r_a, v.r_ay, r_send = [
        jnp.concatenate([gd.reshape(2, 2, -1, gd.shape[-1]), go], 2)
        for gd, go in zip(gd_parts, go_parts)
    ]
    v.r_b = p.to_core(r_send)
    v.dot = dots("nd,btd->bnt", v.pop.wo, v.pop.d_a).astype(LOW)
    v = sync(v)

    full = slice(None)
    rows = count // 2
    branch = summed(p, lambda i: mm(v.hidden[i * rows : (i + 1) * rows], v.wd))
    v.out_done = (v.pop.middle + branch.reshape(batch, length, D)).astype(LOW)
    del v.hidden, v.wd
    v.r_ay, v.r_bx = p.to_y(v.r_ay), p.to_x(x_other(v.r_b))
    v.back0 = attention_backward(
        0, v.meta, v.qt, v.dot, *v.att, v.kxt, v.vxt, v.keys, ()
    )
    v = sync(v)
    layer_out = v.pop.out_done
    v.r_a = add_low(v.r_a, v.pop.r_ay)
    v.r_b = add_low(x_own(v.r_b), v.pop.r_bx)
    v.r_ax, v.r_by = p.to_x(x_other(v.r_a)), p.to_y(half(v.r_b, 1 - y, 3))
    d_keys = v.back0[1]
    v.dk0, v.dk_far0 = d_keys[:2], p.down_y(d_keys[2:].astype(LOW))
    v.back1 = attention_backward(
        1, v.meta, v.qt, v.dot, *v.att, v.kxt, v.vxt, v.keys, v.back0[2:]
    )
    v = sync(v)

    back0, back1 = v.pop.back0, v.pop.back1
    v.far1 = p.down_y(back1[1][2:].astype(LOW))
    v.dk1 = back1[1][:2]
    v.dk0 = (v.dk0 + v.pop.dk_far0.astype(F32)).astype(LOW).reshape(1, 2 * length, LAT)
    plan = []
    for n in range(2):
        for s in range(2):
            plan += [
                lambda x, y, c, n=n, s=s: (n, (slice(None), lanes((c ^ s) * 128, 128)), s, n)
            ]
    v.kv_mine, kv_send = placed(p, plan, back1[2:], [(2, GW, 128)] * 2)
    v.kv_come = p.to_core(kv_send)
    r_a = add_low(x_own(v.pop.r_a), v.pop.r_ax)[:, 0]
    r_b = add_low(half(v.pop.r_b, y, 3), v.pop.r_by)[:, 0]
    v.r = ordered(core, r_a, r_b, 0)

    def r_step(k):
        return p.to_z(half(v.r, (p.z + k) % 4, 0, 4), k)

    v.dq_t = jnp.stack([back0[0], back1[0]])
    v.gq = dots("btd,bnt->dn", v.first, v.dq_t).astype(LOW).reshape(4, 2, 128, GW)
    v = sync(v)
    v.r1, v.r2, v.r3 = r_step(1), r_step(2), r_step(3)
    dk1 = (v.pop.dk1 + v.pop.far1.astype(F32)).astype(LOW).reshape(1, 2 * length, LAT)
    d_latent = jnp.concatenate([v.pop.dk0, dk1])
    gl = dots("btd,btl->dl", v.pop.first, d_latent).astype(LOW).reshape(4, 2, 128, LAT)
    plan = []
    for n, (r, k) in enumerate(RELATIVE):
        plan += [
            lambda x, y, c, n=n, r=r, k=k: (
                0, (full, x ^ r, full, lanes((y ^ k) * 256, 256)), n, (full, full, pl.ds(0, 256)),
            ),
            lambda x, y, c, n=n, r=r, k=k: (
                1, (full, x ^ r, full, lanes((y ^ k) * 128, 128)), n, (full, full, pl.ds(384, 128)),
            ),
        ]
        for s in range(2):
            plan += [
                lambda x, y, c, n=n, r=r, k=k, s=s: (
                    2 + s, (y ^ k, full, x ^ r), n, (pl.ds(2 * (c ^ s), 2), full, pl.ds(256, 128)),
                )
            ]
    kv = [part.reshape(2, 2, 2, 128, 128) for part in (v.pop.kv_mine, v.pop.kv_come)]
    v.found = spread(p, placed(p, plan, (v.pop.gq, gl, *kv), [(4, 128, 512)] * 4))
    dq_t = v.pop.dq_t

    def first_grad(i):
        part = slice(i * length, (i + 1) * length)
        by_q = dots("bnt,dn->btd", dq_t[:, :, part], v.wq)
        return by_q + dots("btl,dl->btd", d_latent[:, part], v.wl)

    d_first = summed(p, first_grad)
    own = tokens.astype(F32)
    inverse1 = inverse_rms(own)
    normed1 = own * inverse1
    gains = jnp.stack([jnp.sum(d_first * normed1, axis=(0, 1)), v.pop.gain2_sum])
    v.gains = gains.astype(LOW).reshape(2, 4, 2, 128)
    v.tokens_done = v.d_middle + norm_back(d_first, normed1, inverse1, v.gain1)
    v = sync(v)
    grad_tokens = v.pop.tokens_done
    v.r = add_all([half(v.r, p.z, 0, 4), v.pop.r1, v.pop.r2, v.pop.r3])[0]
    gains = jnp.moveaxis(v.pop.gains, 0, 1).reshape(4, 4, 128)
    gains = jnp.pad(gains, ((0, 0), (0, 4), (0, 384)))
    v.q = z_scatter(p, jnp.concatenate([add_all(v.pop.found), gains], 1))
    v.gg = gg
    v.gg = add_low(v.gg, p.to_y(v.gg))
    v = sync(v)
    v.q1 = p.to_y(v.q)
    v.gg1, v.r1 = p.to_core(v.gg), p.to_y(v.r)
    v = sync(v)
    grad_gate = ordered(core, v.gg[:, :ff], v.gg1[:, :ff], 1).astype(F32)
    grad_up = ordered(core, v.gg[:, ff:], v.gg1[:, ff:], 1).astype(F32)
    r = ordered(y, v.r, v.r1, 1)
    grad_rows = ordered(core, r, p.to_core(r), 1).astype(F32)
    grad_down, grad_output = grad_rows[: ff // 4], grad_rows[ff // 4 :]
    gains = add_low(v.q[128:132, :128], v.q1[128:132, :128])
    x_gains = p.to_x(gains)
    q0, q1 = pick(y, v.q, v.q1), pick(y, v.q1, v.q)
    mine = jnp.concatenate([q0, q1], 1)
    mine = lax.dynamic_update_slice(mine, gains, (128, 0))
    other = p.to_core(mine)
    x_other_gains = p.send(gains, lambda s, d: (s ^ 1, d ^ 1))
    zero, one = pick(core, mine, other), pick(core, other, mine)

    def columns(start, width):
        found = [part[:128, i : i + width] for part in (zero, one) for i in (start, start + 512)]
        return jnp.concatenate(found, 1).astype(F32)

    def expand_grad(start):
        return jnp.concatenate([p_[:128, start : start + 128] for p_ in (zero, one)], 1)

    near_gains = pick(x, gains, x_gains).astype(F32) + pick(x, x_gains, gains).astype(F32)
    far = other[128:132, :128]
    far_gains = pick(x, far, x_other_gains).astype(F32) + pick(x, x_other_gains, far).astype(F32)
    gains = half((near_gains + far_gains).reshape(2, 2, 128), x, 1)[:, 0]
    return (
        layer_out, grad_tokens, gains[0], columns(0, 256), columns(384, 128),
        expand_grad(256).T.astype(F32), expand_grad(768).T.astype(F32), grad_output, gains[1],
        grad_gate, grad_up, grad_down,
    )


def per_device(*arguments):
    p = Place()
    return (square_layer if p.square else plain_layer)(p, *arguments)


def solution(mesh):
    rows, gain, weight, across = P("dp", "seq", None), P("dp"), P("dp", None), P(None, "dp")
    return jax.shard_map(
        per_device,
        mesh=mesh,
        in_specs=(
            rows, gain, weight, weight, across, across, weight, gain, weight, weight, weight, rows,
            P("dp", None),
        ),
        out_specs=(
            rows, rows, gain, weight, weight, across, across, weight, gain, weight, weight, weight,
        ),
        check_vma=False,
    )
```

```python
import jax
import jax.numpy as jnp
from jax import lax
from jax.experimental import pallas as pl
from jax.experimental.pallas import tpu as pltpu
from jax.sharding import PartitionSpec as P

D = 1024
H = 16
HD = 64
KVH = 2
LAT = 256
GH = H // KVH
GW = D // KVH
EPS = 1e-06
SCALE = HD ** (-0.5)
LOG2E = 1.4426950408889634
NEG = -1e30

LOW = jnp.bfloat16
F32 = jnp.float32
ALL = ("seq", "dp")
VMEM_LIMIT = 56 * 1024 * 1024


def mm(left, right):
    return jnp.dot(left, right, preferred_element_type=F32)


def tn(left, right):
    return lax.dot_general(left, right, (((0,), (0,)), ((), ())), preferred_element_type=F32)


def nt(left, right):
    return lax.dot_general(left, right, (((1,), (1,)), ((), ())), preferred_element_type=F32)


def block_bias(k0, q0, first, width):
    kpos = k0 + lax.broadcasted_iota(jnp.int32, (width, width), 0)
    qpos = q0 + lax.broadcasted_iota(jnp.int32, (width, width), 1)
    lowest = jnp.where(qpos >= first, first, 0)
    return jnp.where((kpos <= qpos) & (kpos >= lowest), 0.0, NEG)


def block_needed(k0, q0, first, width):
    before = jnp.logical_and(q0 >= first, k0 + (width - 1) < first)
    return jnp.logical_and(k0 <= q0, jnp.logical_not(before))


def forward_kernel(nkb, batch, width, meta, qt, kxt, vxt, c, o_low, o_full, mix_out, lse_out, q_s, acc, m_s, l_s, p_s):
    b, qb = pl.program_id(0), pl.program_id(1)
    q0, first, diag = meta[nkb + qb], meta[nkb + 2 + b], meta[nkb + 2 + batch] + qb
    for h in range(GH):
        cols = slice(h * width, (h + 1) * width)
        rows = slice(h * HD, (h + 1) * HD)
        q_s[:, cols] = (tn(kxt[rows, :], qt[0, rows, :]) * (SCALE * LOG2E)).astype(LOW)
    m_s[...] = jnp.full_like(m_s, NEG)
    l_s[...] = jnp.zeros_like(l_s)
    acc[...] = jnp.zeros_like(acc)

    def step(j, carry):
        kb = lax.rem(diag + j, nkb)
        k0 = meta[kb]

        @pl.when(block_needed(k0, q0, first, width))
        def _():
            bias = block_bias(k0, q0, first, width)
            keys = c[0, kb]
            keys_t = keys.T
            alphas = []
            for h in range(GH):
                cols = slice(h * width, (h + 1) * width)
                s = mm(keys, q_s[:, cols]) + bias
                m_old = m_s[:, cols]
                m_new = jnp.maximum(m_old, jnp.max(s, axis=0, keepdims=True))
                p = jnp.exp2(s - m_new)
                alpha = jnp.exp2(m_old - m_new)
                m_s[:, cols] = m_new
                l_s[:, cols] = l_s[:, cols] * alpha + jnp.sum(p, axis=0, keepdims=True)
                p_s[:, cols] = p.astype(LOW)
                alphas.append(alpha)
            acc[...] = acc[...] * jnp.concatenate(alphas, 1) + mm(keys_t, p_s[...])

        return carry

    lax.fori_loop(0, nkb, step, 0)
    for h in range(GH):
        cols = slice(h * width, (h + 1) * width)
        rows = slice(h * HD, (h + 1) * HD)
        total = l_s[:, cols]
        mixed = (acc[:, cols] * (1.0 / total)).astype(LOW)
        mix_out[0, 0, :, cols] = mixed
        out = mm(vxt[rows, :], mixed)
        o_full[0, rows, :] = out
        o_low[0, rows, :] = out.astype(LOW)
        lse_out[0, 0, :, cols] = m_s[:, cols] + jnp.log(total) * LOG2E


def backward_kernel(
    b, nkb, batch, width, add_dw, meta, qt, dot_, o_full, mix, lse, kxt, vxt, c, *refs
):
    refs = list(refs)
    dk_old, dv_old = (refs.pop(0), refs.pop(0)) if add_dw else (None, None)
    dqt, dc, dkxt, dvxt, q_s, do_t, delta, dq, ds_s, p_s = refs
    qb = pl.program_id(0)
    q0, first, diag = meta[nkb + qb], meta[nkb + 2 + b], meta[nkb + 2 + batch] + qb

    @pl.when(qb == 0)
    def _():
        dc[...] = jnp.zeros_like(dc)
        dkxt[...] = dk_old[...] if add_dw else jnp.zeros_like(dkxt)
        dvxt[...] = dv_old[...] if add_dw else jnp.zeros_like(dvxt)


    for h in range(GH):
        cols = slice(h * width, (h + 1) * width)
        rows = slice(h * HD, (h + 1) * HD)
        qh, kh, doh, vh = qt[0, rows, :], kxt[rows, :], dot_[0, rows, :], vxt[rows, :]
        q_s[:, cols] = (tn(kh, qh) * (SCALE * LOG2E)).astype(LOW)
        do_t[:, cols] = tn(vh, doh).astype(LOW)
        delta[:, cols] = jnp.sum(doh.astype(F32) * o_full[0, rows, :], axis=0, keepdims=True)
    dq[...] = jnp.zeros_like(dq)

    def step(j, carry):
        kb = lax.rem(diag + j, nkb)
        k0 = meta[kb]

        @pl.when(block_needed(k0, q0, first, width))
        def _():
            bias = block_bias(k0, q0, first, width)
            keys = c[0, kb]
            keys_t = keys.T
            for h in range(GH):
                cols = slice(h * width, (h + 1) * width)
                s = mm(keys, q_s[:, cols]) + bias
                p = jnp.exp2(s - lse[0, 0, :, cols])
                dp = mm(keys, do_t[:, cols])
                ds = (p * (dp - delta[:, cols])).astype(LOW)
                p_s[:, cols] = p.astype(LOW)
                ds_s[:, cols] = ds
            dq[...] += mm(keys_t, ds_s[...])
            dc[kb] += nt(ds_s[...], q_s[...]) * (1.0 / LOG2E) + nt(p_s[...], do_t[...])

        return carry

    lax.fori_loop(0, nkb, step, 0)
    for h in range(GH):
        cols = slice(h * width, (h + 1) * width)
        rows = slice(h * HD, (h + 1) * HD)
        dq_low = (dq[:, cols] * SCALE).astype(LOW)
        dqt[rows, :] = mm(kxt[rows, :], dq_low).astype(LOW)
        dkxt[rows, :] += nt(qt[0, rows, :], dq_low)
        dvxt[rows, :] += nt(dot_[0, rows, :], mix[0, 0, :, cols])


def attention_forward(meta, qt, kxt, vxt, c):
    batch, nkb, width, _ = c.shape
    wide = GH * width
    pairs = batch * 7 * GH * width * width * LAT
    expand = pl.BlockSpec((GW, LAT), lambda b, q: (0, 0))
    q_spec = pl.BlockSpec((1, GW, width), lambda b, q: (b, 0, q))
    return pl.pallas_call(
        lambda *refs: forward_kernel(nkb, batch, width, *refs),
        grid=(batch, 2),
        in_specs=[
            pl.BlockSpec(memory_space=pltpu.SMEM),
            q_spec,
            expand,
            expand,
            pl.BlockSpec((1, nkb, width, LAT), lambda b, q: (b, 0, 0, 0)),
        ],
        out_specs=[
            q_spec,
            q_spec,
            pl.BlockSpec((1, 1, LAT, wide), lambda b, q: (b, q, 0, 0)),
            pl.BlockSpec((1, 1, 1, wide), lambda b, q: (b, q, 0, 0)),
        ],
        out_shape=[
            jax.ShapeDtypeStruct(qt.shape, LOW),
            jax.ShapeDtypeStruct(qt.shape, F32),
            jax.ShapeDtypeStruct((batch, 2, LAT, wide), LOW),
            jax.ShapeDtypeStruct((batch, 2, 1, wide), F32),
        ],
        scratch_shapes=[
            pltpu.VMEM((LAT, wide), LOW),
            pltpu.VMEM((LAT, wide), F32),
            pltpu.VMEM((1, wide), F32),
            pltpu.VMEM((1, wide), F32),
            pltpu.VMEM((width, wide), LOW),
        ],
        compiler_params=pltpu.CompilerParams(
            dimension_semantics=("arbitrary", "arbitrary"), vmem_limit_bytes=VMEM_LIMIT
        ),
        cost_estimate=pl.CostEstimate(
            flops=4 * pairs, bytes_accessed=16 << 20, transcendentals=batch * 7 * GH * width * width
        ),
        name="attention_forward",
    )(meta, qt, kxt, vxt, c)


def attention_backward(b, meta, qt, dot_, o_full, mix, lse, kxt, vxt, c, old_dw):
    batch, nkb, width, _ = c.shape
    wide = GH * width
    pairs = 7 * GH * width * width * LAT * 2
    expand = pl.BlockSpec((GW, LAT), lambda q: (0, 0))
    return pl.pallas_call(
        lambda *refs: backward_kernel(b, nkb, batch, width, bool(old_dw), *refs),
        grid=(2,),
        in_specs=[
            pl.BlockSpec(memory_space=pltpu.SMEM),
            pl.BlockSpec((1, GW, width), lambda q: (b, 0, q)),
            pl.BlockSpec((1, GW, width), lambda q: (b, 0, q)),
            pl.BlockSpec((1, GW, width), lambda q: (b, 0, q)),
            pl.BlockSpec((1, 1, LAT, wide), lambda q: (b, q, 0, 0)),
            pl.BlockSpec((1, 1, 1, wide), lambda q: (b, q, 0, 0)),
            expand,
            expand,
            pl.BlockSpec((1, nkb, width, LAT), lambda q: (b, 0, 0, 0)),
        ]
        + [expand] * len(old_dw),
        out_specs=[
            pl.BlockSpec((GW, width), lambda q: (0, q)),
            pl.BlockSpec((nkb, width, LAT), lambda q: (0, 0, 0)),
            expand,
            expand,
        ],
        out_shape=[
            jax.ShapeDtypeStruct((GW, 2 * width), LOW),
            jax.ShapeDtypeStruct((nkb, width, LAT), F32),
            jax.ShapeDtypeStruct(kxt.shape, F32),
            jax.ShapeDtypeStruct(vxt.shape, F32),
        ],
        scratch_shapes=[
            pltpu.VMEM((LAT, wide), LOW),
            pltpu.VMEM((LAT, wide), LOW),
            pltpu.VMEM((1, wide), F32),
            pltpu.VMEM((LAT, wide), F32),
            pltpu.VMEM((width, wide), LOW),
            pltpu.VMEM((width, wide), LOW),
        ],
        compiler_params=pltpu.CompilerParams(
            dimension_semantics=("arbitrary",), vmem_limit_bytes=VMEM_LIMIT
        ),
        cost_estimate=pl.CostEstimate(
            flops=5 * pairs, bytes_accessed=10 << 20, transcendentals=7 * GH * width * width
        ),
        name="attention_backward",
    )(meta, qt, dot_, o_full, mix, lse, kxt, vxt, c, *old_dw)


def hidden_kernel(x, w, act, hidden):
    width = hidden.shape[1]
    both = mm(x[...], w[...])
    act[...] = both
    gate, up = both[:, :width], both[:, width:]
    hidden[...] = (gate * jax.nn.sigmoid(gate) * up).astype(LOW)


def hidden_back_kernel(cot, down, w, act, grad, own, other):
    width = down.shape[0]
    d_hidden = nt(cot[...], down[...])
    gate, up = act[:, :width], act[:, width:]
    sig = jax.nn.sigmoid(gate)
    grad[:, :width] = (d_hidden * up * sig * (1.0 + gate * (1.0 - sig))).astype(LOW)
    grad[:, width:] = (d_hidden * (gate * sig)).astype(LOW)
    back = nt(grad[...], w[...])
    mine = pl.program_id(0) < pl.num_programs(0) // 2

    @pl.when(mine)
    def _():
        own[...] = back

    @pl.when(jnp.logical_not(mine))
    def _():
        other[...] = back.astype(LOW)


TILE = 256


def tiled(width):
    return pl.BlockSpec((TILE, width), lambda i: (i, 0))


def resident(shape):
    return pl.BlockSpec(shape, lambda i: (0, 0), pipeline_mode=pl.Buffered(1))


def feed_forward(x, w):
    count, both = x.shape[0], w.shape[1]
    return pl.pallas_call(
        hidden_kernel,
        grid=(count // TILE,),
        in_specs=[tiled(x.shape[1]), resident(w.shape)],
        out_specs=[tiled(both), tiled(both // 2)],
        out_shape=[
            jax.ShapeDtypeStruct((count, both), F32),
            jax.ShapeDtypeStruct((count, both // 2), LOW),
        ],
        compiler_params=pltpu.CompilerParams(vmem_limit_bytes=VMEM_LIMIT),
        cost_estimate=pl.CostEstimate(
            flops=2 * x.size * both, bytes_accessed=20 << 20, transcendentals=count * both // 2
        ),
        name="feed_forward",
    )(x, w)


def feed_forward_back(cot, down, w, act):
    count, both = act.shape
    width, steps = w.shape[0], count // TILE
    return pl.pallas_call(
        hidden_back_kernel,
        grid=(steps,),
        in_specs=[tiled(cot.shape[1]), resident(down.shape), resident(w.shape), tiled(both)],
        out_specs=[
            tiled(both),
            pl.BlockSpec((TILE, width), lambda i: (jnp.minimum(i, steps // 2 - 1), 0)),
            pl.BlockSpec((TILE, width), lambda i: (jnp.maximum(i - steps // 2, 0), 0)),
        ],
        out_shape=[
            jax.ShapeDtypeStruct((count, both), LOW),
            jax.ShapeDtypeStruct((count // 2, width), F32),
            jax.ShapeDtypeStruct((count // 2, width), LOW),
        ],
        compiler_params=pltpu.CompilerParams(vmem_limit_bytes=VMEM_LIMIT),
        cost_estimate=pl.CostEstimate(
            flops=3 * cot.size * both, bytes_accessed=30 << 20, transcendentals=count * both // 2
        ),
        name="feed_forward_back",
    )(cot, down, w, act)


class Place:
    def __init__(self):
        self.seq, self.dp = lax.axis_size("seq"), lax.axis_size("dp")
        s, d = lax.axis_index("seq"), lax.axis_index("dp")
        self.core, self.chip = s % 2, s // 2
        self.y, self.x, self.z = s // 2, d % 2, d // 2
        self.square = self.seq == 4 and self.dp == 8

    def pairs(self, move):
        found = []
        for s in range(self.seq):
            for d in range(self.dp):
                target = move(s, d)
                if target is not None:
                    found.append((s * self.dp + d, target[0] * self.dp + target[1]))
        return found

    def send(self, value, move):
        return lax.ppermute(value, ALL, self.pairs(move))

    def to_core(self, value):
        return self.send(value, lambda s, d: (s ^ 1, d))

    def to_y(self, value):
        return self.send(value, lambda s, d: (s ^ 2, d))

    def to_x(self, value):
        return self.send(value, lambda s, d: (s, d ^ 1))

    def to_z(self, value, step):
        return self.send(value, lambda s, d: (s, (d + 2 * step) % 8))

    def up_y(self, value):
        return self.send(value, lambda s, d: (s + 2, d) if s < 2 else None)

    def down_y(self, value):
        return self.send(value, lambda s, d: (s - 2, d) if s >= 2 else None)


def half(value, index, axis, count=2):
    size = value.shape[axis] // count
    return lax.dynamic_slice_in_dim(value, index * size, size, axis)


def ordered(flag, own, other, axis):
    return jnp.where(
        flag == 0, jnp.concatenate([own, other], axis), jnp.concatenate([other, own], axis)
    )


def after(value, *others):
    return lax.optimization_barrier((value, others))[0]


def add_low(own, other):
    return (own.astype(F32) + other.astype(F32)).astype(LOW)


class Plain:
    def __init__(self, place):
        self.p = place
        count = place.seq // 2
        self.same_core = [[2 * i + c for i in range(count)] for c in range(2)]
        self.chip = [[2 * i, 2 * i + 1] for i in range(count)]

    def gather(self, w):
        core = self.p.core

        def full(value, axis=0):
            return lax.all_gather(value.astype(LOW), "dp", axis=axis, tiled=True)

        out = {name: full(half(w[name], core, 1)) for name in ("query", "latent", "gate", "up")}
        out["key_t"] = half(full(w["key"].T), core, 0)
        out["value_t"] = half(full(w["value"].T), core, 0)
        out["output"] = half(full(w["output"]), core, 0)
        out["down"] = half(full(w["down"]), core, 0)
        out["gain1"], out["gain2"] = full(w["gain1"]), full(w["gain2"])
        return out

    def columns(self, grad):
        share = lax.psum_scatter(grad.astype(LOW), "dp", scatter_dimension=0, tiled=True)
        share = lax.psum(share, "seq", axis_index_groups=self.same_core)
        return lax.all_gather(
            share, "seq", axis=1, tiled=True, axis_index_groups=self.chip
        ).astype(F32)

    def rows(self, grad):
        grad = grad.astype(LOW)
        grad = ordered(self.p.core, grad, jnp.zeros_like(grad), 0)
        share = lax.psum_scatter(grad, "dp", scatter_dimension=0, tiled=True)
        return lax.psum(share, "seq").astype(F32)

    def gain(self, grad):
        share = lax.psum_scatter(grad.astype(LOW), "dp", scatter_dimension=0, tiled=True)
        return lax.psum(share, "seq").astype(F32)


def inverse_rms(values):
    return lax.rsqrt(jnp.mean(values * values, axis=-1, keepdims=True) + EPS)


def norm_back(grad, normed, inverse, gain):
    scaled = grad * gain
    return inverse * (scaled - normed * jnp.mean(scaled * normed, axis=-1, keepdims=True))


def dots(spec, left, right):
    return jnp.einsum(spec, left, right, preferred_element_type=F32)


def pick(flag, zero, one):
    return jnp.where(flag == 0, zero, one)


def chip(p, own):
    return jnp.stack([own, p.to_core(own)], axis=1)


def chip_sum(p, partial):
    return partial[:, 0] + p.to_core(partial[:, 1].astype(LOW)).astype(F32)


def plain_layer(
    p, tokens, attn_gain, query_weight, latent_weight, key_expand, value_expand, output_weight,
    mlp_gain, gate_weight, up_weight, down_weight, cotangent, lengths,
):
    ways = Plain(p)
    batch, length, _ = tokens.shape
    count = 2 * batch * length
    w = ways.gather(
        {
            "gain1": attn_gain, "query": query_weight, "latent": latent_weight,
            "key": key_expand, "value": value_expand, "output": output_weight,
            "gain2": mlp_gain, "gate": gate_weight, "up": up_weight, "down": down_weight,
        }
    )
    gain1, gain2 = w["gain1"].astype(F32), w["gain2"].astype(F32)
    firsts = lengths[:, 0]
    chips = p.seq // 2
    rows = chip(p, tokens).astype(F32)
    first_low = (rows * inverse_rms(rows) * gain1).astype(LOW)
    first_flat = first_low.reshape(batch, 2 * length, D)
    latent = dots("btd,dl->btl", first_flat, w["latent"]).astype(LOW)
    query_t = dots("dn,btd->bnt", w["query"], first_flat).astype(LOW)
    blocks = latent.reshape(batch, 2, length, LAT)
    starts = jnp.stack([p.core, 1 - p.core]).astype(jnp.int32) * length
    base = p.chip * 2 * length
    keys = lax.all_gather(blocks, "seq", axis=1, tiled=True, axis_index_groups=ways.same_core)
    key_starts = (
        2 * length * jnp.arange(chips, dtype=jnp.int32)[:, None] + starts[None, :]
    ).reshape(-1)
    diag = (2 * p.chip).astype(jnp.int32).reshape(1)
    meta = jnp.concatenate([key_starts, base + starts, firsts, diag]).astype(jnp.int32)
    out_low, *att = attention_forward(meta, query_t, w["key_t"], w["value_t"], keys)
    branch = dots("bnt,nd->btd", out_low, w["output"])
    middle = tokens.astype(F32) + chip_sum(p, branch.reshape(batch, 2, length, D))
    inverse2 = inverse_rms(middle)
    normed2 = middle * inverse2
    second = chip(p, (normed2 * gain2).astype(LOW)).reshape(count, D)
    cot = chip(p, cotangent).reshape(count, D)
    gate = mm(second, w["gate"])
    up = mm(second, w["up"])
    sig = jax.nn.sigmoid(gate)
    act = gate * sig
    hidden = (act * up).astype(LOW)
    partial = mm(hidden, w["down"]).reshape(batch, 2, length, D)
    layer_out = (middle + chip_sum(p, partial)).astype(LOW)
    grad_down = ways.rows(tn(hidden, cot))
    d_hidden = nt(cot, w["down"])
    d_gate = (d_hidden * up * sig * (1.0 + gate * (1.0 - sig))).astype(LOW)
    d_up = (d_hidden * act).astype(LOW)
    grad_gate, grad_up = ways.columns(tn(second, d_gate)), ways.columns(tn(second, d_up))
    partial = (nt(d_gate, w["gate"]) + nt(d_up, w["up"])).reshape(batch, 2, length, D)
    d_second = chip_sum(p, partial)
    gain2_sum = jnp.sum(d_second * normed2, axis=(0, 1))
    d_middle = cotangent.astype(F32) + norm_back(d_second, normed2, inverse2, gain2)
    d_a = chip(p, d_middle.astype(LOW)).reshape(batch, 2 * length, D)
    grad_output = ways.rows(dots("bnt,btd->nd", out_low, d_a))
    d_out_t = dots("nd,btd->bnt", w["output"], d_a).astype(LOW)
    d_queries, d_keys, sums = [], [], ()
    for b in range(batch):
        found = attention_backward(
            b, meta, query_t, d_out_t, *att, w["key_t"], w["value_t"], keys, sums
        )
        sums = found[2:]
        d_queries.append(found[0])
        d_keys.append(found[1])
    dq_t, d_keys = jnp.stack(d_queries), jnp.stack(d_keys)
    d_key_t, d_value_t = sums
    d_blocks = lax.psum_scatter(
        d_keys.astype(LOW), "seq", scatter_dimension=1, tiled=True,
        axis_index_groups=ways.same_core,
    )
    d_latent = d_blocks.astype(LOW).reshape(batch, 2 * length, LAT)
    grad_query = ways.columns(dots("btd,bnt->dn", first_flat, dq_t))
    grad_latent = ways.columns(dots("btd,btl->dl", first_flat, d_latent))
    d_first = dots("bnt,dn->btd", dq_t, w["query"]) + dots("btl,dl->btd", d_latent, w["latent"])
    d_first = chip_sum(p, d_first.reshape(batch, 2, length, D))
    own = tokens.astype(F32)
    inverse1 = inverse_rms(own)
    normed1 = own * inverse1
    gain1_sum = jnp.sum(d_first * normed1, axis=(0, 1))
    grad_tokens = d_middle + norm_back(d_first, normed1, inverse1, gain1)
    return (
        layer_out, grad_tokens, ways.gain(gain1_sum), grad_query, grad_latent,
        ways.rows(d_key_t).T, ways.rows(d_value_t).T, grad_output, ways.gain(gain2_sum),
        grad_gate, grad_up, grad_down,
    )


class Live:
    def __init__(self, values):
        self.__dict__.update(values)

    @property
    def pop(self):
        return Taken(self)


class Taken:
    def __init__(self, live):
        self.live = live

    def __getattr__(self, name):
        return self.live.__dict__.pop(name)


def sync(v):
    return Live(lax.optimization_barrier(dict(v.__dict__)))


def in_z(p, seen):
    out = []
    for z in range(4):
        back = (p.z - z) % 4
        pair = [jnp.where(back % 2 == 0, seen[k], seen[k + 1]) for k in (0, 2)]
        out.append(jnp.where(back < 2, pair[0], pair[1]))
    return jnp.stack(out)


def z_scatter(p, parts):
    total = half(parts, p.z, 0, 4)[0].astype(F32)
    for k in (1, 2, 3):
        total = total + p.to_z(half(parts, (p.z + k) % 4, 0, 4), k)[0].astype(F32)
    return total.astype(LOW)


def summed(p, make):
    come = p.to_core(make(1).astype(LOW))
    return make(0) + come.astype(F32)


def core_first(p, own):
    return jnp.concatenate([own, p.to_core(own)], 0)


def to_xy(p, value):
    return p.send(value, lambda s, d: (s ^ 2, d ^ 1))


def add_all(parts):
    return sum(part.astype(F32) for part in parts).astype(LOW)


def place_kernel(plan, sources, outs, where, *refs):
    src, dst = refs[:sources], refs[sources:]
    spot = where[0], where[1], where[2]
    for make in plan:
        source, there, out, here = make(*spot)
        if isinstance(source, int):
            dst[out][here] = src[source][there].astype(LOW)
            continue
        flag, sides = source[0], source[1:]
        for value in range(2):

            @pl.when(flag == value)
            def _(side=sides[value], there=there, out=out, here=here):
                dst[out][here] = src[side][there].astype(LOW)


def placed(p, plan, sources, shapes):
    where = jnp.stack([p.x, p.y, p.core]).astype(jnp.int32)
    inside = pl.BlockSpec(memory_space=pltpu.VMEM)
    return pl.pallas_call(
        lambda *refs: place_kernel(plan, len(sources), len(shapes), *refs),
        in_specs=[pl.BlockSpec(memory_space=pltpu.SMEM)] + [inside] * len(sources),
        out_specs=[inside] * len(shapes),
        out_shape=[jax.ShapeDtypeStruct(shape, LOW) for shape in shapes],
        compiler_params=pltpu.CompilerParams(vmem_limit_bytes=VMEM_LIMIT),
        name="place",
    )(where, *sources)


def lanes(start, width):
    return pl.ds(pl.multiple_of(start, 128), width)


RELATIVE = [(0, 0), (1, 0), (0, 1), (1, 1)]


def spread(p, parts):
    return parts[0], p.to_x(parts[1]), p.to_y(parts[2]), to_xy(p, parts[3])


def square_layer(
    p, tokens, attn_gain, query_weight, latent_weight, key_expand, value_expand, output_weight,
    mlp_gain, gate_weight, up_weight, down_weight, cotangent, lengths,
):
    batch, length, _ = tokens.shape
    count = 2 * batch * length
    core, x, y = p.core, p.x, p.y
    ff = gate_weight.shape[1] // 2
    quarter = 2 * core + y
    v = Live({})

    def cols(value, parts, index):
        return half(value, index, 1, parts).astype(LOW)

    def x_own(value):
        return half(value, x, 1)

    def x_other(value):
        return half(value, 1 - x, 1)

    v.pgu = jnp.concatenate([cols(gate_weight, 2, core), cols(up_weight, 2, core)], 1)
    v.tok = p.to_core(tokens)
    v = sync(v)
    kv = half(pick(y, key_expand, value_expand), core, 0).astype(LOW).T
    gains = jnp.stack([attn_gain, mlp_gain] + [jnp.zeros_like(attn_gain)] * 6).astype(LOW)
    piece = [
        cols(latent_weight, 4, quarter), cols(output_weight, 4, quarter),
        cols(query_weight, 4, quarter), kv,
    ]
    piece = jnp.concatenate(piece, 1)
    pad = jnp.zeros((8, piece.shape[1] - 128), LOW)
    piece = jnp.concatenate([piece, jnp.concatenate([gains, pad], 1)], 0)
    seen = [piece] + [p.to_z(piece, k) for k in (1, 2, 3)]
    w_gu = after(v.pop.pgu, seen[1])
    w_gu = lax.all_gather(w_gu, "dp", axis=0, tiled=True)
    first = in_z(p, seen)
    v.a, v.b = first[:, :, :384], first[:, :, 384:]
    rows = jnp.stack([tokens, v.pop.tok], 1).astype(F32)
    v.normed1 = rows * inverse_rms(rows)
    v.pd = cols(down_weight, 4, quarter)
    v = sync(v)

    v.ax, v.by = p.to_x(v.a), p.to_y(v.b)
    v = sync(v)
    v.zd2 = p.to_z(v.pd, 2)
    v.ay, v.axy = p.to_y(v.a), p.to_y(v.ax)
    v.bx, v.bxy = p.to_x(v.b), p.to_x(v.by)
    v = sync(v)

    v.zd1, v.zd3 = p.to_z(v.pd, 1), p.to_z(v.pd, 3)
    v.from_ab = (v.pop.a, v.pop.ax, v.pop.ay, v.pop.axy, v.pop.b, v.pop.bx, v.pop.by, v.pop.bxy)
    plan = []
    for n, (r, k) in enumerate(RELATIVE):
        low = pl.ds(0, 128)
        plan += [
            lambda x, y, c, n=n, r=r, k=k: (
                n, (slice(None), low, pl.ds(0, 128)), 0,
                (slice(None), x ^ r, slice(None), lanes((y ^ k) * 128, 128)),
            ),
            lambda x, y, c, n=n, r=r, k=k: (
                4 + n, (slice(None), low, pl.ds(0, 256)), 1,
                (slice(None), x ^ r, slice(None), lanes((y ^ k) * 256, 256)),
            ),
            lambda x, y, c, n=n: (n, (pl.ds(2 * (1 - c), 2), low, pl.ds(128, 256)), 2, n),
            lambda x, y, c, n=n: (4 + n, (pl.ds(2 * (1 - c), 2), low, pl.ds(256, 128)), 3, n),
        ]
    wl, wq, v.wo_send, v.kv_send = placed(
        p, plan, v.from_ab,
        [(4, 2, 128, LAT), (4, 2, 128, GW), (4, 2, 128, 256), (4, 2, 128, 128)],
    )
    v.wl, v.wq = wl.reshape(D, LAT), wq.reshape(D, GW)
    gains = [part[:, 128:130, :128] for part in v.from_ab[:2]]
    gains = pick(x, jnp.stack(gains, 2), jnp.stack(gains[::-1], 2)).astype(F32)
    v.gain1, v.gain2 = gains[:, 0].reshape(D), gains[:, 1].reshape(D)
    v.first = (v.pop.normed1 * v.gain1).astype(LOW).reshape(batch, 2 * length, D)
    v.keys = dots("btd,dl->btl", v.first, v.wl).astype(LOW).reshape(batch, 2, length, LAT)
    v = sync(v)
    far_keys = p.up_y(v.keys)
    wo_come, kv_come = p.to_core(v.pop.wo_send), p.to_core(v.pop.kv_send)
    v.zd = in_z(p, [v.pop.pd, v.pop.zd1, v.pop.zd2, v.pop.zd3])
    v.dax, v.dby = p.to_x(v.zd[:2]), p.to_y(v.zd[2:])
    v.qt = dots("dn,btd->bnt", v.wq, v.first).astype(LOW)
    plan = []
    for n, (r, k) in enumerate(RELATIVE):
        for s in range(2):
            plan += [
                lambda x, y, c, n=n, r=r, k=k, s=s: (
                    (n, (pl.ds(2 * c, 2), pl.ds(0, 128), pl.ds(128, 256))) if s == 0 else (8, n)
                ) + (0, (slice(None), x ^ r, slice(None), lanes(((c ^ s) * 2 + (y ^ k)) * 256, 256))),
                lambda x, y, c, n=n, r=r, k=k, s=s: (
                    (4 + n, (pl.ds(2 * c, 2), pl.ds(0, 128), pl.ds(256, 128))) if s == 0 else (9, n)
                ) + (1, (y ^ k, slice(None), x ^ r, slice(None), lanes((c ^ s) * 128, 128))),
            ]
    wo, kv = placed(
        p, plan, (*v.pop.from_ab, wo_come, kv_come), [(2, 2, 128, D), (2, 2, 2, 128, LAT)]
    )
    v.wo, kv = wo.reshape(GW, D), kv.reshape(2, GW, LAT)
    v.kxt, v.vxt = kv[0], kv[1]
    starts = jnp.stack([core, 1 - core]).astype(jnp.int32) * length
    base = p.chip * 2 * length
    far = pick(p.chip, 2 * length, 0)
    meta = [base + starts, far + starts, base + starts, lengths[:, 0], jnp.zeros((1,), jnp.int32)]
    v.meta = jnp.concatenate(meta).astype(jnp.int32)
    v.keys = jnp.concatenate([v.keys, far_keys], axis=1)
    v = sync(v)

    v.cot = core_first(p, cotangent.reshape(count // 2, D))
    v.day, v.daxy = p.to_y(v.zd[:2]), p.to_y(v.dax)
    v.dbx, v.dbxy = p.to_x(v.zd[2:]), p.to_x(v.dby)
    cot = half(v.cot, core, 1)
    v.cot_c = [half(cot, i, 1) for i in (y, 1 - y)] + [half(v.cot, 1 - core, 1)]
    v.out, *v.att = attention_forward(v.meta, v.qt, v.kxt, v.vxt, v.keys)
    v = sync(v)

    branch = summed(
        p, lambda i: dots("bnt,nd->btd", v.out[:, :, i * length : (i + 1) * length], v.wo)
    )
    v.middle = tokens.astype(F32) + branch
    v.inv2 = inverse_rms(v.middle)
    second = v.middle * v.inv2 * v.gain2
    v.second = core_first(p, second.astype(LOW).reshape(count // 2, D))
    v = sync(v)

    front, back = v.zd[:2], v.pop.zd[2:]
    sides = (front, v.pop.dax, v.pop.day, v.pop.daxy, back, v.pop.dbx, v.pop.dby, v.pop.dbxy)
    whole = slice(None)
    plan = [lambda x, y, c, n=n: ((c, 4 + n, n), whole, 0, n) for n in range(4)]
    v.come = p.to_core(placed(p, plan, sides, [(4, 2, ff // 4, 256)])[0])
    v.sides = sides
    v.w_gu = w_gu
    v.act, v.hidden = feed_forward(v.second, v.w_gu)
    v = sync(v)
    plan = []
    for n, (r, k) in enumerate(RELATIVE):
        for s in range(2):
            plan += [
                lambda x, y, c, n=n, r=r, k=k, s=s: (
                    ((c, n, 4 + n), whole) if s == 0 else (8, n)
                ) + (
                    0, (whole, x ^ r, whole, lanes(((c ^ s) * 2 + (y ^ k)) * 256, 256)),
                )
            ]
    wd = placed(p, plan, (*v.pop.sides, v.pop.come), [(2, 2, ff // 4, D)])[0]
    v.wd = wd.reshape(ff, D)

    v.d_gu, v.ds_own, v.ds_other = feed_forward_back(v.cot, v.wd, v.pop.w_gu, v.pop.act)
    v = sync(v)
    d_second = (v.pop.ds_own + p.to_core(v.pop.ds_other).astype(F32)).reshape(batch, length, D)
    gg = tn(v.pop.second, v.pop.d_gu).astype(LOW)
    gg = lax.psum_scatter(gg, "dp", scatter_dimension=0, tiled=True)
    normed2 = v.middle * v.inv2
    v.gain2_sum = jnp.sum(d_second * normed2, axis=(0, 1))
    v.d_middle = cotangent.astype(F32) + norm_back(d_second, normed2, v.pop.inv2, v.pop.gain2)
    v.d_a = chip(p, v.d_middle.astype(LOW)).reshape(batch, 2 * length, D)
    v = sync(v)
    go = dots("bnt,btd->nd", v.pop.out, v.d_a).astype(LOW).reshape(2, 2, 128, D)
    go_core = half(go, core, 3)
    go_parts = [half(go_core, y, 3), half(go_core, 1 - y, 3), half(go, 1 - core, 3)]
    gd_parts = [tn(v.hidden, part).astype(LOW) for part in v.pop.cot_c]
    v.r_a, v.r_ay, r_send = [
        jnp.concatenate([gd.reshape(2, 2, -1, gd.shape[-1]), go], 2)
        for gd, go in zip(gd_parts, go_parts)
    ]
    v.r_b = p.to_core(r_send)
    v.dot = dots("nd,btd->bnt", v.pop.wo, v.pop.d_a).astype(LOW)
    v = sync(v)

    full = slice(None)
    rows = count // 2
    branch = summed(p, lambda i: mm(v.hidden[i * rows : (i + 1) * rows], v.wd))
    v.out_done = (v.pop.middle + branch.reshape(batch, length, D)).astype(LOW)
    del v.hidden, v.wd
    v.r_ay, v.r_bx = p.to_y(v.r_ay), p.to_x(x_other(v.r_b))
    v.back0 = attention_backward(
        0, v.meta, v.qt, v.dot, *v.att, v.kxt, v.vxt, v.keys, ()
    )
    v = sync(v)
    layer_out = v.pop.out_done
    v.r_a = add_low(v.r_a, v.pop.r_ay)
    v.r_b = add_low(x_own(v.r_b), v.pop.r_bx)
    v.r_ax, v.r_by = p.to_x(x_other(v.r_a)), p.to_y(half(v.r_b, 1 - y, 3))
    d_keys = v.back0[1]
    v.dk0, v.dk_far0 = d_keys[:2], p.down_y(d_keys[2:].astype(LOW))
    v.back1 = attention_backward(
        1, v.meta, v.qt, v.dot, *v.att, v.kxt, v.vxt, v.keys, v.back0[2:]
    )
    v = sync(v)

    back0, back1 = v.pop.back0, v.pop.back1
    v.far1 = p.down_y(back1[1][2:].astype(LOW))
    v.dk1 = back1[1][:2]
    v.dk0 = (v.dk0 + v.pop.dk_far0.astype(F32)).astype(LOW).reshape(1, 2 * length, LAT)
    plan = []
    for n in range(2):
        for s in range(2):
            plan += [
                lambda x, y, c, n=n, s=s: (n, (slice(None), lanes((c ^ s) * 128, 128)), s, n)
            ]
    v.kv_mine, kv_send = placed(p, plan, back1[2:], [(2, GW, 128)] * 2)
    v.kv_come = p.to_core(kv_send)
    r_a = add_low(x_own(v.pop.r_a), v.pop.r_ax)[:, 0]
    r_b = add_low(half(v.pop.r_b, y, 3), v.pop.r_by)[:, 0]
    v.r = ordered(core, r_a, r_b, 0)

    def r_step(k):
        return p.to_z(half(v.r, (p.z + k) % 4, 0, 4), k)

    v.dq_t = jnp.stack([back0[0], back1[0]])
    v.gq = dots("btd,bnt->dn", v.first, v.dq_t).astype(LOW).reshape(4, 2, 128, GW)
    v = sync(v)
    v.r1, v.r2, v.r3 = r_step(1), r_step(2), r_step(3)
    dk1 = (v.pop.dk1 + v.pop.far1.astype(F32)).astype(LOW).reshape(1, 2 * length, LAT)
    d_latent = jnp.concatenate([v.pop.dk0, dk1])
    gl = dots("btd,btl->dl", v.pop.first, d_latent).astype(LOW).reshape(4, 2, 128, LAT)
    plan = []
    for n, (r, k) in enumerate(RELATIVE):
        plan += [
            lambda x, y, c, n=n, r=r, k=k: (
                0, (full, x ^ r, full, lanes((y ^ k) * 256, 256)), n, (full, full, pl.ds(0, 256)),
            ),
            lambda x, y, c, n=n, r=r, k=k: (
                1, (full, x ^ r, full, lanes((y ^ k) * 128, 128)), n, (full, full, pl.ds(384, 128)),
            ),
        ]
        for s in range(2):
            plan += [
                lambda x, y, c, n=n, r=r, k=k, s=s: (
                    2 + s, (y ^ k, full, x ^ r), n, (pl.ds(2 * (c ^ s), 2), full, pl.ds(256, 128)),
                )
            ]
    kv = [part.reshape(2, 2, 2, 128, 128) for part in (v.pop.kv_mine, v.pop.kv_come)]
    v.found = spread(p, placed(p, plan, (v.pop.gq, gl, *kv), [(4, 128, 512)] * 4))
    dq_t = v.pop.dq_t

    def first_grad(i):
        part = slice(i * length, (i + 1) * length)
        by_q = dots("bnt,dn->btd", dq_t[:, :, part], v.wq)
        return by_q + dots("btl,dl->btd", d_latent[:, part], v.wl)

    d_first = summed(p, first_grad)
    own = tokens.astype(F32)
    inverse1 = inverse_rms(own)
    normed1 = own * inverse1
    gains = jnp.stack([jnp.sum(d_first * normed1, axis=(0, 1)), v.pop.gain2_sum])
    v.gains = gains.astype(LOW).reshape(2, 4, 2, 128)
    v.tokens_done = v.d_middle + norm_back(d_first, normed1, inverse1, v.gain1)
    v = sync(v)
    grad_tokens = v.pop.tokens_done
    v.r = add_all([half(v.r, p.z, 0, 4), v.pop.r1, v.pop.r2, v.pop.r3])[0]
    gains = jnp.moveaxis(v.pop.gains, 0, 1).reshape(4, 4, 128)
    gains = jnp.pad(gains, ((0, 0), (0, 4), (0, 384)))
    v.q = z_scatter(p, jnp.concatenate([add_all(v.pop.found), gains], 1))
    v.gg = gg
    v.gg = add_low(v.gg, p.to_y(v.gg))
    v = sync(v)
    v.q1 = p.to_y(v.q)
    v.gg1, v.r1 = p.to_core(v.gg), p.to_y(v.r)
    v = sync(v)
    grad_gate = ordered(core, v.gg[:, :ff], v.gg1[:, :ff], 1).astype(F32)
    grad_up = ordered(core, v.gg[:, ff:], v.gg1[:, ff:], 1).astype(F32)
    r = ordered(y, v.r, v.r1, 1)
    grad_rows = ordered(core, r, p.to_core(r), 1).astype(F32)
    grad_down, grad_output = grad_rows[: ff // 4], grad_rows[ff // 4 :]
    gains = add_low(v.q[128:132, :128], v.q1[128:132, :128])
    x_gains = p.to_x(gains)
    q0, q1 = pick(y, v.q, v.q1), pick(y, v.q1, v.q)
    mine = jnp.concatenate([q0, q1], 1)
    mine = lax.dynamic_update_slice(mine, gains, (128, 0))
    other = p.to_core(mine)
    x_other_gains = p.send(gains, lambda s, d: (s ^ 1, d ^ 1))
    zero, one = pick(core, mine, other), pick(core, other, mine)

    def columns(start, width):
        found = [part[:128, i : i + width] for part in (zero, one) for i in (start, start + 512)]
        return jnp.concatenate(found, 1).astype(F32)

    def expand_grad(start):
        return jnp.concatenate([p_[:128, start : start + 128] for p_ in (zero, one)], 1)

    near_gains = pick(x, gains, x_gains).astype(F32) + pick(x, x_gains, gains).astype(F32)
    far = other[128:132, :128]
    far_gains = pick(x, far, x_other_gains).astype(F32) + pick(x, x_other_gains, far).astype(F32)
    gains = half((near_gains + far_gains).reshape(2, 2, 128), x, 1)[:, 0]
    return (
        layer_out, grad_tokens, gains[0], columns(0, 256), columns(384, 128),
        expand_grad(256).T.astype(F32), expand_grad(768).T.astype(F32), grad_output, gains[1],
        grad_gate, grad_up, grad_down,
    )


def per_device(*arguments):
    p = Place()
    return (square_layer if p.square else plain_layer)(p, *arguments)


def solution(mesh):
    rows, gain, weight, across = P("dp", "seq", None), P("dp"), P("dp", None), P(None, "dp")
    return jax.shard_map(
        per_device,
        mesh=mesh,
        in_specs=(
            rows, gain, weight, weight, across, across, weight, gain, weight, weight, weight, rows,
            P("dp", None),
        ),
        out_specs=(
            rows, rows, gain, weight, weight, across, across, weight, gain, weight, weight, weight,
        ),
        check_vma=False,
    )
```

```python
import jax
import jax.numpy as jnp
from jax import lax
from jax.experimental import pallas as pl
from jax.experimental.pallas import tpu as pltpu
from jax.sharding import PartitionSpec as P

D = 1024
H = 16
HD = 64
KVH = 2
LAT = 256
GH = H // KVH
GW = D // KVH
EPS = 1e-06
SCALE = HD ** (-0.5)
LOG2E = 1.4426950408889634
NEG = -1e30

LOW = jnp.bfloat16
F32 = jnp.float32
ALL = ("seq", "dp")
VMEM_LIMIT = 56 * 1024 * 1024


def mm(left, right):
    return jnp.dot(left, right, preferred_element_type=F32)


def tn(left, right):
    return lax.dot_general(left, right, (((0,), (0,)), ((), ())), preferred_element_type=F32)


def nt(left, right):
    return lax.dot_general(left, right, (((1,), (1,)), ((), ())), preferred_element_type=F32)


def block_bias(k0, q0, first, width):
    kpos = k0 + lax.broadcasted_iota(jnp.int32, (width, width), 0)
    qpos = q0 + lax.broadcasted_iota(jnp.int32, (width, width), 1)
    lowest = jnp.where(qpos >= first, first, 0)
    return jnp.where((kpos <= qpos) & (kpos >= lowest), 0.0, NEG)


def block_needed(k0, q0, first, width):
    before = jnp.logical_and(q0 >= first, k0 + (width - 1) < first)
    return jnp.logical_and(k0 <= q0, jnp.logical_not(before))


def forward_kernel(nkb, batch, width, meta, qt, kxt, vxt, c, o_low, o_full, mix_out, lse_out, q_s, acc, m_s, l_s, p_s):
    b, qb = pl.program_id(0), pl.program_id(1)
    q0, first, diag = meta[nkb + qb], meta[nkb + 2 + b], meta[nkb + 2 + batch] + qb
    for h in range(GH):
        cols = slice(h * width, (h + 1) * width)
        rows = slice(h * HD, (h + 1) * HD)
        q_s[:, cols] = (tn(kxt[rows, :], qt[0, rows, :]) * (SCALE * LOG2E)).astype(LOW)
    m_s[...] = jnp.full_like(m_s, NEG)
    l_s[...] = jnp.zeros_like(l_s)
    acc[...] = jnp.zeros_like(acc)

    def step(j, carry):
        kb = lax.rem(diag + j, nkb)
        k0 = meta[kb]

        @pl.when(block_needed(k0, q0, first, width))
        def _():
            bias = block_bias(k0, q0, first, width)
            keys = c[0, kb]
            keys_t = keys.T
            alphas = []
            for h in range(GH):
                cols = slice(h * width, (h + 1) * width)
                s = mm(keys, q_s[:, cols]) + bias
                m_old = m_s[:, cols]
                m_new = jnp.maximum(m_old, jnp.max(s, axis=0, keepdims=True))
                p = jnp.exp2(s - m_new)
                alpha = jnp.exp2(m_old - m_new)
                m_s[:, cols] = m_new
                l_s[:, cols] = l_s[:, cols] * alpha + jnp.sum(p, axis=0, keepdims=True)
                p_s[:, cols] = p.astype(LOW)
                alphas.append(alpha)
            acc[...] = acc[...] * jnp.concatenate(alphas, 1) + mm(keys_t, p_s[...])

        return carry

    lax.fori_loop(0, nkb, step, 0)
    for h in range(GH):
        cols = slice(h * width, (h + 1) * width)
        rows = slice(h * HD, (h + 1) * HD)
        total = l_s[:, cols]
        mixed = (acc[:, cols] * (1.0 / total)).astype(LOW)
        mix_out[0, 0, :, cols] = mixed
        out = mm(vxt[rows, :], mixed)
        o_full[0, rows, :] = out
        o_low[0, rows, :] = out.astype(LOW)
        lse_out[0, 0, :, cols] = m_s[:, cols] + jnp.log(total) * LOG2E


def backward_kernel(
    b, nkb, batch, width, add_dw, meta, qt, dot_, o_full, mix, lse, kxt, vxt, c, *refs
):
    refs = list(refs)
    dk_old, dv_old = (refs.pop(0), refs.pop(0)) if add_dw else (None, None)
    dqt, dc, dkxt, dvxt, q_s, do_t, delta, dq, ds_s, p_s = refs
    qb = pl.program_id(0)
    q0, first, diag = meta[nkb + qb], meta[nkb + 2 + b], meta[nkb + 2 + batch] + qb

    @pl.when(qb == 0)
    def _():
        dc[...] = jnp.zeros_like(dc)
        dkxt[...] = dk_old[...] if add_dw else jnp.zeros_like(dkxt)
        dvxt[...] = dv_old[...] if add_dw else jnp.zeros_like(dvxt)


    for h in range(GH):
        cols = slice(h * width, (h + 1) * width)
        rows = slice(h * HD, (h + 1) * HD)
        qh, kh, doh, vh = qt[0, rows, :], kxt[rows, :], dot_[0, rows, :], vxt[rows, :]
        q_s[:, cols] = (tn(kh, qh) * (SCALE * LOG2E)).astype(LOW)
        do_t[:, cols] = tn(vh, doh).astype(LOW)
        delta[:, cols] = jnp.sum(doh.astype(F32) * o_full[0, rows, :], axis=0, keepdims=True)
    dq[...] = jnp.zeros_like(dq)

    def step(j, carry):
        kb = lax.rem(diag + j, nkb)
        k0 = meta[kb]

        @pl.when(block_needed(k0, q0, first, width))
        def _():
            bias = block_bias(k0, q0, first, width)
            keys = c[0, kb]
            keys_t = keys.T
            for h in range(GH):
                cols = slice(h * width, (h + 1) * width)
                s = mm(keys, q_s[:, cols]) + bias
                p = jnp.exp2(s - lse[0, 0, :, cols])
                dp = mm(keys, do_t[:, cols])
                ds = (p * (dp - delta[:, cols])).astype(LOW)
                p_s[:, cols] = p.astype(LOW)
                ds_s[:, cols] = ds
            dq[...] += mm(keys_t, ds_s[...])
            dc[kb] += nt(ds_s[...], q_s[...]) * (1.0 / LOG2E) + nt(p_s[...], do_t[...])

        return carry

    lax.fori_loop(0, nkb, step, 0)
    for h in range(GH):
        cols = slice(h * width, (h + 1) * width)
        rows = slice(h * HD, (h + 1) * HD)
        dq_low = (dq[:, cols] * SCALE).astype(LOW)
        dqt[rows, :] = mm(kxt[rows, :], dq_low).astype(LOW)
        dkxt[rows, :] += nt(qt[0, rows, :], dq_low)
        dvxt[rows, :] += nt(dot_[0, rows, :], mix[0, 0, :, cols])


def attention_forward(meta, qt, kxt, vxt, c):
    batch, nkb, width, _ = c.shape
    wide = GH * width
    pairs = batch * 7 * GH * width * width * LAT
    expand = pl.BlockSpec((GW, LAT), lambda b, q: (0, 0))
    q_spec = pl.BlockSpec((1, GW, width), lambda b, q: (b, 0, q))
    return pl.pallas_call(
        lambda *refs: forward_kernel(nkb, batch, width, *refs),
        grid=(batch, 2),
        in_specs=[
            pl.BlockSpec(memory_space=pltpu.SMEM),
            q_spec,
            expand,
            expand,
            pl.BlockSpec((1, nkb, width, LAT), lambda b, q: (b, 0, 0, 0)),
        ],
        out_specs=[
            q_spec,
            q_spec,
            pl.BlockSpec((1, 1, LAT, wide), lambda b, q: (b, q, 0, 0)),
            pl.BlockSpec((1, 1, 1, wide), lambda b, q: (b, q, 0, 0)),
        ],
        out_shape=[
            jax.ShapeDtypeStruct(qt.shape, LOW),
            jax.ShapeDtypeStruct(qt.shape, F32),
            jax.ShapeDtypeStruct((batch, 2, LAT, wide), LOW),
            jax.ShapeDtypeStruct((batch, 2, 1, wide), F32),
        ],
        scratch_shapes=[
            pltpu.VMEM((LAT, wide), LOW),
            pltpu.VMEM((LAT, wide), F32),
            pltpu.VMEM((1, wide), F32),
            pltpu.VMEM((1, wide), F32),
            pltpu.VMEM((width, wide), LOW),
        ],
        compiler_params=pltpu.CompilerParams(
            dimension_semantics=("arbitrary", "arbitrary"), vmem_limit_bytes=VMEM_LIMIT
        ),
        cost_estimate=pl.CostEstimate(
            flops=4 * pairs, bytes_accessed=16 << 20, transcendentals=batch * 7 * GH * width * width
        ),
        name="attention_forward",
    )(meta, qt, kxt, vxt, c)


def attention_backward(b, meta, qt, dot_, o_full, mix, lse, kxt, vxt, c, old_dw):
    batch, nkb, width, _ = c.shape
    wide = GH * width
    pairs = 7 * GH * width * width * LAT * 2
    expand = pl.BlockSpec((GW, LAT), lambda q: (0, 0))
    return pl.pallas_call(
        lambda *refs: backward_kernel(b, nkb, batch, width, bool(old_dw), *refs),
        grid=(2,),
        in_specs=[
            pl.BlockSpec(memory_space=pltpu.SMEM),
            pl.BlockSpec((1, GW, width), lambda q: (b, 0, q)),
            pl.BlockSpec((1, GW, width), lambda q: (b, 0, q)),
            pl.BlockSpec((1, GW, width), lambda q: (b, 0, q)),
            pl.BlockSpec((1, 1, LAT, wide), lambda q: (b, q, 0, 0)),
            pl.BlockSpec((1, 1, 1, wide), lambda q: (b, q, 0, 0)),
            expand,
            expand,
            pl.BlockSpec((1, nkb, width, LAT), lambda q: (b, 0, 0, 0)),
        ]
        + [expand] * len(old_dw),
        out_specs=[
            pl.BlockSpec((GW, width), lambda q: (0, q)),
            pl.BlockSpec((nkb, width, LAT), lambda q: (0, 0, 0)),
            expand,
            expand,
        ],
        out_shape=[
            jax.ShapeDtypeStruct((GW, 2 * width), LOW),
            jax.ShapeDtypeStruct((nkb, width, LAT), F32),
            jax.ShapeDtypeStruct(kxt.shape, F32),
            jax.ShapeDtypeStruct(vxt.shape, F32),
        ],
        scratch_shapes=[
            pltpu.VMEM((LAT, wide), LOW),
            pltpu.VMEM((LAT, wide), LOW),
            pltpu.VMEM((1, wide), F32),
            pltpu.VMEM((LAT, wide), F32),
            pltpu.VMEM((width, wide), LOW),
            pltpu.VMEM((width, wide), LOW),
        ],
        compiler_params=pltpu.CompilerParams(
            dimension_semantics=("arbitrary",), vmem_limit_bytes=VMEM_LIMIT
        ),
        cost_estimate=pl.CostEstimate(
            flops=5 * pairs, bytes_accessed=10 << 20, transcendentals=7 * GH * width * width
        ),
        name="attention_backward",
    )(meta, qt, dot_, o_full, mix, lse, kxt, vxt, c, *old_dw)


def hidden_kernel(x, w, act, hidden):
    width = hidden.shape[1]
    both = mm(x[...], w[...])
    act[...] = both
    gate, up = both[:, :width], both[:, width:]
    hidden[...] = (gate * jax.nn.sigmoid(gate) * up).astype(LOW)


def hidden_back_kernel(cot, down, w, act, grad, own, other):
    width = down.shape[0]
    d_hidden = nt(cot[...], down[...])
    gate, up = act[:, :width], act[:, width:]
    sig = jax.nn.sigmoid(gate)
    grad[:, :width] = (d_hidden * up * sig * (1.0 + gate * (1.0 - sig))).astype(LOW)
    grad[:, width:] = (d_hidden * (gate * sig)).astype(LOW)
    back = nt(grad[...], w[...])
    mine = pl.program_id(0) < pl.num_programs(0) // 2

    @pl.when(mine)
    def _():
        own[...] = back

    @pl.when(jnp.logical_not(mine))
    def _():
        other[...] = back.astype(LOW)


TILE = 256


def tiled(width):
    return pl.BlockSpec((TILE, width), lambda i: (i, 0))


def resident(shape):
    return pl.BlockSpec(shape, lambda i: (0, 0), pipeline_mode=pl.Buffered(1))


def feed_forward(x, w):
    count, both = x.shape[0], w.shape[1]
    return pl.pallas_call(
        hidden_kernel,
        grid=(count // TILE,),
        in_specs=[tiled(x.shape[1]), resident(w.shape)],
        out_specs=[tiled(both), tiled(both // 2)],
        out_shape=[
            jax.ShapeDtypeStruct((count, both), F32),
            jax.ShapeDtypeStruct((count, both // 2), LOW),
        ],
        compiler_params=pltpu.CompilerParams(vmem_limit_bytes=VMEM_LIMIT),
        cost_estimate=pl.CostEstimate(
            flops=2 * x.size * both, bytes_accessed=20 << 20, transcendentals=count * both // 2
        ),
        name="feed_forward",
    )(x, w)


def feed_forward_back(cot, down, w, act):
    count, both = act.shape
    width, steps = w.shape[0], count // TILE
    return pl.pallas_call(
        hidden_back_kernel,
        grid=(steps,),
        in_specs=[tiled(cot.shape[1]), resident(down.shape), resident(w.shape), tiled(both)],
        out_specs=[
            tiled(both),
            pl.BlockSpec((TILE, width), lambda i: (jnp.minimum(i, steps // 2 - 1), 0)),
            pl.BlockSpec((TILE, width), lambda i: (jnp.maximum(i - steps // 2, 0), 0)),
        ],
        out_shape=[
            jax.ShapeDtypeStruct((count, both), LOW),
            jax.ShapeDtypeStruct((count // 2, width), F32),
            jax.ShapeDtypeStruct((count // 2, width), LOW),
        ],
        compiler_params=pltpu.CompilerParams(vmem_limit_bytes=VMEM_LIMIT),
        cost_estimate=pl.CostEstimate(
            flops=3 * cot.size * both, bytes_accessed=30 << 20, transcendentals=count * both // 2
        ),
        name="feed_forward_back",
    )(cot, down, w, act)


class Place:
    def __init__(self):
        self.seq, self.dp = lax.axis_size("seq"), lax.axis_size("dp")
        s, d = lax.axis_index("seq"), lax.axis_index("dp")
        self.core, self.chip = s % 2, s // 2
        self.y, self.x, self.z = s // 2, d % 2, d // 2
        self.square = self.seq == 4 and self.dp == 8

    def pairs(self, move):
        found = []
        for s in range(self.seq):
            for d in range(self.dp):
                target = move(s, d)
                if target is not None:
                    found.append((s * self.dp + d, target[0] * self.dp + target[1]))
        return found

    def send(self, value, move):
        return lax.ppermute(value, ALL, self.pairs(move))

    def to_core(self, value):
        return self.send(value, lambda s, d: (s ^ 1, d))

    def to_y(self, value):
        return self.send(value, lambda s, d: (s ^ 2, d))

    def to_x(self, value):
        return self.send(value, lambda s, d: (s, d ^ 1))

    def to_z(self, value, step):
        return self.send(value, lambda s, d: (s, (d + 2 * step) % 8))

    def up_y(self, value):
        return self.send(value, lambda s, d: (s + 2, d) if s < 2 else None)

    def down_y(self, value):
        return self.send(value, lambda s, d: (s - 2, d) if s >= 2 else None)


def half(value, index, axis, count=2):
    size = value.shape[axis] // count
    return lax.dynamic_slice_in_dim(value, index * size, size, axis)


def ordered(flag, own, other, axis):
    return jnp.where(
        flag == 0, jnp.concatenate([own, other], axis), jnp.concatenate([other, own], axis)
    )


def after(value, *others):
    return lax.optimization_barrier((value, others))[0]


def add_low(own, other):
    return (own.astype(F32) + other.astype(F32)).astype(LOW)


class Plain:
    def __init__(self, place):
        self.p = place
        count = place.seq // 2
        self.same_core = [[2 * i + c for i in range(count)] for c in range(2)]
        self.chip = [[2 * i, 2 * i + 1] for i in range(count)]

    def gather(self, w):
        core = self.p.core

        def full(value, axis=0):
            return lax.all_gather(value.astype(LOW), "dp", axis=axis, tiled=True)

        out = {name: full(half(w[name], core, 1)) for name in ("query", "latent", "gate", "up")}
        out["key_t"] = half(full(w["key"].T), core, 0)
        out["value_t"] = half(full(w["value"].T), core, 0)
        out["output"] = half(full(w["output"]), core, 0)
        out["down"] = half(full(w["down"]), core, 0)
        out["gain1"], out["gain2"] = full(w["gain1"]), full(w["gain2"])
        return out

    def columns(self, grad):
        share = lax.psum_scatter(grad.astype(LOW), "dp", scatter_dimension=0, tiled=True)
        share = lax.psum(share, "seq", axis_index_groups=self.same_core)
        return lax.all_gather(
            share, "seq", axis=1, tiled=True, axis_index_groups=self.chip
        ).astype(F32)

    def rows(self, grad):
        grad = grad.astype(LOW)
        grad = ordered(self.p.core, grad, jnp.zeros_like(grad), 0)
        share = lax.psum_scatter(grad, "dp", scatter_dimension=0, tiled=True)
        return lax.psum(share, "seq").astype(F32)

    def gain(self, grad):
        share = lax.psum_scatter(grad.astype(LOW), "dp", scatter_dimension=0, tiled=True)
        return lax.psum(share, "seq").astype(F32)


def inverse_rms(values):
    return lax.rsqrt(jnp.mean(values * values, axis=-1, keepdims=True) + EPS)


def norm_back(grad, normed, inverse, gain):
    scaled = grad * gain
    return inverse * (scaled - normed * jnp.mean(scaled * normed, axis=-1, keepdims=True))


def dots(spec, left, right):
    return jnp.einsum(spec, left, right, preferred_element_type=F32)


def pick(flag, zero, one):
    return jnp.where(flag == 0, zero, one)


def chip(p, own):
    return jnp.stack([own, p.to_core(own)], axis=1)


def chip_sum(p, partial):
    return partial[:, 0] + p.to_core(partial[:, 1].astype(LOW)).astype(F32)


def plain_layer(
    p, tokens, attn_gain, query_weight, latent_weight, key_expand, value_expand, output_weight,
    mlp_gain, gate_weight, up_weight, down_weight, cotangent, lengths,
):
    ways = Plain(p)
    batch, length, _ = tokens.shape
    count = 2 * batch * length
    w = ways.gather(
        {
            "gain1": attn_gain, "query": query_weight, "latent": latent_weight,
            "key": key_expand, "value": value_expand, "output": output_weight,
            "gain2": mlp_gain, "gate": gate_weight, "up": up_weight, "down": down_weight,
        }
    )
    gain1, gain2 = w["gain1"].astype(F32), w["gain2"].astype(F32)
    firsts = lengths[:, 0]
    chips = p.seq // 2
    rows = chip(p, tokens).astype(F32)
    first_low = (rows * inverse_rms(rows) * gain1).astype(LOW)
    first_flat = first_low.reshape(batch, 2 * length, D)
    latent = dots("btd,dl->btl", first_flat, w["latent"]).astype(LOW)
    query_t = dots("dn,btd->bnt", w["query"], first_flat).astype(LOW)
    blocks = latent.reshape(batch, 2, length, LAT)
    starts = jnp.stack([p.core, 1 - p.core]).astype(jnp.int32) * length
    base = p.chip * 2 * length
    keys = lax.all_gather(blocks, "seq", axis=1, tiled=True, axis_index_groups=ways.same_core)
    key_starts = (
        2 * length * jnp.arange(chips, dtype=jnp.int32)[:, None] + starts[None, :]
    ).reshape(-1)
    diag = (2 * p.chip).astype(jnp.int32).reshape(1)
    meta = jnp.concatenate([key_starts, base + starts, firsts, diag]).astype(jnp.int32)
    out_low, *att = attention_forward(meta, query_t, w["key_t"], w["value_t"], keys)
    branch = dots("bnt,nd->btd", out_low, w["output"])
    middle = tokens.astype(F32) + chip_sum(p, branch.reshape(batch, 2, length, D))
    inverse2 = inverse_rms(middle)
    normed2 = middle * inverse2
    second = chip(p, (normed2 * gain2).astype(LOW)).reshape(count, D)
    cot = chip(p, cotangent).reshape(count, D)
    gate = mm(second, w["gate"])
    up = mm(second, w["up"])
    sig = jax.nn.sigmoid(gate)
    act = gate * sig
    hidden = (act * up).astype(LOW)
    partial = mm(hidden, w["down"]).reshape(batch, 2, length, D)
    layer_out = (middle + chip_sum(p, partial)).astype(LOW)
    grad_down = ways.rows(tn(hidden, cot))
    d_hidden = nt(cot, w["down"])
    d_gate = (d_hidden * up * sig * (1.0 + gate * (1.0 - sig))).astype(LOW)
    d_up = (d_hidden * act).astype(LOW)
    grad_gate, grad_up = ways.columns(tn(second, d_gate)), ways.columns(tn(second, d_up))
    partial = (nt(d_gate, w["gate"]) + nt(d_up, w["up"])).reshape(batch, 2, length, D)
    d_second = chip_sum(p, partial)
    gain2_sum = jnp.sum(d_second * normed2, axis=(0, 1))
    d_middle = cotangent.astype(F32) + norm_back(d_second, normed2, inverse2, gain2)
    d_a = chip(p, d_middle.astype(LOW)).reshape(batch, 2 * length, D)
    grad_output = ways.rows(dots("bnt,btd->nd", out_low, d_a))
    d_out_t = dots("nd,btd->bnt", w["output"], d_a).astype(LOW)
    d_queries, d_keys, sums = [], [], ()
    for b in range(batch):
        found = attention_backward(
            b, meta, query_t, d_out_t, *att, w["key_t"], w["value_t"], keys, sums
        )
        sums = found[2:]
        d_queries.append(found[0])
        d_keys.append(found[1])
    dq_t, d_keys = jnp.stack(d_queries), jnp.stack(d_keys)
    d_key_t, d_value_t = sums
    d_blocks = lax.psum_scatter(
        d_keys.astype(LOW), "seq", scatter_dimension=1, tiled=True,
        axis_index_groups=ways.same_core,
    )
    d_latent = d_blocks.astype(LOW).reshape(batch, 2 * length, LAT)
    grad_query = ways.columns(dots("btd,bnt->dn", first_flat, dq_t))
    grad_latent = ways.columns(dots("btd,btl->dl", first_flat, d_latent))
    d_first = dots("bnt,dn->btd", dq_t, w["query"]) + dots("btl,dl->btd", d_latent, w["latent"])
    d_first = chip_sum(p, d_first.reshape(batch, 2, length, D))
    own = tokens.astype(F32)
    inverse1 = inverse_rms(own)
    normed1 = own * inverse1
    gain1_sum = jnp.sum(d_first * normed1, axis=(0, 1))
    grad_tokens = d_middle + norm_back(d_first, normed1, inverse1, gain1)
    return (
        layer_out, grad_tokens, ways.gain(gain1_sum), grad_query, grad_latent,
        ways.rows(d_key_t).T, ways.rows(d_value_t).T, grad_output, ways.gain(gain2_sum),
        grad_gate, grad_up, grad_down,
    )


class Live:
    def __init__(self, values):
        self.__dict__.update(values)

    @property
    def pop(self):
        return Taken(self)


class Taken:
    def __init__(self, live):
        self.live = live

    def __getattr__(self, name):
        return self.live.__dict__.pop(name)


def sync(v):
    return Live(lax.optimization_barrier(dict(v.__dict__)))


def in_z(p, seen):
    out = []
    for z in range(4):
        back = (p.z - z) % 4
        pair = [jnp.where(back % 2 == 0, seen[k], seen[k + 1]) for k in (0, 2)]
        out.append(jnp.where(back < 2, pair[0], pair[1]))
    return jnp.stack(out)


def z_scatter(p, parts):
    total = half(parts, p.z, 0, 4)[0].astype(F32)
    for k in (1, 2, 3):
        total = total + p.to_z(half(parts, (p.z + k) % 4, 0, 4), k)[0].astype(F32)
    return total.astype(LOW)


def summed(p, make):
    come = p.to_core(make(1).astype(LOW))
    return make(0) + come.astype(F32)


def core_first(p, own):
    return jnp.concatenate([own, p.to_core(own)], 0)


def to_xy(p, value):
    return p.send(value, lambda s, d: (s ^ 2, d ^ 1))


def add_all(parts):
    return sum(part.astype(F32) for part in parts).astype(LOW)


def place_kernel(plan, sources, outs, where, *refs):
    src, dst = refs[:sources], refs[sources:]
    spot = where[0], where[1], where[2]
    for make in plan:
        source, there, out, here = make(*spot)
        if isinstance(source, int):
            dst[out][here] = src[source][there].astype(LOW)
            continue
        flag, sides = source[0], source[1:]
        for value in range(2):

            @pl.when(flag == value)
            def _(side=sides[value], there=there, out=out, here=here):
                dst[out][here] = src[side][there].astype(LOW)


def placed(p, plan, sources, shapes):
    where = jnp.stack([p.x, p.y, p.core]).astype(jnp.int32)
    inside = pl.BlockSpec(memory_space=pltpu.VMEM)
    return pl.pallas_call(
        lambda *refs: place_kernel(plan, len(sources), len(shapes), *refs),
        in_specs=[pl.BlockSpec(memory_space=pltpu.SMEM)] + [inside] * len(sources),
        out_specs=[inside] * len(shapes),
        out_shape=[jax.ShapeDtypeStruct(shape, LOW) for shape in shapes],
        compiler_params=pltpu.CompilerParams(vmem_limit_bytes=VMEM_LIMIT),
        name="place",
    )(where, *sources)


def lanes(start, width):
    return pl.ds(pl.multiple_of(start, 128), width)


RELATIVE = [(0, 0), (1, 0), (0, 1), (1, 1)]


def spread(p, parts):
    return parts[0], p.to_x(parts[1]), p.to_y(parts[2]), to_xy(p, parts[3])


def square_layer(
    p, tokens, attn_gain, query_weight, latent_weight, key_expand, value_expand, output_weight,
    mlp_gain, gate_weight, up_weight, down_weight, cotangent, lengths,
):
    batch, length, _ = tokens.shape
    count = 2 * batch * length
    core, x, y = p.core, p.x, p.y
    ff = gate_weight.shape[1] // 2
    quarter = 2 * core + y
    v = Live({})

    def cols(value, parts, index):
        return half(value, index, 1, parts).astype(LOW)

    def x_own(value):
        return half(value, x, 1)

    def x_other(value):
        return half(value, 1 - x, 1)

    v.pgu = jnp.concatenate([cols(gate_weight, 2, core), cols(up_weight, 2, core)], 1)
    v.tok = p.to_core(tokens)
    v = sync(v)
    kv = half(pick(y, key_expand, value_expand), core, 0).astype(LOW).T
    gains = jnp.stack([attn_gain, mlp_gain] + [jnp.zeros_like(attn_gain)] * 6).astype(LOW)
    piece = [
        cols(latent_weight, 4, quarter), cols(output_weight, 4, quarter),
        cols(query_weight, 4, quarter), kv,
    ]
    piece = jnp.concatenate(piece, 1)
    pad = jnp.zeros((8, piece.shape[1] - 128), LOW)
    piece = jnp.concatenate([piece, jnp.concatenate([gains, pad], 1)], 0)
    seen = [piece] + [p.to_z(piece, k) for k in (1, 2, 3)]
    w_gu = after(v.pop.pgu, seen[1])
    w_gu = lax.all_gather(w_gu, "dp", axis=0, tiled=True)
    first = in_z(p, seen)
    v.a, v.b = first[:, :, :384], first[:, :, 384:]
    rows = jnp.stack([tokens, v.pop.tok], 1).astype(F32)
    v.normed1 = rows * inverse_rms(rows)
    v.pd = cols(down_weight, 4, quarter)
    v = sync(v)

    v.ax, v.by = p.to_x(v.a), p.to_y(v.b)
    v = sync(v)
    v.zd2 = p.to_z(v.pd, 2)
    v.ay, v.axy = p.to_y(v.a), p.to_y(v.ax)
    v.bx, v.bxy = p.to_x(v.b), p.to_x(v.by)
    v = sync(v)

    v.zd1, v.zd3 = p.to_z(v.pd, 1), p.to_z(v.pd, 3)
    v.from_ab = (v.pop.a, v.pop.ax, v.pop.ay, v.pop.axy, v.pop.b, v.pop.bx, v.pop.by, v.pop.bxy)
    plan = []
    for n, (r, k) in enumerate(RELATIVE):
        low = pl.ds(0, 128)
        plan += [
            lambda x, y, c, n=n, r=r, k=k: (
                n, (slice(None), low, pl.ds(0, 128)), 0,
                (slice(None), x ^ r, slice(None), lanes((y ^ k) * 128, 128)),
            ),
            lambda x, y, c, n=n, r=r, k=k: (
                4 + n, (slice(None), low, pl.ds(0, 256)), 1,
                (slice(None), x ^ r, slice(None), lanes((y ^ k) * 256, 256)),
            ),
            lambda x, y, c, n=n: (n, (pl.ds(2 * (1 - c), 2), low, pl.ds(128, 256)), 2, n),
            lambda x, y, c, n=n: (4 + n, (pl.ds(2 * (1 - c), 2), low, pl.ds(256, 128)), 3, n),
        ]
    wl, wq, v.wo_send, v.kv_send = placed(
        p, plan, v.from_ab,
        [(4, 2, 128, LAT), (4, 2, 128, GW), (4, 2, 128, 256), (4, 2, 128, 128)],
    )
    v.wl, v.wq = wl.reshape(D, LAT), wq.reshape(D, GW)
    gains = [part[:, 128:130, :128] for part in v.from_ab[:2]]
    gains = pick(x, jnp.stack(gains, 2), jnp.stack(gains[::-1], 2)).astype(F32)
    v.gain1, v.gain2 = gains[:, 0].reshape(D), gains[:, 1].reshape(D)
    v.first = (v.pop.normed1 * v.gain1).astype(LOW).reshape(batch, 2 * length, D)
    v.keys = dots("btd,dl->btl", v.first, v.wl).astype(LOW).reshape(batch, 2, length, LAT)
    v = sync(v)
    far_keys = p.up_y(v.keys)
    wo_come, kv_come = p.to_core(v.pop.wo_send), p.to_core(v.pop.kv_send)
    v.zd = in_z(p, [v.pop.pd, v.pop.zd1, v.pop.zd2, v.pop.zd3])
    v.dax, v.dby = p.to_x(v.zd[:2]), p.to_y(v.zd[2:])
    v.qt = dots("dn,btd->bnt", v.wq, v.first).astype(LOW)
    plan = []
    for n, (r, k) in enumerate(RELATIVE):
        for s in range(2):
            plan += [
                lambda x, y, c, n=n, r=r, k=k, s=s: (
                    (n, (pl.ds(2 * c, 2), pl.ds(0, 128), pl.ds(128, 256))) if s == 0 else (8, n)
                ) + (0, (slice(None), x ^ r, slice(None), lanes(((c ^ s) * 2 + (y ^ k)) * 256, 256))),
                lambda x, y, c, n=n, r=r, k=k, s=s: (
                    (4 + n, (pl.ds(2 * c, 2), pl.ds(0, 128), pl.ds(256, 128))) if s == 0 else (9, n)
                ) + (1, (y ^ k, slice(None), x ^ r, slice(None), lanes((c ^ s) * 128, 128))),
            ]
    wo, kv = placed(
        p, plan, (*v.pop.from_ab, wo_come, kv_come), [(2, 2, 128, D), (2, 2, 2, 128, LAT)]
    )
    v.wo, kv = wo.reshape(GW, D), kv.reshape(2, GW, LAT)
    v.kxt, v.vxt = kv[0], kv[1]
    starts = jnp.stack([core, 1 - core]).astype(jnp.int32) * length
    base = p.chip * 2 * length
    far = pick(p.chip, 2 * length, 0)
    meta = [base + starts, far + starts, base + starts, lengths[:, 0], jnp.zeros((1,), jnp.int32)]
    v.meta = jnp.concatenate(meta).astype(jnp.int32)
    v.keys = jnp.concatenate([v.keys, far_keys], axis=1)
    v = sync(v)

    v.cot = core_first(p, cotangent.reshape(count // 2, D))
    v.day, v.daxy = p.to_y(v.zd[:2]), p.to_y(v.dax)
    v.dbx, v.dbxy = p.to_x(v.zd[2:]), p.to_x(v.dby)
    cot = half(v.cot, core, 1)
    v.cot_c = [half(cot, i, 1) for i in (y, 1 - y)] + [half(v.cot, 1 - core, 1)]
    v.out, *v.att = attention_forward(v.meta, v.qt, v.kxt, v.vxt, v.keys)
    v = sync(v)

    branch = summed(
        p, lambda i: dots("bnt,nd->btd", v.out[:, :, i * length : (i + 1) * length], v.wo)
    )
    v.middle = tokens.astype(F32) + branch
    v.inv2 = inverse_rms(v.middle)
    second = v.middle * v.inv2 * v.gain2
    v.second = core_first(p, second.astype(LOW).reshape(count // 2, D))
    v = sync(v)

    front, back = v.zd[:2], v.pop.zd[2:]
    sides = (front, v.pop.dax, v.pop.day, v.pop.daxy, back, v.pop.dbx, v.pop.dby, v.pop.dbxy)
    whole = slice(None)
    plan = [lambda x, y, c, n=n: ((c, 4 + n, n), whole, 0, n) for n in range(4)]
    v.come = p.to_core(placed(p, plan, sides, [(4, 2, ff // 4, 256)])[0])
    v.sides = sides
    v.w_gu = w_gu
    v.act, v.hidden = feed_forward(v.second, v.w_gu)
    v = sync(v)
    plan = []
    for n, (r, k) in enumerate(RELATIVE):
        for s in range(2):
            plan += [
                lambda x, y, c, n=n, r=r, k=k, s=s: (
                    ((c, n, 4 + n), whole) if s == 0 else (8, n)
                ) + (
                    0, (whole, x ^ r, whole, lanes(((c ^ s) * 2 + (y ^ k)) * 256, 256)),
                )
            ]
    wd = placed(p, plan, (*v.pop.sides, v.pop.come), [(2, 2, ff // 4, D)])[0]
    v.wd = wd.reshape(ff, D)

    v.d_gu, v.ds_own, v.ds_other = feed_forward_back(v.cot, v.wd, v.pop.w_gu, v.pop.act)
    v = sync(v)
    v.ds_other = p.to_core(v.ds_other)
    v.gg = tn(v.pop.second, v.pop.d_gu).astype(LOW)
    v = sync(v)
    gg = lax.psum_scatter(v.pop.gg, "dp", scatter_dimension=0, tiled=True)
    d_second = (v.pop.ds_own + v.pop.ds_other.astype(F32)).reshape(batch, length, D)
    normed2 = v.middle * v.inv2
    v.gain2_sum = jnp.sum(d_second * normed2, axis=(0, 1))
    v.d_middle = cotangent.astype(F32) + norm_back(d_second, normed2, v.pop.inv2, v.pop.gain2)
    v.d_a = chip(p, v.d_middle.astype(LOW)).reshape(batch, 2 * length, D)
    go = dots("bnt,btd->nd", v.pop.out, v.d_a).astype(LOW).reshape(2, 2, 128, D)
    go_core = half(go, core, 3)
    go_parts = [half(go_core, y, 3), half(go_core, 1 - y, 3), half(go, 1 - core, 3)]
    gd_parts = [tn(v.hidden, part).astype(LOW) for part in v.pop.cot_c]
    v.r_a, v.r_ay, r_send = [
        jnp.concatenate([gd.reshape(2, 2, -1, gd.shape[-1]), go], 2)
        for gd, go in zip(gd_parts, go_parts)
    ]
    v.r_b = p.to_core(r_send)
    v.dot = dots("nd,btd->bnt", v.pop.wo, v.pop.d_a).astype(LOW)
    v = sync(v)

    full = slice(None)
    rows = count // 2
    branch = summed(p, lambda i: mm(v.hidden[i * rows : (i + 1) * rows], v.wd))
    v.out_done = (v.pop.middle + branch.reshape(batch, length, D)).astype(LOW)
    del v.hidden, v.wd
    v.r_ay, v.r_bx = p.to_y(v.r_ay), p.to_x(x_other(v.r_b))
    v.back0 = attention_backward(
        0, v.meta, v.qt, v.dot, *v.att, v.kxt, v.vxt, v.keys, ()
    )
    v = sync(v)
    layer_out = v.pop.out_done
    v.r_a = add_low(v.r_a, v.pop.r_ay)
    v.r_b = add_low(x_own(v.r_b), v.pop.r_bx)
    v.r_ax, v.r_by = p.to_x(x_other(v.r_a)), p.to_y(half(v.r_b, 1 - y, 3))
    d_keys = v.back0[1]
    v.dk0, v.dk_far0 = d_keys[:2], p.down_y(d_keys[2:].astype(LOW))
    v.back1 = attention_backward(
        1, v.meta, v.qt, v.dot, *v.att, v.kxt, v.vxt, v.keys, v.back0[2:]
    )
    v = sync(v)

    back0, back1 = v.pop.back0, v.pop.back1
    v.far1 = p.down_y(back1[1][2:].astype(LOW))
    v.dk1 = back1[1][:2]
    v.dk0 = (v.dk0 + v.pop.dk_far0.astype(F32)).astype(LOW).reshape(1, 2 * length, LAT)
    plan = []
    for n in range(2):
        for s in range(2):
            plan += [
                lambda x, y, c, n=n, s=s: (n, (slice(None), lanes((c ^ s) * 128, 128)), s, n)
            ]
    v.kv_mine, kv_send = placed(p, plan, back1[2:], [(2, GW, 128)] * 2)
    v.kv_come = p.to_core(kv_send)
    r_a = add_low(x_own(v.pop.r_a), v.pop.r_ax)[:, 0]
    r_b = add_low(half(v.pop.r_b, y, 3), v.pop.r_by)[:, 0]
    v.r = ordered(core, r_a, r_b, 0)

    def r_step(k):
        return p.to_z(half(v.r, (p.z + k) % 4, 0, 4), k)

    v.dq_t = jnp.stack([back0[0], back1[0]])
    v.gq = dots("btd,bnt->dn", v.first, v.dq_t).astype(LOW).reshape(4, 2, 128, GW)
    v = sync(v)
    v.r1, v.r2 = r_step(1), r_step(2)
    dk1 = (v.pop.dk1 + v.pop.far1.astype(F32)).astype(LOW).reshape(1, 2 * length, LAT)
    d_latent = jnp.concatenate([v.pop.dk0, dk1])
    gl = dots("btd,btl->dl", v.pop.first, d_latent).astype(LOW).reshape(4, 2, 128, LAT)
    plan = []
    for n, (r, k) in enumerate(RELATIVE):
        plan += [
            lambda x, y, c, n=n, r=r, k=k: (
                0, (full, x ^ r, full, lanes((y ^ k) * 256, 256)), n, (full, full, pl.ds(0, 256)),
            ),
            lambda x, y, c, n=n, r=r, k=k: (
                1, (full, x ^ r, full, lanes((y ^ k) * 128, 128)), n, (full, full, pl.ds(384, 128)),
            ),
        ]
        for s in range(2):
            plan += [
                lambda x, y, c, n=n, r=r, k=k, s=s: (
                    2 + s, (y ^ k, full, x ^ r), n, (pl.ds(2 * (c ^ s), 2), full, pl.ds(256, 128)),
                )
            ]
    kv = [part.reshape(2, 2, 2, 128, 128) for part in (v.pop.kv_mine, v.pop.kv_come)]
    v.found = spread(p, placed(p, plan, (v.pop.gq, gl, *kv), [(4, 128, 512)] * 4))
    dq_t = v.pop.dq_t

    def first_grad(i):
        part = slice(i * length, (i + 1) * length)
        by_q = dots("bnt,dn->btd", dq_t[:, :, part], v.wq)
        return by_q + dots("btl,dl->btd", d_latent[:, part], v.wl)

    d_first = summed(p, first_grad)
    own = tokens.astype(F32)
    inverse1 = inverse_rms(own)
    normed1 = own * inverse1
    gains = jnp.stack([jnp.sum(d_first * normed1, axis=(0, 1)), v.pop.gain2_sum])
    v.gains = gains.astype(LOW).reshape(2, 4, 2, 128)
    v.tokens_done = v.d_middle + norm_back(d_first, normed1, inverse1, v.gain1)
    v = sync(v)
    grad_tokens = v.pop.tokens_done
    v.r3 = r_step(3)
    gains = jnp.moveaxis(v.pop.gains, 0, 1).reshape(4, 4, 128)
    gains = jnp.pad(gains, ((0, 0), (0, 4), (0, 384)))
    v.q = z_scatter(p, jnp.concatenate([add_all(v.pop.found), gains], 1))
    v.gg = gg
    v.gg = add_low(v.gg, p.to_y(v.gg))
    v = sync(v)
    v.q1 = p.to_y(v.q)
    v.gg1 = p.to_core(v.gg)
    v.r = add_all([half(v.r, p.z, 0, 4), v.pop.r1, v.pop.r2, v.pop.r3])[0]
    v = sync(v)
    v.r1 = p.to_y(v.r)
    grad_gate = ordered(core, v.gg[:, :ff], v.gg1[:, :ff], 1).astype(F32)
    grad_up = ordered(core, v.gg[:, ff:], v.gg1[:, ff:], 1).astype(F32)
    gains = add_low(v.q[128:132, :128], v.q1[128:132, :128])
    x_gains = p.to_x(gains)
    q0, q1 = pick(y, v.q, v.q1), pick(y, v.q1, v.q)
    mine = jnp.concatenate([q0, q1], 1)
    mine = lax.dynamic_update_slice(mine, gains, (128, 0))
    other = p.to_core(mine)
    x_other_gains = p.send(gains, lambda s, d: (s ^ 1, d ^ 1))
    v.ends = grad_gate, grad_up, gains, mine, other, x_gains, x_other_gains
    v = sync(v)
    grad_gate, grad_up, gains, mine, other, x_gains, x_other_gains = v.ends
    own_rows = ordered(y, v.r, v.r1, 1)
    other_rows = p.to_core(own_rows)
    grad_down, grad_output = [
        ordered(core, own_rows[part], other_rows[part], 1).astype(F32)
        for part in (slice(0, ff // 4), slice(ff // 4, None))
    ]
    zero, one = pick(core, mine, other), pick(core, other, mine)

    def columns(start, width):
        found = [part[:128, i : i + width] for part in (zero, one) for i in (start, start + 512)]
        return jnp.concatenate(found, 1).astype(F32)

    def expand_grad(start):
        return jnp.concatenate([p_[:128, start : start + 128] for p_ in (zero, one)], 1)

    near_gains = pick(x, gains, x_gains).astype(F32) + pick(x, x_gains, gains).astype(F32)
    far = other[128:132, :128]
    far_gains = pick(x, far, x_other_gains).astype(F32) + pick(x, x_other_gains, far).astype(F32)
    gains = half((near_gains + far_gains).reshape(2, 2, 128), x, 1)[:, 0]
    return (
        layer_out, grad_tokens, gains[0], columns(0, 256), columns(384, 128),
        expand_grad(256).T.astype(F32), expand_grad(768).T.astype(F32), grad_output, gains[1],
        grad_gate, grad_up, grad_down,
    )


def per_device(*arguments):
    p = Place()
    return (square_layer if p.square else plain_layer)(p, *arguments)


def solution(mesh):
    rows, gain, weight, across = P("dp", "seq", None), P("dp"), P("dp", None), P(None, "dp")
    return jax.shard_map(
        per_device,
        mesh=mesh,
        in_specs=(
            rows, gain, weight, weight, across, across, weight, gain, weight, weight, weight, rows,
            P("dp", None),
        ),
        out_specs=(
            rows, rows, gain, weight, weight, across, across, weight, gain, weight, weight, weight,
        ),
        check_vma=False,
    )
```

```python
import jax
import jax.numpy as jnp
from jax import lax
from jax.experimental import pallas as pl
from jax.experimental.pallas import tpu as pltpu
from jax.sharding import PartitionSpec as P

D = 1024
H = 16
HD = 64
KVH = 2
LAT = 256
GH = H // KVH
GW = D // KVH
EPS = 1e-06
SCALE = HD ** (-0.5)
LOG2E = 1.4426950408889634
NEG = -1e30

LOW = jnp.bfloat16
F32 = jnp.float32
ALL = ("seq", "dp")
VMEM_LIMIT = 56 * 1024 * 1024


def mm(left, right):
    return jnp.dot(left, right, preferred_element_type=F32)


def tn(left, right):
    return lax.dot_general(left, right, (((0,), (0,)), ((), ())), preferred_element_type=F32)


def nt(left, right):
    return lax.dot_general(left, right, (((1,), (1,)), ((), ())), preferred_element_type=F32)


def block_bias(k0, q0, first, width):
    kpos = k0 + lax.broadcasted_iota(jnp.int32, (width, width), 0)
    qpos = q0 + lax.broadcasted_iota(jnp.int32, (width, width), 1)
    lowest = jnp.where(qpos >= first, first, 0)
    return jnp.where((kpos <= qpos) & (kpos >= lowest), 0.0, NEG)


def block_needed(k0, q0, first, width):
    before = jnp.logical_and(q0 >= first, k0 + (width - 1) < first)
    return jnp.logical_and(k0 <= q0, jnp.logical_not(before))


def forward_kernel(nkb, batch, width, meta, qt, kxt, vxt, c, o_low, o_full, mix_out, lse_out, q_s, acc, m_s, l_s, p_s):
    b, qb = pl.program_id(0), pl.program_id(1)
    q0, first, diag = meta[nkb + qb], meta[nkb + 2 + b], meta[nkb + 2 + batch] + qb
    for h in range(GH):
        cols = slice(h * width, (h + 1) * width)
        rows = slice(h * HD, (h + 1) * HD)
        q_s[:, cols] = (tn(kxt[rows, :], qt[0, rows, :]) * (SCALE * LOG2E)).astype(LOW)
    m_s[...] = jnp.full_like(m_s, NEG)
    l_s[...] = jnp.zeros_like(l_s)
    acc[...] = jnp.zeros_like(acc)

    def step(j, carry):
        kb = lax.rem(diag + j, nkb)
        k0 = meta[kb]

        @pl.when(block_needed(k0, q0, first, width))
        def _():
            bias = block_bias(k0, q0, first, width)
            keys = c[0, kb]
            keys_t = keys.T
            alphas = []
            for h in range(GH):
                cols = slice(h * width, (h + 1) * width)
                s = mm(keys, q_s[:, cols]) + bias
                m_old = m_s[:, cols]
                m_new = jnp.maximum(m_old, jnp.max(s, axis=0, keepdims=True))
                p = jnp.exp2(s - m_new)
                alpha = jnp.exp2(m_old - m_new)
                m_s[:, cols] = m_new
                l_s[:, cols] = l_s[:, cols] * alpha + jnp.sum(p, axis=0, keepdims=True)
                p_s[:, cols] = p.astype(LOW)
                alphas.append(alpha)
            acc[...] = acc[...] * jnp.concatenate(alphas, 1) + mm(keys_t, p_s[...])

        return carry

    lax.fori_loop(0, nkb, step, 0)
    for h in range(GH):
        cols = slice(h * width, (h + 1) * width)
        rows = slice(h * HD, (h + 1) * HD)
        total = l_s[:, cols]
        mixed = (acc[:, cols] * (1.0 / total)).astype(LOW)
        mix_out[0, 0, :, cols] = mixed
        out = mm(vxt[rows, :], mixed)
        o_full[0, rows, :] = out
        o_low[0, rows, :] = out.astype(LOW)
        lse_out[0, 0, :, cols] = m_s[:, cols] + jnp.log(total) * LOG2E


def backward_kernel(
    b, nkb, batch, width, add_dw, meta, qt, dot_, o_full, mix, lse, kxt, vxt, c, *refs
):
    refs = list(refs)
    dk_old, dv_old = (refs.pop(0), refs.pop(0)) if add_dw else (None, None)
    dqt, dc, dkxt, dvxt, q_s, do_t, delta, dq, ds_s, p_s = refs
    qb = pl.program_id(0)
    q0, first, diag = meta[nkb + qb], meta[nkb + 2 + b], meta[nkb + 2 + batch] + qb

    @pl.when(qb == 0)
    def _():
        dc[...] = jnp.zeros_like(dc)
        dkxt[...] = dk_old[...] if add_dw else jnp.zeros_like(dkxt)
        dvxt[...] = dv_old[...] if add_dw else jnp.zeros_like(dvxt)


    for h in range(GH):
        cols = slice(h * width, (h + 1) * width)
        rows = slice(h * HD, (h + 1) * HD)
        qh, kh, doh, vh = qt[0, rows, :], kxt[rows, :], dot_[0, rows, :], vxt[rows, :]
        q_s[:, cols] = (tn(kh, qh) * (SCALE * LOG2E)).astype(LOW)
        do_t[:, cols] = tn(vh, doh).astype(LOW)
        delta[:, cols] = jnp.sum(doh.astype(F32) * o_full[0, rows, :], axis=0, keepdims=True)
    dq[...] = jnp.zeros_like(dq)

    def step(j, carry):
        kb = lax.rem(diag + j, nkb)
        k0 = meta[kb]

        @pl.when(block_needed(k0, q0, first, width))
        def _():
            bias = block_bias(k0, q0, first, width)
            keys = c[0, kb]
            keys_t = keys.T
            for h in range(GH):
                cols = slice(h * width, (h + 1) * width)
                s = mm(keys, q_s[:, cols]) + bias
                p = jnp.exp2(s - lse[0, 0, :, cols])
                dp = mm(keys, do_t[:, cols])
                ds = (p * (dp - delta[:, cols])).astype(LOW)
                p_s[:, cols] = p.astype(LOW)
                ds_s[:, cols] = ds
            dq[...] += mm(keys_t, ds_s[...])
            dc[kb] += nt(ds_s[...], q_s[...]) * (1.0 / LOG2E) + nt(p_s[...], do_t[...])

        return carry

    lax.fori_loop(0, nkb, step, 0)
    for h in range(GH):
        cols = slice(h * width, (h + 1) * width)
        rows = slice(h * HD, (h + 1) * HD)
        dq_low = (dq[:, cols] * SCALE).astype(LOW)
        dqt[rows, :] = mm(kxt[rows, :], dq_low).astype(LOW)
        dkxt[rows, :] += nt(qt[0, rows, :], dq_low)
        dvxt[rows, :] += nt(dot_[0, rows, :], mix[0, 0, :, cols])


def attention_forward(meta, qt, kxt, vxt, c):
    batch, nkb, width, _ = c.shape
    wide = GH * width
    pairs = batch * 7 * GH * width * width * LAT
    expand = pl.BlockSpec((GW, LAT), lambda b, q: (0, 0))
    q_spec = pl.BlockSpec((1, GW, width), lambda b, q: (b, 0, q))
    return pl.pallas_call(
        lambda *refs: forward_kernel(nkb, batch, width, *refs),
        grid=(batch, 2),
        in_specs=[
            pl.BlockSpec(memory_space=pltpu.SMEM),
            q_spec,
            expand,
            expand,
            pl.BlockSpec((1, nkb, width, LAT), lambda b, q: (b, 0, 0, 0)),
        ],
        out_specs=[
            q_spec,
            q_spec,
            pl.BlockSpec((1, 1, LAT, wide), lambda b, q: (b, q, 0, 0)),
            pl.BlockSpec((1, 1, 1, wide), lambda b, q: (b, q, 0, 0)),
        ],
        out_shape=[
            jax.ShapeDtypeStruct(qt.shape, LOW),
            jax.ShapeDtypeStruct(qt.shape, F32),
            jax.ShapeDtypeStruct((batch, 2, LAT, wide), LOW),
            jax.ShapeDtypeStruct((batch, 2, 1, wide), F32),
        ],
        scratch_shapes=[
            pltpu.VMEM((LAT, wide), LOW),
            pltpu.VMEM((LAT, wide), F32),
            pltpu.VMEM((1, wide), F32),
            pltpu.VMEM((1, wide), F32),
            pltpu.VMEM((width, wide), LOW),
        ],
        compiler_params=pltpu.CompilerParams(
            dimension_semantics=("arbitrary", "arbitrary"), vmem_limit_bytes=VMEM_LIMIT
        ),
        cost_estimate=pl.CostEstimate(
            flops=4 * pairs, bytes_accessed=16 << 20, transcendentals=batch * 7 * GH * width * width
        ),
        name="attention_forward",
    )(meta, qt, kxt, vxt, c)


def attention_backward(b, meta, qt, dot_, o_full, mix, lse, kxt, vxt, c, old_dw):
    batch, nkb, width, _ = c.shape
    wide = GH * width
    pairs = 7 * GH * width * width * LAT * 2
    expand = pl.BlockSpec((GW, LAT), lambda q: (0, 0))
    return pl.pallas_call(
        lambda *refs: backward_kernel(b, nkb, batch, width, bool(old_dw), *refs),
        grid=(2,),
        in_specs=[
            pl.BlockSpec(memory_space=pltpu.SMEM),
            pl.BlockSpec((1, GW, width), lambda q: (b, 0, q)),
            pl.BlockSpec((1, GW, width), lambda q: (b, 0, q)),
            pl.BlockSpec((1, GW, width), lambda q: (b, 0, q)),
            pl.BlockSpec((1, 1, LAT, wide), lambda q: (b, q, 0, 0)),
            pl.BlockSpec((1, 1, 1, wide), lambda q: (b, q, 0, 0)),
            expand,
            expand,
            pl.BlockSpec((1, nkb, width, LAT), lambda q: (b, 0, 0, 0)),
        ]
        + [expand] * len(old_dw),
        out_specs=[
            pl.BlockSpec((GW, width), lambda q: (0, q)),
            pl.BlockSpec((nkb, width, LAT), lambda q: (0, 0, 0)),
            expand,
            expand,
        ],
        out_shape=[
            jax.ShapeDtypeStruct((GW, 2 * width), LOW),
            jax.ShapeDtypeStruct((nkb, width, LAT), F32),
            jax.ShapeDtypeStruct(kxt.shape, F32),
            jax.ShapeDtypeStruct(vxt.shape, F32),
        ],
        scratch_shapes=[
            pltpu.VMEM((LAT, wide), LOW),
            pltpu.VMEM((LAT, wide), LOW),
            pltpu.VMEM((1, wide), F32),
            pltpu.VMEM((LAT, wide), F32),
            pltpu.VMEM((width, wide), LOW),
            pltpu.VMEM((width, wide), LOW),
        ],
        compiler_params=pltpu.CompilerParams(
            dimension_semantics=("arbitrary",), vmem_limit_bytes=VMEM_LIMIT
        ),
        cost_estimate=pl.CostEstimate(
            flops=5 * pairs, bytes_accessed=10 << 20, transcendentals=7 * GH * width * width
        ),
        name="attention_backward",
    )(meta, qt, dot_, o_full, mix, lse, kxt, vxt, c, *old_dw)


def hidden_kernel(x, w, act, hidden):
    width = hidden.shape[1]
    both = mm(x[...], w[...])
    act[...] = both
    gate, up = both[:, :width], both[:, width:]
    hidden[...] = (gate * jax.nn.sigmoid(gate) * up).astype(LOW)


def hidden_back_kernel(cot, down, w, act, grad, own, other):
    width = down.shape[0]
    d_hidden = nt(cot[...], down[...])
    gate, up = act[:, :width], act[:, width:]
    sig = jax.nn.sigmoid(gate)
    grad[:, :width] = (d_hidden * up * sig * (1.0 + gate * (1.0 - sig))).astype(LOW)
    grad[:, width:] = (d_hidden * (gate * sig)).astype(LOW)
    back = nt(grad[...], w[...])
    mine = pl.program_id(0) < pl.num_programs(0) // 2

    @pl.when(mine)
    def _():
        own[...] = back

    @pl.when(jnp.logical_not(mine))
    def _():
        other[...] = back.astype(LOW)


TILE = 256


def tiled(width):
    return pl.BlockSpec((TILE, width), lambda i: (i, 0))


def resident(shape):
    return pl.BlockSpec(shape, lambda i: (0, 0), pipeline_mode=pl.Buffered(1))


def feed_forward(x, w):
    count, both = x.shape[0], w.shape[1]
    return pl.pallas_call(
        hidden_kernel,
        grid=(count // TILE,),
        in_specs=[tiled(x.shape[1]), resident(w.shape)],
        out_specs=[tiled(both), tiled(both // 2)],
        out_shape=[
            jax.ShapeDtypeStruct((count, both), F32),
            jax.ShapeDtypeStruct((count, both // 2), LOW),
        ],
        compiler_params=pltpu.CompilerParams(vmem_limit_bytes=VMEM_LIMIT),
        cost_estimate=pl.CostEstimate(
            flops=2 * x.size * both, bytes_accessed=20 << 20, transcendentals=count * both // 2
        ),
        name="feed_forward",
    )(x, w)


def feed_forward_back(cot, down, w, act):
    count, both = act.shape
    width, steps = w.shape[0], count // TILE
    return pl.pallas_call(
        hidden_back_kernel,
        grid=(steps,),
        in_specs=[tiled(cot.shape[1]), resident(down.shape), resident(w.shape), tiled(both)],
        out_specs=[
            tiled(both),
            pl.BlockSpec((TILE, width), lambda i: (jnp.minimum(i, steps // 2 - 1), 0)),
            pl.BlockSpec((TILE, width), lambda i: (jnp.maximum(i - steps // 2, 0), 0)),
        ],
        out_shape=[
            jax.ShapeDtypeStruct((count, both), LOW),
            jax.ShapeDtypeStruct((count // 2, width), F32),
            jax.ShapeDtypeStruct((count // 2, width), LOW),
        ],
        compiler_params=pltpu.CompilerParams(vmem_limit_bytes=VMEM_LIMIT),
        cost_estimate=pl.CostEstimate(
            flops=3 * cot.size * both, bytes_accessed=30 << 20, transcendentals=count * both // 2
        ),
        name="feed_forward_back",
    )(cot, down, w, act)


class Place:
    def __init__(self):
        self.seq, self.dp = lax.axis_size("seq"), lax.axis_size("dp")
        s, d = lax.axis_index("seq"), lax.axis_index("dp")
        self.core, self.chip = s % 2, s // 2
        self.y, self.x, self.z = s // 2, d % 2, d // 2
        self.square = self.seq == 4 and self.dp == 8

    def pairs(self, move):
        found = []
        for s in range(self.seq):
            for d in range(self.dp):
                target = move(s, d)
                if target is not None:
                    found.append((s * self.dp + d, target[0] * self.dp + target[1]))
        return found

    def send(self, value, move):
        return lax.ppermute(value, ALL, self.pairs(move))

    def to_core(self, value):
        return self.send(value, lambda s, d: (s ^ 1, d))

    def to_y(self, value):
        return self.send(value, lambda s, d: (s ^ 2, d))

    def to_x(self, value):
        return self.send(value, lambda s, d: (s, d ^ 1))

    def to_z(self, value, step):
        return self.send(value, lambda s, d: (s, (d + 2 * step) % 8))

    def up_y(self, value):
        return self.send(value, lambda s, d: (s + 2, d) if s < 2 else None)

    def down_y(self, value):
        return self.send(value, lambda s, d: (s - 2, d) if s >= 2 else None)


def half(value, index, axis, count=2):
    size = value.shape[axis] // count
    return lax.dynamic_slice_in_dim(value, index * size, size, axis)


def ordered(flag, own, other, axis):
    return jnp.where(
        flag == 0, jnp.concatenate([own, other], axis), jnp.concatenate([other, own], axis)
    )


def after(value, *others):
    return lax.optimization_barrier((value, others))[0]


def add_low(own, other):
    return (own.astype(F32) + other.astype(F32)).astype(LOW)


class Plain:
    def __init__(self, place):
        self.p = place
        count = place.seq // 2
        self.same_core = [[2 * i + c for i in range(count)] for c in range(2)]
        self.chip = [[2 * i, 2 * i + 1] for i in range(count)]

    def gather(self, w):
        core = self.p.core

        def full(value, axis=0):
            return lax.all_gather(value.astype(LOW), "dp", axis=axis, tiled=True)

        out = {name: full(half(w[name], core, 1)) for name in ("query", "latent", "gate", "up")}
        out["key_t"] = half(full(w["key"].T), core, 0)
        out["value_t"] = half(full(w["value"].T), core, 0)
        out["output"] = half(full(w["output"]), core, 0)
        out["down"] = half(full(w["down"]), core, 0)
        out["gain1"], out["gain2"] = full(w["gain1"]), full(w["gain2"])
        return out

    def columns(self, grad):
        share = lax.psum_scatter(grad.astype(LOW), "dp", scatter_dimension=0, tiled=True)
        share = lax.psum(share, "seq", axis_index_groups=self.same_core)
        return lax.all_gather(
            share, "seq", axis=1, tiled=True, axis_index_groups=self.chip
        ).astype(F32)

    def rows(self, grad):
        grad = grad.astype(LOW)
        grad = ordered(self.p.core, grad, jnp.zeros_like(grad), 0)
        share = lax.psum_scatter(grad, "dp", scatter_dimension=0, tiled=True)
        return lax.psum(share, "seq").astype(F32)

    def gain(self, grad):
        share = lax.psum_scatter(grad.astype(LOW), "dp", scatter_dimension=0, tiled=True)
        return lax.psum(share, "seq").astype(F32)


def inverse_rms(values):
    return lax.rsqrt(jnp.mean(values * values, axis=-1, keepdims=True) + EPS)


def norm_back(grad, normed, inverse, gain):
    scaled = grad * gain
    return inverse * (scaled - normed * jnp.mean(scaled * normed, axis=-1, keepdims=True))


def dots(spec, left, right):
    return jnp.einsum(spec, left, right, preferred_element_type=F32)


def pick(flag, zero, one):
    return jnp.where(flag == 0, zero, one)


def chip(p, own):
    return jnp.stack([own, p.to_core(own)], axis=1)


def chip_sum(p, partial):
    return partial[:, 0] + p.to_core(partial[:, 1].astype(LOW)).astype(F32)


def plain_layer(
    p, tokens, attn_gain, query_weight, latent_weight, key_expand, value_expand, output_weight,
    mlp_gain, gate_weight, up_weight, down_weight, cotangent, lengths,
):
    ways = Plain(p)
    batch, length, _ = tokens.shape
    count = 2 * batch * length
    w = ways.gather(
        {
            "gain1": attn_gain, "query": query_weight, "latent": latent_weight,
            "key": key_expand, "value": value_expand, "output": output_weight,
            "gain2": mlp_gain, "gate": gate_weight, "up": up_weight, "down": down_weight,
        }
    )
    gain1, gain2 = w["gain1"].astype(F32), w["gain2"].astype(F32)
    firsts = lengths[:, 0]
    chips = p.seq // 2
    rows = chip(p, tokens).astype(F32)
    first_low = (rows * inverse_rms(rows) * gain1).astype(LOW)
    first_flat = first_low.reshape(batch, 2 * length, D)
    latent = dots("btd,dl->btl", first_flat, w["latent"]).astype(LOW)
    query_t = dots("dn,btd->bnt", w["query"], first_flat).astype(LOW)
    blocks = latent.reshape(batch, 2, length, LAT)
    starts = jnp.stack([p.core, 1 - p.core]).astype(jnp.int32) * length
    base = p.chip * 2 * length
    keys = lax.all_gather(blocks, "seq", axis=1, tiled=True, axis_index_groups=ways.same_core)
    key_starts = (
        2 * length * jnp.arange(chips, dtype=jnp.int32)[:, None] + starts[None, :]
    ).reshape(-1)
    diag = (2 * p.chip).astype(jnp.int32).reshape(1)
    meta = jnp.concatenate([key_starts, base + starts, firsts, diag]).astype(jnp.int32)
    out_low, *att = attention_forward(meta, query_t, w["key_t"], w["value_t"], keys)
    branch = dots("bnt,nd->btd", out_low, w["output"])
    middle = tokens.astype(F32) + chip_sum(p, branch.reshape(batch, 2, length, D))
    inverse2 = inverse_rms(middle)
    normed2 = middle * inverse2
    second = chip(p, (normed2 * gain2).astype(LOW)).reshape(count, D)
    cot = chip(p, cotangent).reshape(count, D)
    gate = mm(second, w["gate"])
    up = mm(second, w["up"])
    sig = jax.nn.sigmoid(gate)
    act = gate * sig
    hidden = (act * up).astype(LOW)
    partial = mm(hidden, w["down"]).reshape(batch, 2, length, D)
    layer_out = (middle + chip_sum(p, partial)).astype(LOW)
    grad_down = ways.rows(tn(hidden, cot))
    d_hidden = nt(cot, w["down"])
    d_gate = (d_hidden * up * sig * (1.0 + gate * (1.0 - sig))).astype(LOW)
    d_up = (d_hidden * act).astype(LOW)
    grad_gate, grad_up = ways.columns(tn(second, d_gate)), ways.columns(tn(second, d_up))
    partial = (nt(d_gate, w["gate"]) + nt(d_up, w["up"])).reshape(batch, 2, length, D)
    d_second = chip_sum(p, partial)
    gain2_sum = jnp.sum(d_second * normed2, axis=(0, 1))
    d_middle = cotangent.astype(F32) + norm_back(d_second, normed2, inverse2, gain2)
    d_a = chip(p, d_middle.astype(LOW)).reshape(batch, 2 * length, D)
    grad_output = ways.rows(dots("bnt,btd->nd", out_low, d_a))
    d_out_t = dots("nd,btd->bnt", w["output"], d_a).astype(LOW)
    d_queries, d_keys, sums = [], [], ()
    for b in range(batch):
        found = attention_backward(
            b, meta, query_t, d_out_t, *att, w["key_t"], w["value_t"], keys, sums
        )
        sums = found[2:]
        d_queries.append(found[0])
        d_keys.append(found[1])
    dq_t, d_keys = jnp.stack(d_queries), jnp.stack(d_keys)
    d_key_t, d_value_t = sums
    d_blocks = lax.psum_scatter(
        d_keys.astype(LOW), "seq", scatter_dimension=1, tiled=True,
        axis_index_groups=ways.same_core,
    )
    d_latent = d_blocks.astype(LOW).reshape(batch, 2 * length, LAT)
    grad_query = ways.columns(dots("btd,bnt->dn", first_flat, dq_t))
    grad_latent = ways.columns(dots("btd,btl->dl", first_flat, d_latent))
    d_first = dots("bnt,dn->btd", dq_t, w["query"]) + dots("btl,dl->btd", d_latent, w["latent"])
    d_first = chip_sum(p, d_first.reshape(batch, 2, length, D))
    own = tokens.astype(F32)
    inverse1 = inverse_rms(own)
    normed1 = own * inverse1
    gain1_sum = jnp.sum(d_first * normed1, axis=(0, 1))
    grad_tokens = d_middle + norm_back(d_first, normed1, inverse1, gain1)
    return (
        layer_out, grad_tokens, ways.gain(gain1_sum), grad_query, grad_latent,
        ways.rows(d_key_t).T, ways.rows(d_value_t).T, grad_output, ways.gain(gain2_sum),
        grad_gate, grad_up, grad_down,
    )


class Live:
    def __init__(self, values):
        self.__dict__.update(values)

    @property
    def pop(self):
        return Taken(self)


class Taken:
    def __init__(self, live):
        self.live = live

    def __getattr__(self, name):
        return self.live.__dict__.pop(name)


def sync(v):
    return Live(lax.optimization_barrier(dict(v.__dict__)))


def in_z(p, seen):
    out = []
    for z in range(4):
        back = (p.z - z) % 4
        pair = [jnp.where(back % 2 == 0, seen[k], seen[k + 1]) for k in (0, 2)]
        out.append(jnp.where(back < 2, pair[0], pair[1]))
    return jnp.stack(out)


def z_scatter(p, parts):
    total = half(parts, p.z, 0, 4)[0].astype(F32)
    for k in (1, 2, 3):
        total = total + p.to_z(half(parts, (p.z + k) % 4, 0, 4), k)[0].astype(F32)
    return total.astype(LOW)


def summed(p, make):
    come = p.to_core(make(1).astype(LOW))
    return make(0) + come.astype(F32)


def core_first(p, own):
    return jnp.concatenate([own, p.to_core(own)], 0)


def to_xy(p, value):
    return p.send(value, lambda s, d: (s ^ 2, d ^ 1))


def add_all(parts):
    return sum(part.astype(F32) for part in parts).astype(LOW)


def place_kernel(plan, sources, outs, where, *refs):
    src, dst = refs[:sources], refs[sources:]
    spot = where[0], where[1], where[2]
    for make in plan:
        source, there, out, here = make(*spot)
        if isinstance(source, int):
            dst[out][here] = src[source][there].astype(LOW)
            continue
        flag, sides = source[0], source[1:]
        for value in range(2):

            @pl.when(flag == value)
            def _(side=sides[value], there=there, out=out, here=here):
                dst[out][here] = src[side][there].astype(LOW)


def placed(p, plan, sources, shapes):
    where = jnp.stack([p.x, p.y, p.core]).astype(jnp.int32)
    inside = pl.BlockSpec(memory_space=pltpu.VMEM)
    return pl.pallas_call(
        lambda *refs: place_kernel(plan, len(sources), len(shapes), *refs),
        in_specs=[pl.BlockSpec(memory_space=pltpu.SMEM)] + [inside] * len(sources),
        out_specs=[inside] * len(shapes),
        out_shape=[jax.ShapeDtypeStruct(shape, LOW) for shape in shapes],
        compiler_params=pltpu.CompilerParams(vmem_limit_bytes=VMEM_LIMIT),
        name="place",
    )(where, *sources)


def lanes(start, width):
    return pl.ds(pl.multiple_of(start, 128), width)


RELATIVE = [(0, 0), (1, 0), (0, 1), (1, 1)]


def spread(p, parts):
    return parts[0], p.to_x(parts[1]), p.to_y(parts[2]), to_xy(p, parts[3])


def square_layer(
    p, tokens, attn_gain, query_weight, latent_weight, key_expand, value_expand, output_weight,
    mlp_gain, gate_weight, up_weight, down_weight, cotangent, lengths,
):
    batch, length, _ = tokens.shape
    count = 2 * batch * length
    core, x, y = p.core, p.x, p.y
    ff = gate_weight.shape[1] // 2
    quarter = 2 * core + y
    v = Live({})

    def cols(value, parts, index):
        return half(value, index, 1, parts).astype(LOW)

    def x_own(value):
        return half(value, x, 1)

    def x_other(value):
        return half(value, 1 - x, 1)

    v.pgu = jnp.concatenate([cols(gate_weight, 2, core), cols(up_weight, 2, core)], 1)
    v.tok = p.to_core(tokens)
    v = sync(v)
    kv = half(pick(y, key_expand, value_expand), core, 0).astype(LOW).T
    gains = jnp.stack([attn_gain, mlp_gain] + [jnp.zeros_like(attn_gain)] * 6).astype(LOW)
    piece = [
        cols(latent_weight, 4, quarter), cols(output_weight, 4, quarter),
        cols(query_weight, 4, quarter), kv,
    ]
    piece = jnp.concatenate(piece, 1)
    pad = jnp.zeros((8, piece.shape[1] - 128), LOW)
    piece = jnp.concatenate([piece, jnp.concatenate([gains, pad], 1)], 0)
    seen = [piece] + [p.to_z(piece, k) for k in (1, 2, 3)]
    w_gu = after(v.pop.pgu, seen[1])
    w_gu = lax.all_gather(w_gu, "dp", axis=0, tiled=True)
    first = in_z(p, seen)
    v.a, v.b = first[:, :, :384], first[:, :, 384:]
    rows = jnp.stack([tokens, v.pop.tok], 1).astype(F32)
    v.normed1 = rows * inverse_rms(rows)
    v.pd = cols(down_weight, 4, quarter)
    v = sync(v)

    v.ax, v.by = p.to_x(v.a), p.to_y(v.b)
    v.zd1 = p.to_z(v.pd, 1)
    v = sync(v)
    v.zd2 = p.to_z(v.pd, 2)
    v.ay, v.axy = p.to_y(v.a), p.to_y(v.ax)
    v.bx, v.bxy = p.to_x(v.b), p.to_x(v.by)
    v = sync(v)

    v.zd3 = p.to_z(v.pd, 3)
    v.from_ab = (v.pop.a, v.pop.ax, v.pop.ay, v.pop.axy, v.pop.b, v.pop.bx, v.pop.by, v.pop.bxy)
    plan = []
    for n, (r, k) in enumerate(RELATIVE):
        low = pl.ds(0, 128)
        plan += [
            lambda x, y, c, n=n, r=r, k=k: (
                n, (slice(None), low, pl.ds(0, 128)), 0,
                (slice(None), x ^ r, slice(None), lanes((y ^ k) * 128, 128)),
            ),
            lambda x, y, c, n=n, r=r, k=k: (
                4 + n, (slice(None), low, pl.ds(0, 256)), 1,
                (slice(None), x ^ r, slice(None), lanes((y ^ k) * 256, 256)),
            ),
            lambda x, y, c, n=n: (n, (pl.ds(2 * (1 - c), 2), low, pl.ds(128, 256)), 2, n),
            lambda x, y, c, n=n: (4 + n, (pl.ds(2 * (1 - c), 2), low, pl.ds(256, 128)), 3, n),
        ]
    wl, wq, v.wo_send, v.kv_send = placed(
        p, plan, v.from_ab,
        [(4, 2, 128, LAT), (4, 2, 128, GW), (4, 2, 128, 256), (4, 2, 128, 128)],
    )
    v.wl, v.wq = wl.reshape(D, LAT), wq.reshape(D, GW)
    gains = [part[:, 128:130, :128] for part in v.from_ab[:2]]
    gains = pick(x, jnp.stack(gains, 2), jnp.stack(gains[::-1], 2)).astype(F32)
    v.gain1, v.gain2 = gains[:, 0].reshape(D), gains[:, 1].reshape(D)
    v.first = (v.pop.normed1 * v.gain1).astype(LOW).reshape(batch, 2 * length, D)
    v.keys = dots("btd,dl->btl", v.first, v.wl).astype(LOW).reshape(batch, 2, length, LAT)
    v = sync(v)
    far_keys = p.up_y(v.keys)
    wo_come, kv_come = p.to_core(v.pop.wo_send), p.to_core(v.pop.kv_send)
    v.zd = in_z(p, [v.pop.pd, v.pop.zd1, v.pop.zd2, v.pop.zd3])
    v.dax, v.dby = p.to_x(v.zd[:2]), p.to_y(v.zd[2:])
    v.qt = dots("dn,btd->bnt", v.wq, v.first).astype(LOW)
    plan = []
    for n, (r, k) in enumerate(RELATIVE):
        for s in range(2):
            plan += [
                lambda x, y, c, n=n, r=r, k=k, s=s: (
                    (n, (pl.ds(2 * c, 2), pl.ds(0, 128), pl.ds(128, 256))) if s == 0 else (8, n)
                ) + (0, (slice(None), x ^ r, slice(None), lanes(((c ^ s) * 2 + (y ^ k)) * 256, 256))),
                lambda x, y, c, n=n, r=r, k=k, s=s: (
                    (4 + n, (pl.ds(2 * c, 2), pl.ds(0, 128), pl.ds(256, 128))) if s == 0 else (9, n)
                ) + (1, (y ^ k, slice(None), x ^ r, slice(None), lanes((c ^ s) * 128, 128))),
            ]
    wo, kv = placed(
        p, plan, (*v.pop.from_ab, wo_come, kv_come), [(2, 2, 128, D), (2, 2, 2, 128, LAT)]
    )
    v.wo, kv = wo.reshape(GW, D), kv.reshape(2, GW, LAT)
    v.kxt, v.vxt = kv[0], kv[1]
    starts = jnp.stack([core, 1 - core]).astype(jnp.int32) * length
    base = p.chip * 2 * length
    far = pick(p.chip, 2 * length, 0)
    meta = [base + starts, far + starts, base + starts, lengths[:, 0], jnp.zeros((1,), jnp.int32)]
    v.meta = jnp.concatenate(meta).astype(jnp.int32)
    v.keys = jnp.concatenate([v.keys, far_keys], axis=1)
    v = sync(v)

    v.cot = core_first(p, cotangent.reshape(count // 2, D))
    v.day, v.daxy = p.to_y(v.zd[:2]), p.to_y(v.dax)
    v.dbx, v.dbxy = p.to_x(v.zd[2:]), p.to_x(v.dby)
    cot = half(v.cot, core, 1)
    v.cot_c = [half(cot, i, 1) for i in (y, 1 - y)] + [half(v.cot, 1 - core, 1)]
    v.out, *v.att = attention_forward(v.meta, v.qt, v.kxt, v.vxt, v.keys)
    v = sync(v)

    branch = summed(
        p, lambda i: dots("bnt,nd->btd", v.out[:, :, i * length : (i + 1) * length], v.wo)
    )
    v.middle = tokens.astype(F32) + branch
    v.inv2 = inverse_rms(v.middle)
    second = v.middle * v.inv2 * v.gain2
    v.second = core_first(p, second.astype(LOW).reshape(count // 2, D))
    v = sync(v)

    front, back = v.zd[:2], v.pop.zd[2:]
    sides = (front, v.pop.dax, v.pop.day, v.pop.daxy, back, v.pop.dbx, v.pop.dby, v.pop.dbxy)
    whole = slice(None)
    plan = [lambda x, y, c, n=n: ((c, 4 + n, n), whole, 0, n) for n in range(4)]
    v.come = p.to_core(placed(p, plan, sides, [(4, 2, ff // 4, 256)])[0])
    v.sides = sides
    v.w_gu = w_gu
    v.act, v.hidden = feed_forward(v.second, v.w_gu)
    v = sync(v)
    plan = []
    for n, (r, k) in enumerate(RELATIVE):
        for s in range(2):
            plan += [
                lambda x, y, c, n=n, r=r, k=k, s=s: (
                    ((c, n, 4 + n), whole) if s == 0 else (8, n)
                ) + (
                    0, (whole, x ^ r, whole, lanes(((c ^ s) * 2 + (y ^ k)) * 256, 256)),
                )
            ]
    wd = placed(p, plan, (*v.pop.sides, v.pop.come), [(2, 2, ff // 4, D)])[0]
    v.wd = wd.reshape(ff, D)

    v.d_gu, v.ds_own, v.ds_other = feed_forward_back(v.cot, v.wd, v.pop.w_gu, v.pop.act)
    v = sync(v)
    v.ds_other = p.to_core(v.ds_other)
    v.gg = tn(v.pop.second, v.pop.d_gu).astype(LOW)
    v = sync(v)
    gg = lax.psum_scatter(v.pop.gg, "dp", scatter_dimension=0, tiled=True)
    d_second = (v.pop.ds_own + v.pop.ds_other.astype(F32)).reshape(batch, length, D)
    normed2 = v.middle * v.inv2
    v.gain2_sum = jnp.sum(d_second * normed2, axis=(0, 1))
    v.d_middle = cotangent.astype(F32) + norm_back(d_second, normed2, v.pop.inv2, v.pop.gain2)
    v.d_a = chip(p, v.d_middle.astype(LOW)).reshape(batch, 2 * length, D)
    go = dots("bnt,btd->nd", v.pop.out, v.d_a).astype(LOW).reshape(2, 2, 128, D)
    go_core = half(go, core, 3)
    go_parts = [half(go_core, y, 3), half(go_core, 1 - y, 3), half(go, 1 - core, 3)]
    gd_parts = [tn(v.hidden, part).astype(LOW) for part in v.pop.cot_c]
    v.r_a, v.r_ay, r_send = [
        jnp.concatenate([gd.reshape(2, 2, -1, gd.shape[-1]), go], 2)
        for gd, go in zip(gd_parts, go_parts)
    ]
    v.r_b = p.to_core(r_send)
    v.dot = dots("nd,btd->bnt", v.pop.wo, v.pop.d_a).astype(LOW)
    v = sync(v)

    full = slice(None)
    rows = count // 2
    branch = summed(p, lambda i: mm(v.hidden[i * rows : (i + 1) * rows], v.wd))
    v.out_done = (v.pop.middle + branch.reshape(batch, length, D)).astype(LOW)
    del v.hidden, v.wd
    v.r_ay, v.r_bx = p.to_y(v.r_ay), p.to_x(x_other(v.r_b))
    v.back0 = attention_backward(
        0, v.meta, v.qt, v.dot, *v.att, v.kxt, v.vxt, v.keys, ()
    )
    v = sync(v)
    layer_out = v.pop.out_done
    v.r_a = add_low(v.r_a, v.pop.r_ay)
    v.r_b = add_low(x_own(v.r_b), v.pop.r_bx)
    v.r_ax, v.r_by = p.to_x(x_other(v.r_a)), p.to_y(half(v.r_b, 1 - y, 3))
    d_keys = v.back0[1]
    v.dk0, v.dk_far0 = d_keys[:2], p.down_y(d_keys[2:].astype(LOW))
    v.back1 = attention_backward(
        1, v.meta, v.qt, v.dot, *v.att, v.kxt, v.vxt, v.keys, v.back0[2:]
    )
    v = sync(v)

    back0, back1 = v.pop.back0, v.pop.back1
    v.far1 = p.down_y(back1[1][2:].astype(LOW))
    v.dk1 = back1[1][:2]
    v.dk0 = (v.dk0 + v.pop.dk_far0.astype(F32)).astype(LOW).reshape(1, 2 * length, LAT)
    plan = []
    for n in range(2):
        for s in range(2):
            plan += [
                lambda x, y, c, n=n, s=s: (n, (slice(None), lanes((c ^ s) * 128, 128)), s, n)
            ]
    v.kv_mine, kv_send = placed(p, plan, back1[2:], [(2, GW, 128)] * 2)
    v.kv_come = p.to_core(kv_send)
    r_a = add_low(x_own(v.pop.r_a), v.pop.r_ax)[:, 0]
    r_b = add_low(half(v.pop.r_b, y, 3), v.pop.r_by)[:, 0]
    v.r = ordered(core, r_a, r_b, 0)

    def r_step(k):
        return p.to_z(half(v.r, (p.z + k) % 4, 0, 4), k)

    v.dq_t = jnp.stack([back0[0], back1[0]])
    v.gq = dots("btd,bnt->dn", v.first, v.dq_t).astype(LOW).reshape(4, 2, 128, GW)
    v = sync(v)
    v.r1, v.r2 = r_step(1), r_step(2)
    dk1 = (v.pop.dk1 + v.pop.far1.astype(F32)).astype(LOW).reshape(1, 2 * length, LAT)
    d_latent = jnp.concatenate([v.pop.dk0, dk1])
    gl = dots("btd,btl->dl", v.pop.first, d_latent).astype(LOW).reshape(4, 2, 128, LAT)
    plan = []
    for n, (r, k) in enumerate(RELATIVE):
        plan += [
            lambda x, y, c, n=n, r=r, k=k: (
                0, (full, x ^ r, full, lanes((y ^ k) * 256, 256)), n, (full, full, pl.ds(0, 256)),
            ),
            lambda x, y, c, n=n, r=r, k=k: (
                1, (full, x ^ r, full, lanes((y ^ k) * 128, 128)), n, (full, full, pl.ds(384, 128)),
            ),
        ]
        for s in range(2):
            plan += [
                lambda x, y, c, n=n, r=r, k=k, s=s: (
                    2 + s, (y ^ k, full, x ^ r), n, (pl.ds(2 * (c ^ s), 2), full, pl.ds(256, 128)),
                )
            ]
    kv = [part.reshape(2, 2, 2, 128, 128) for part in (v.pop.kv_mine, v.pop.kv_come)]
    v.found = spread(p, placed(p, plan, (v.pop.gq, gl, *kv), [(4, 128, 512)] * 4))
    dq_t = v.pop.dq_t

    def first_grad(i):
        part = slice(i * length, (i + 1) * length)
        by_q = dots("bnt,dn->btd", dq_t[:, :, part], v.wq)
        return by_q + dots("btl,dl->btd", d_latent[:, part], v.wl)

    d_first = summed(p, first_grad)
    own = tokens.astype(F32)
    inverse1 = inverse_rms(own)
    normed1 = own * inverse1
    gains = jnp.stack([jnp.sum(d_first * normed1, axis=(0, 1)), v.pop.gain2_sum])
    v.gains = gains.astype(LOW).reshape(2, 4, 2, 128)
    v.tokens_done = v.d_middle + norm_back(d_first, normed1, inverse1, v.gain1)
    v = sync(v)
    grad_tokens = v.pop.tokens_done
    v.r3 = r_step(3)
    gains = jnp.moveaxis(v.pop.gains, 0, 1).reshape(4, 4, 128)
    gains = jnp.pad(gains, ((0, 0), (0, 4), (0, 384)))
    v.q = z_scatter(p, jnp.concatenate([add_all(v.pop.found), gains], 1))
    v.gg = gg
    v.gg = add_low(v.gg, p.to_y(v.gg))
    v = sync(v)
    v.q1 = p.to_y(v.q)
    v.gg1 = p.to_core(v.gg)
    v.r = add_all([half(v.r, p.z, 0, 4), v.pop.r1, v.pop.r2, v.pop.r3])[0]
    v = sync(v)
    v.r1 = p.to_y(v.r)
    grad_gate = ordered(core, v.gg[:, :ff], v.gg1[:, :ff], 1).astype(F32)
    grad_up = ordered(core, v.gg[:, ff:], v.gg1[:, ff:], 1).astype(F32)
    gains = add_low(v.q[128:132, :128], v.q1[128:132, :128])
    x_gains = p.to_x(gains)
    q0, q1 = pick(y, v.q, v.q1), pick(y, v.q1, v.q)
    mine = jnp.concatenate([q0, q1], 1)
    mine = lax.dynamic_update_slice(mine, gains, (128, 0))
    other = p.to_core(mine)
    x_other_gains = p.send(gains, lambda s, d: (s ^ 1, d ^ 1))
    v.ends = grad_gate, grad_up, gains, mine, other, x_gains, x_other_gains
    v = sync(v)
    grad_gate, grad_up, gains, mine, other, x_gains, x_other_gains = v.ends
    own_rows = ordered(y, v.r, v.r1, 1)
    other_rows = p.to_core(own_rows)
    grad_down, grad_output = [
        ordered(core, own_rows[part], other_rows[part], 1).astype(F32)
        for part in (slice(0, ff // 4), slice(ff // 4, None))
    ]
    zero, one = pick(core, mine, other), pick(core, other, mine)

    def columns(start, width):
        found = [part[:128, i : i + width] for part in (zero, one) for i in (start, start + 512)]
        return jnp.concatenate(found, 1).astype(F32)

    def expand_grad(start):
        return jnp.concatenate([p_[:128, start : start + 128] for p_ in (zero, one)], 1)

    near_gains = pick(x, gains, x_gains).astype(F32) + pick(x, x_gains, gains).astype(F32)
    far = other[128:132, :128]
    far_gains = pick(x, far, x_other_gains).astype(F32) + pick(x, x_other_gains, far).astype(F32)
    gains = half((near_gains + far_gains).reshape(2, 2, 128), x, 1)[:, 0]
    return (
        layer_out, grad_tokens, gains[0], columns(0, 256), columns(384, 128),
        expand_grad(256).T.astype(F32), expand_grad(768).T.astype(F32), grad_output, gains[1],
        grad_gate, grad_up, grad_down,
    )


def per_device(*arguments):
    p = Place()
    return (square_layer if p.square else plain_layer)(p, *arguments)


def solution(mesh):
    rows, gain, weight, across = P("dp", "seq", None), P("dp"), P("dp", None), P(None, "dp")
    return jax.shard_map(
        per_device,
        mesh=mesh,
        in_specs=(
            rows, gain, weight, weight, across, across, weight, gain, weight, weight, weight, rows,
            P("dp", None),
        ),
        out_specs=(
            rows, rows, gain, weight, weight, across, across, weight, gain, weight, weight, weight,
        ),
        check_vma=False,
    )
```
